32 devices in a mesh: gx: 8 (over z, y), gy: 4 (over x, core).
Axes of the slice: x: 2, y: 2, z: 4, core: 2. Of those that a mesh axis runs over, the one named last changes fastest.
Arguments:
- tokens: bfloat16 [128, 256, 768], P(('gx', 'gy')), may hold values from -6 to 6
- segment_ids: int32 [128, 256], P(('gx', 'gy')), may hold values from 0 to 7, never falling along the last dimension, each value on 1 to 64 neighbouring positions
- pad_mask: int32 [128, 256], P(('gx', 'gy')), may hold values 0 or 1
- w_qkv: bfloat16 [768, 2304], P(('gx', 'gy')), may hold values from -0.21875 to 0.21875
- w_out: bfloat16 [768, 768], P(('gx', 'gy')), may hold values from -0.875 to 0.875
- w_up: bfloat16 [768, 3072], P(('gx', 'gy')), may hold values from -0.21875 to 0.21875
- w_down: bfloat16 [3072, 768], P(('gx', 'gy')), may hold values from -0.109375 to 0.109375
- gain_one: bfloat16 [768], P(('gx', 'gy')), may hold values from 0.099609375 to 1.8984375
- shift_one: bfloat16 [768], P(('gx', 'gy')), may hold values from -3 to 3
- bias_query: bfloat16 [768], P(('gx', 'gy')), may hold values from -3 to 3
- bias_value: bfloat16 [768], P(('gx', 'gy')), may hold values from -3 to 3
- bias_out: bfloat16 [768], P(('gx', 'gy')), may hold values from -2 to 2
- gain_two: bfloat16 [768], P(('gx', 'gy')), may hold values from 0.099609375 to 1.8984375
- shift_two: bfloat16 [768], P(('gx', 'gy')), may hold values from -3 to 3
- bias_up: bfloat16 [3072], P(('gx', 'gy')), may hold values from -3 to 3
- bias_down: bfloat16 [768], P(('gx', 'gy')), may hold values from -2 to 2
- cotangent: bfloat16 [128, 256, 768], P(('gx', 'gy')), may hold values from -6 to 6
Outputs:
- output: bfloat16 [128, 256, 768], P(('gx', 'gy'))
- grad_tokens: float32 [128, 256, 768], P(('gx', 'gy'))
- grad_w_qkv: float32 [768, 2304], P(('gx', 'gy'))
- grad_w_out: float32 [768, 768], P(('gx', 'gy'))
- grad_w_up: float32 [768, 3072], P(('gx', 'gy'))
- grad_w_down: float32 [3072, 768], P(('gx', 'gy'))
- grad_gain_one: float32 [768], P(('gx', 'gy'))
- grad_shift_one: float32 [768], P(('gx', 'gy'))
- grad_bias_query: float32 [768], P(('gx', 'gy'))
- grad_bias_value: float32 [768], P(('gx', 'gy'))
- grad_bias_out: float32 [768], P(('gx', 'gy'))
- grad_gain_two: float32 [768], P(('gx', 'gy'))
- grad_shift_two: float32 [768], P(('gx', 'gy'))
- grad_bias_up: float32 [3072], P(('gx', 'gy'))
- grad_bias_down: float32 [768], P(('gx', 'gy'))
The draws below stay inside these ranges and needn't reach their ends.
Inputs may be any that keep to these rules, and one draw needn't show every extreme that they name: `segment_ids`: within a row the numbers never fall and each caption takes 1 to 64 positions, one exactly 64.
All inputs are finite; a program needn't handle non-finite values. No bound on the sum of `pad_mask` on one device may be relied on, other than what follows from the above.
Results may differ from the reference program's by a relative error of at most 0.012.
Values may be sent and summed in bfloat16 or wider, within the bound.
No kernel may reach another device: no remote copies, remote signals or barrier semaphores. Data moves between devices by JAX's collectives and lax.ppermute only.
A program may use at most 192 MiB of HBM per device.

```python
import math
import jax
import jax.numpy as jnp
import numpy as np
from jax import lax

D = 768
HEADS = 12
HDIM = 64
FF = 3072
LEN = 256
SEGMAX = 64
ROWS = 128
SEGS = 8


def place_ends(entries, rng, least, high):
    longest = entries.shape.index(max(entries.shape))
    spots = []
    for shift in (0, 1):
        where = [jax.random.randint(jax.random.fold_in(rng, axis), (), 0, length) for axis, length in enumerate(entries.shape)]
        where[longest] = (where[longest] + shift) % entries.shape[longest]
        spots.append(tuple(where))
    return entries.at[spots[0]].set(least).at[spots[1]].set(high)


def spiked(entries, key, source, target, shards_of, factor):
    def block_of(dim):
        return (jnp.arange(entries.shape[dim]) // (entries.shape[dim] // shards_of)).reshape((-1,) + (1,) * (entries.ndim - 1 - dim))

    first = jax.random.permutation(key, shards_of)[block_of(target)]
    far = (block_of(target) + shards_of // 2) % shards_of
    return jnp.where((block_of(source) == first) | (block_of(source) == far), factor * entries, entries)


def block_scale(key, shape, shards, low, largest):
    def one(axis_at, parts):
        heights = jax.random.uniform(jax.random.fold_in(jax.random.fold_in(key, 6), axis_at), (parts,), jnp.float32, low / len(shards), largest / len(shards))
        return jnp.repeat(jnp.exp(heights), shape[axis_at] // parts).reshape((-1,) + (1,) * (len(shape) - axis_at - 1))

    factor_of = one(*shards[0])
    for cut in shards[1:]:
        factor_of = factor_of * one(*cut)
    return factor_of


def profile(number_of, total, limit, lean):
    weights = [(1 << 20) // math.isqrt(standing ** lean) + 1 for standing in range(2, number_of + 1)]
    surplus, counts = total - limit - (number_of - 1), [1] * (number_of - 1)
    while surplus > 0:
        movable = [i for i in range(number_of - 1) if counts[i] < limit]
        pool, remaining = sum([weights[i] for i in movable]), surplus
        for i in movable:
            addition = min(limit - counts[i], max(1, remaining * weights[i] // pool), surplus)
            counts[i] = counts[i] + addition
            surplus = surplus - addition
    return np.array([limit] + counts)


def uneven(own_key, count, total, limit, skew):
    if count == 2:
        one = jax.random.randint(own_key, (), max(1, total - limit), min(limit, total - 1) + 1)
        return jnp.stack([one, total - one])
    lengths = jnp.asarray(profile(count, total, limit, skew), jnp.int32)
    twos = (count - 1) // 2
    giver, receiver = lengths[1:1 + 2 * twos:2], lengths[2:2 + 2 * twos:2]
    margin = jnp.minimum(giver - 1, limit - receiver)
    shifted = jax.random.randint(jax.random.fold_in(own_key, 1), (twos,), 0, 1 << 20) % (margin + 1)
    lengths = lengths.at[1:1 + 2 * twos:2].set(giver - shifted).at[2:2 + 2 * twos:2].set(receiver + shifted)
    return lengths[jax.random.permutation(jax.random.fold_in(own_key, 2), count)]


def noise(rng, dims, deviation, bound, shards=(), dtype=jnp.bfloat16):
    values = jax.random.normal(rng, dims, jnp.float32) * deviation
    if len(shards) > 0:
        values = block_scale(rng, dims, shards, -0.22, 0.18) * values
    return jnp.clip(values, min=-bound, max=bound).astype(dtype)


def noise_with(stream_key, dims, scale, reach, pieces, heavy, dtype=jnp.bfloat16):
    drawn = scale * jax.random.normal(stream_key, dims, jnp.float32)
    if pieces:
        drawn = drawn * block_scale(stream_key, dims, pieces, -0.22, 0.18)
    return jnp.clip(spiked(drawn, jax.random.fold_in(stream_key, 3), *heavy), -reach, reach).astype(dtype)


def setup_inputs(seed: int = 0) -> dict:
    arg_keys = jax.random.split(jax.random.key(seed), 18)
    return {
        "tokens": noise(arg_keys[0], (ROWS, LEN, D), 1.0, 6.0, ((0, 32),)),
        "segment_ids": jax.vmap(lambda own: jnp.searchsorted(jnp.cumsum(uneven(own, SEGS, LEN, SEGMAX, 0)), jnp.arange(LEN), side="right"))(jax.random.split(arg_keys[1], ROWS)).reshape((ROWS, LEN)).astype(jnp.int32),
        "pad_mask": place_ends((jax.random.randint(arg_keys[2], (ROWS, LEN), 0, 8) < 7).astype(jnp.int32), jax.random.fold_in(arg_keys[2], 1), 0, 1),
        "w_qkv": noise(arg_keys[3], (D, 3 * D), D ** -0.5, 0.21875, ((0, 32),)),
        "w_out": noise(arg_keys[4], (D, D), (D // 16) ** -0.5, 0.875, ((0, 32),)),
        "w_up": noise(arg_keys[5], (D, FF), D ** -0.5, 0.21875, ((0, 32),)),
        "w_down": noise(arg_keys[6], (FF, D), FF ** -0.5, 0.109375, ((0, 32),)),
        "gain_one": jnp.clip(1.0 + 0.18 * jax.random.normal(arg_keys[7], (D,), jnp.float32), 0.099609375, 1.8984375).astype(jnp.bfloat16),
        "shift_one": noise(arg_keys[8], (D,), 0.5, 3.0, ((0, 32),)),
        "bias_query": noise(arg_keys[9], (D,), 0.5, 3.0, ((0, 32),)),
        "bias_value": noise(arg_keys[10], (D,), 0.5, 3.0, ((0, 32),)),
        "bias_out": noise(arg_keys[11], (D,), 0.3, 2.0, ((0, 32),)),
        "gain_two": jnp.clip(1.0 + 0.18 * jax.random.normal(arg_keys[12], (D,), jnp.float32), 0.099609375, 1.8984375).astype(jnp.bfloat16),
        "shift_two": noise(arg_keys[13], (D,), 0.5, 3.0, ((0, 32),)),
        "bias_up": noise(arg_keys[14], (FF,), 0.5, 3.0, ((0, 32),)),
        "bias_down": noise(arg_keys[15], (D,), 0.3, 2.0, ((0, 32),)),
        "cotangent": noise_with(arg_keys[16], (ROWS, LEN, D), 1.0, 6.0, ((0, 32),), (0, 2, 32, 2.75)),
    }


@jax.custom_vjp
def low(v):
    return lax.optimization_barrier(v.astype(jnp.bfloat16)).astype(jnp.float32)

@jax.custom_vjp
def low_back(v):
    return v

def low_keep(v):
    return (low(v), None)

def low_pass(kept, grad):
    return (grad,)

def back_keep(v):
    return (v, None)

def back_low(kept, grad):
    return (low(grad),)
low.defvjp(low_keep, low_pass)
low_back.defvjp(back_keep, back_low)
HIGHEST = lax.Precision.HIGHEST

def layer_norm(values, gain, shift):
    centre = values - lax.optimization_barrier(jnp.mean(values, axis=-1, keepdims=True))
    spread = lax.optimization_barrier(jnp.mean(centre * centre, axis=-1, keepdims=True))
    return centre * lax.rsqrt(spread + 1e-06) * gain + shift

def attend_mask(segment_ids, pad_mask):
    length = segment_ids.shape[-1]
    positions = jnp.arange(length)
    same = segment_ids[:, :, None] == segment_ids[:, None, :]
    real = pad_mask[:, None, :] == 1
    itself = positions[:, None] == positions[None, :]
    return same & (real | itself[None])

def project(left, matrix):
    return jnp.einsum('gld,de->gle', left, matrix, precision=HIGHEST)

def forward(inputs, segment_ids, pad_mask, params):
    w_qkv, w_out, w_up, w_down, gain_one, shift_one, bias_query, bias_value, bias_out, gain_two, shift_two, bias_up, bias_down = params
    group, length, width = inputs.shape
    normed = low(layer_norm(inputs, gain_one, shift_one))
    mixed = project(normed, w_qkv)
    query_part = low(low_back(mixed[..., :width] + bias_query)).reshape(group, length, HEADS, HDIM)
    key_part = low(low_back(mixed[..., width:2 * width])).reshape(group, length, HEADS, HDIM)
    value_part = low(low_back(mixed[..., 2 * width:] + bias_value)).reshape(group, length, HEADS, HDIM)
    score_scale = 1.0 / math.sqrt(HDIM)
    raw = jnp.einsum('gqhe,gkhe->ghqk', query_part, key_part, precision=HIGHEST) * score_scale
    allowed = attend_mask(segment_ids, pad_mask)
    scores = low_back(jnp.where(allowed[:, None], raw, -1e+30))
    highest = lax.optimization_barrier(jnp.max(scores, axis=-1, keepdims=True))
    expo = jnp.exp(scores - highest)
    probs = expo / lax.optimization_barrier(jnp.sum(expo, axis=-1, keepdims=True))
    attended = jnp.einsum('ghqk,gkhe->gqhe', low(probs), value_part, precision=HIGHEST)
    attended = low(low_back(attended.reshape(group, length, width)))
    branch = low_back(project(attended, w_out) + bias_out)
    middle = inputs + branch
    normed_two = low(layer_norm(middle, gain_two, shift_two))
    hidden = low_back(project(normed_two, w_up) + bias_up)
    active = low(jax.nn.gelu(hidden, approximate=True))
    return middle + low_back(project(active, w_down) + bias_down)

def add_pair(first, second):
    return first + second

def reference(tokens, segment_ids, pad_mask, w_qkv, w_out, w_up, w_down, gain_one, shift_one, bias_query, bias_value, bias_out, gain_two, shift_two, bias_up, bias_down, cotangent):
    params = tuple((param.astype(jnp.float32) for param in (w_qkv, w_out, w_up, w_down, gain_one, shift_one, bias_query, bias_value, bias_out, gain_two, shift_two, bias_up, bias_down)))
    row_total, length, width = tokens.shape
    row_block = min(16, row_total)
    blocks = row_total // row_block

    def one_block(totals, items):
        block_in, block_seg, block_pad, block_ct = items

        def apply(inputs, weights):
            return forward(inputs, block_seg, block_pad, weights)
        result, pull = jax.vjp(apply, block_in.astype(jnp.float32), params)
        grad_in, grad_params = pull(block_ct.astype(jnp.float32))
        totals = jax.tree.map(add_pair, totals, grad_params)
        return (totals, (result.astype(jnp.bfloat16), grad_in))
    zeros = tuple((jnp.zeros_like(param) for param in params))
    items = (tokens.reshape(blocks, row_block, length, width), segment_ids.reshape(blocks, row_block, length), pad_mask.reshape(blocks, row_block, length), cotangent.reshape(blocks, row_block, length, width))
    totals, (outputs, grads) = lax.scan(one_block, zeros, items)
    return (outputs.reshape(row_total, length, width), grads.reshape(row_total, length, width), totals[0], totals[1], totals[2], totals[3], totals[4], totals[5], totals[6], totals[7], totals[8], totals[9], totals[10], totals[11], totals[12])
```

```python
import math

import jax
import jax.numpy as jnp
from jax import lax
from jax.sharding import PartitionSpec as P

HEADS = 12
HDIM = 64


def layer_norm(values, gain, shift):
    centre = values - jnp.mean(values, axis=-1, keepdims=True)
    spread = jnp.mean(centre * centre, axis=-1, keepdims=True)
    return centre * lax.rsqrt(spread + 1e-06) * gain + shift


def smooth_gate(values):
    return jax.nn.gelu(values, approximate=True)


def attend_mask(segment_ids, pad_mask):
    length = segment_ids.shape[-1]
    positions = jnp.arange(length)
    same = segment_ids[:, :, None] == segment_ids[:, None, :]
    real = pad_mask[:, None, :] == 1
    itself = positions[:, None] == positions[None, :]
    return same & (real | itself[None])


def outer_sum(left, right):
    return lax.dot_general(
        left, right, (((0,), (0,)), ((), ())), preferred_element_type=jnp.float32
    )


def against(left, matrix):
    return lax.dot_general(
        left, matrix, (((1,), (1,)), ((), ())), preferred_element_type=jnp.float32
    )


def score_block(query_part, key_part, allowed):
    raw = jnp.einsum("rqhe,rkhe->rhqk", query_part, key_part, preferred_element_type=jnp.float32)
    raw = raw * (1.0 / math.sqrt(HDIM))
    return jnp.where(allowed[:, None], raw, -1e30)


def collect(
    w_qkv,
    w_out,
    w_up,
    w_down,
    gain_one,
    shift_one,
    bias_query,
    bias_value,
    bias_out,
    gain_two,
    shift_two,
    bias_up,
    bias_down,
):
    return (
        lax.all_gather(w_qkv, ("gx", "gy"), axis=0, tiled=True),
        lax.all_gather(w_out, ("gx", "gy"), axis=0, tiled=True),
        lax.all_gather(w_up, ("gx", "gy"), axis=0, tiled=True),
        lax.all_gather(w_down, ("gx", "gy"), axis=0, tiled=True),
        lax.all_gather(gain_one, ("gx", "gy"), axis=0, tiled=True),
        lax.all_gather(shift_one, ("gx", "gy"), axis=0, tiled=True),
        lax.all_gather(bias_query, ("gx", "gy"), axis=0, tiled=True),
        lax.all_gather(bias_value, ("gx", "gy"), axis=0, tiled=True),
        lax.all_gather(bias_out, ("gx", "gy"), axis=0, tiled=True),
        lax.all_gather(gain_two, ("gx", "gy"), axis=0, tiled=True),
        lax.all_gather(shift_two, ("gx", "gy"), axis=0, tiled=True),
        lax.all_gather(bias_up, ("gx", "gy"), axis=0, tiled=True),
        lax.all_gather(bias_down, ("gx", "gy"), axis=0, tiled=True),
    )


def generic_device(
    tokens,
    segment_ids,
    pad_mask,
    w_qkv,
    w_out,
    w_up,
    w_down,
    gain_one,
    shift_one,
    bias_query,
    bias_value,
    bias_out,
    gain_two,
    shift_two,
    bias_up,
    bias_down,
    cotangent,
):
    row_count, length, width = tokens.shape
    total_rows = row_count * length
    gathered = collect(
        w_qkv,
        w_out,
        w_up,
        w_down,
        gain_one,
        shift_one,
        bias_query,
        bias_value,
        bias_out,
        gain_two,
        shift_two,
        bias_up,
        bias_down,
    )
    full_qkv, full_out, full_up, full_down = (gathered[0], gathered[1], gathered[2], gathered[3])
    gain_first = gathered[4].astype(jnp.float32)
    shift_first = gathered[5].astype(jnp.float32)
    query_bias = gathered[6].astype(jnp.float32)
    value_bias = gathered[7].astype(jnp.float32)
    out_bias = gathered[8].astype(jnp.float32)
    gain_second = gathered[9].astype(jnp.float32)
    shift_second = gathered[10].astype(jnp.float32)
    up_bias = gathered[11].astype(jnp.float32)
    down_bias = gathered[12].astype(jnp.float32)
    allowed = attend_mask(segment_ids, pad_mask)
    inputs = tokens.astype(jnp.float32).reshape(total_rows, width)
    first_norm, first_pull = jax.vjp(layer_norm, inputs, gain_first, shift_first)
    normed = first_norm.astype(jnp.bfloat16)
    mixed = jnp.dot(normed, full_qkv, preferred_element_type=jnp.float32)
    query_part = (
        (mixed[:, :width] + query_bias).astype(jnp.bfloat16).reshape(row_count, length, HEADS, HDIM)
    )
    key_part = (
        mixed[:, width : 2 * width].astype(jnp.bfloat16).reshape(row_count, length, HEADS, HDIM)
    )
    value_part = (
        (mixed[:, 2 * width :] + value_bias)
        .astype(jnp.bfloat16)
        .reshape(row_count, length, HEADS, HDIM)
    )
    scores = score_block(query_part, key_part, allowed)
    highest = jnp.max(scores, axis=-1, keepdims=True)
    log_total = highest + jnp.log(jnp.sum(jnp.exp(scores - highest), axis=-1, keepdims=True))
    weights = jnp.exp(scores - log_total).astype(jnp.bfloat16)
    attended = jnp.einsum(
        "rhqk,rkhe->rqhe", weights, value_part, preferred_element_type=jnp.float32
    )
    attended = attended.reshape(total_rows, width).astype(jnp.bfloat16)
    middle = inputs + jnp.dot(attended, full_out, preferred_element_type=jnp.float32) + out_bias
    second_norm, second_pull = jax.vjp(layer_norm, middle, gain_second, shift_second)
    normed_two = second_norm.astype(jnp.bfloat16)
    hidden = jnp.dot(normed_two, full_up, preferred_element_type=jnp.float32) + up_bias
    active, gate_pull = jax.vjp(smooth_gate, hidden)
    active_low = active.astype(jnp.bfloat16)
    result = middle + jnp.dot(active_low, full_down, preferred_element_type=jnp.float32) + down_bias
    output = result.astype(jnp.bfloat16).reshape(row_count, length, width)
    again = collect(
        w_qkv,
        w_out,
        w_up,
        w_down,
        gain_one,
        shift_one,
        bias_query,
        bias_value,
        bias_out,
        gain_two,
        shift_two,
        bias_up,
        bias_down,
    )
    full_qkv, full_out, full_up, full_down = (again[0], again[1], again[2], again[3])
    down_in = cotangent.reshape(total_rows, width)
    outer_grad = down_in.astype(jnp.float32)
    grad_bias_down = jnp.sum(outer_grad, axis=0)
    grad_w_down = outer_sum(active_low, down_in)
    active_grad = against(down_in, full_down)
    hidden_grad = gate_pull(active_grad)[0].astype(jnp.bfloat16)
    grad_bias_up = jnp.sum(hidden_grad.astype(jnp.float32), axis=0)
    grad_w_up = outer_sum(normed_two, hidden_grad)
    norm_two_grad = against(hidden_grad, full_up)
    middle_part, grad_gain_two, grad_shift_two = second_pull(norm_two_grad)
    middle_grad = outer_grad + middle_part
    branch_grad = middle_grad.astype(jnp.bfloat16)
    grad_bias_out = jnp.sum(branch_grad.astype(jnp.float32), axis=0)
    grad_w_out = outer_sum(attended, branch_grad)
    attended_grad = (
        against(branch_grad, full_out).astype(jnp.bfloat16).reshape(row_count, length, HEADS, HDIM)
    )
    probs = jnp.exp(score_block(query_part, key_part, allowed) - log_total)
    probs_low = probs.astype(jnp.bfloat16)
    value_grad = jnp.einsum(
        "rhqk,rqhe->rkhe", probs_low, attended_grad, preferred_element_type=jnp.float32
    ).astype(jnp.bfloat16)
    prob_grad = jnp.einsum(
        "rqhe,rkhe->rhqk", attended_grad, value_part, preferred_element_type=jnp.float32
    )
    inner_term = jnp.sum(prob_grad * probs, axis=-1, keepdims=True)
    score_grad = (probs * (prob_grad - inner_term)).astype(jnp.bfloat16)
    score_scale = 1.0 / math.sqrt(HDIM)
    query_grad = (
        (
            jnp.einsum("rhqk,rkhe->rqhe", score_grad, key_part, preferred_element_type=jnp.float32)
            * score_scale
        )
        .astype(jnp.bfloat16)
        .reshape(total_rows, width)
    )
    key_grad = (
        (
            jnp.einsum(
                "rhqk,rqhe->rkhe", score_grad, query_part, preferred_element_type=jnp.float32
            )
            * score_scale
        )
        .astype(jnp.bfloat16)
        .reshape(total_rows, width)
    )
    value_flat = value_grad.reshape(total_rows, width)
    mixed_grad = jnp.concatenate([query_grad, key_grad, value_flat], axis=1)
    grad_bias_query = jnp.sum(query_grad.astype(jnp.float32), axis=0)
    grad_bias_value = jnp.sum(value_flat.astype(jnp.float32), axis=0)
    grad_w_qkv = outer_sum(normed, mixed_grad)
    norm_one_grad = against(mixed_grad, full_qkv)
    input_part, grad_gain_one, grad_shift_one = first_pull(norm_one_grad)
    grad_tokens = (middle_grad + input_part).reshape(row_count, length, width)
    shares = (
        lax.psum_scatter(grad_w_qkv, ("gx", "gy"), scatter_dimension=0, tiled=True),
        lax.psum_scatter(grad_w_out, ("gx", "gy"), scatter_dimension=0, tiled=True),
        lax.psum_scatter(grad_w_up, ("gx", "gy"), scatter_dimension=0, tiled=True),
        lax.psum_scatter(grad_w_down, ("gx", "gy"), scatter_dimension=0, tiled=True),
        lax.psum_scatter(grad_gain_one, ("gx", "gy"), scatter_dimension=0, tiled=True),
        lax.psum_scatter(grad_shift_one, ("gx", "gy"), scatter_dimension=0, tiled=True),
        lax.psum_scatter(grad_bias_query, ("gx", "gy"), scatter_dimension=0, tiled=True),
        lax.psum_scatter(grad_bias_value, ("gx", "gy"), scatter_dimension=0, tiled=True),
        lax.psum_scatter(grad_bias_out, ("gx", "gy"), scatter_dimension=0, tiled=True),
        lax.psum_scatter(grad_gain_two, ("gx", "gy"), scatter_dimension=0, tiled=True),
        lax.psum_scatter(grad_shift_two, ("gx", "gy"), scatter_dimension=0, tiled=True),
        lax.psum_scatter(grad_bias_up, ("gx", "gy"), scatter_dimension=0, tiled=True),
        lax.psum_scatter(grad_bias_down, ("gx", "gy"), scatter_dimension=0, tiled=True),
    )
    return (
        output,
        grad_tokens,
        shares[0],
        shares[1],
        shares[2],
        shares[3],
        shares[4],
        shares[5],
        shares[6],
        shares[7],
        shares[8],
        shares[9],
        shares[10],
        shares[11],
        shares[12],
    )


AXES = ("gx", "gy")


def pairs(move):
    out = []
    for d in range(32):
        z, y, x, c = d // 8, (d // 4) % 2, (d // 2) % 2, d % 2
        z, y, x, c = move(z, y, x, c)
        out.append((d, ((z * 2 + y) * 2 + x) * 2 + c))
    return out


SWAP_C = pairs(lambda z, y, x, c: (z, y, x, 1 - c))
SWAP_X = pairs(lambda z, y, x, c: (z, y, 1 - x, c))
SWAP_Y = pairs(lambda z, y, x, c: (z, 1 - y, x, c))
SWAP_Z = [None] + [pairs(lambda z, y, x, c, k=k: (z ^ k, y, x, c)) for k in (1, 2, 3)]


def send(values, perm):
    return lax.ppermute(values, AXES, perm)


def place():
    gx, gy = lax.axis_index("gx"), lax.axis_index("gy")
    return gx // 2, gx % 2, gy // 2, gy % 2


def spread_block(own):
    own = own[None]
    col = jnp.concatenate([own] + [send(own, SWAP_Z[k]) for k in (1, 2, 3)], axis=0)
    along_x, along_y = send(col, SWAP_X), send(col, SWAP_Y)
    far0, far1 = send(along_x[0:2], SWAP_Y), send(along_y[2:4], SWAP_X)
    return [col, along_x, along_y, far0, far1]


def gather_pack(own):
    mine = spread_block(own)
    other = [send(v, SWAP_C) for v in mine]
    return mine, other


def total_pack(mine, theirs):
    got = send(theirs, SWAP_C)

    def both(index):
        return mine[index].astype(jnp.float32) + got[index].astype(jnp.float32)

    low = jnp.bfloat16
    first_x = send(both((slice(None), 1, slice(0, 2))).astype(low), SWAP_X)
    first_y = send(both((1, slice(None), slice(2, 4))).astype(low), SWAP_Y)
    second_y = send((both((1, 0, slice(0, 2))) + first_x[1]).astype(low), SWAP_Y)
    second_x = send((both((0, 1, slice(2, 4))) + first_y[1]).astype(low), SWAP_X)
    near = both((0, 0, slice(0, 2))) + first_x[0] + second_y
    away = both((0, 0, slice(2, 4))) + first_y[0] + second_x
    parts = [near[0], near[1], away[0], away[1]]
    total = parts[0]
    for k in (1, 2, 3):
        total = total + send(parts[k].astype(low), SWAP_Z[k])
    return total


def to_absolute(rel, axis_bits):
    z0, y0, x0 = axis_bits
    rel = jnp.where(y0 == 0, rel, rel[::-1])
    rel = jnp.where(x0 == 0, rel, rel[:, ::-1])
    odd = jnp.concatenate([rel[:, :, 1:2], rel[:, :, 0:1], rel[:, :, 3:4], rel[:, :, 2:3]], axis=2)
    rel = jnp.where(z0 % 2 == 0, rel, odd)
    rel = jnp.where(z0 // 2 == 0, rel, jnp.concatenate([rel[:, :, 2:4], rel[:, :, 0:2]], axis=2))
    return rel


def to_full(pack, bits):
    col, along_x, along_y, far0, far1 = pack
    far = jnp.concatenate([far0, far1], axis=0)
    rel = jnp.stack([jnp.stack([col, along_x]), jnp.stack([along_y, far])])
    absolute = to_absolute(rel, bits)
    return jnp.transpose(absolute, (2, 0, 1, 3, 4)).reshape(16, 48, -1)


def to_relative(full, bits):
    rel = jnp.transpose(full.reshape(4, 2, 2, 48, -1), (1, 2, 0, 3, 4))
    return to_absolute(rel, bits)


def halves_of(own, sibling, core):
    return jnp.where(core == 0, own, sibling), jnp.where(core == 0, sibling, own)


VECTOR_SIZES = (24, 24, 24, 24, 24, 24, 24, 96, 24)


def on_device(
    tokens, segment_ids, pad_mask, w_qkv, w_out, w_up, w_down, gain_one, shift_one, bias_query,
    bias_value, bias_out, gain_two, shift_two, bias_up, bias_down, cotangent,
):
    z0, y0, x0, core = place()
    bits = (z0, y0, x0)
    row_count, length, width = tokens.shape
    total_rows = row_count * length
    vectors = jnp.concatenate(
        [gain_one, shift_one, bias_query, bias_value, bias_out, gain_two, shift_two, bias_up, bias_down]
    )
    vectors = lax.all_gather(jnp.pad(vectors, (0, 96))[None], AXES, axis=0, tiled=True)
    spans, at = [], 0
    for size in VECTOR_SIZES:
        spans.append(vectors[:, at : at + size].astype(jnp.float32))
        at += size
    flat = [v.reshape(-1) for v in spans]
    gain_first, shift_first, query_bias, value_bias, out_bias, gain_second, shift_second = flat[:7]
    down_bias = flat[8]
    up_bias = spans[7].reshape(16, 2, 96).transpose(1, 0, 2).reshape(-1)

    def column_half(side):
        at = side * 384
        up = w_up.reshape(24, 16, 2, 96).transpose(2, 0, 1, 3).reshape(2, 24, 1536)
        return (
            jnp.concatenate(
                [w_qkv[:, at : at + 384], w_qkv[:, 768 + at : 1152 + at],
                 w_qkv[:, 1536 + at : 1920 + at], w_out[:, at : at + 384]], axis=1),
            up[0, :, side * 768 : side * 768 + 768],
            up[1, :, side * 768 : side * 768 + 768],
            w_down[:, at : at + 384],
        )

    zero, one = column_half(0), column_half(1)
    keep = [jnp.where(core == 0, a, b) for a, b in zip(zero, one)]
    give = [jnp.where(core == 0, b, a) for a, b in zip(zero, one)]
    got = [send(v, SWAP_C) for v in give]

    def rows(a, b):
        return jnp.where(core == 0, jnp.concatenate([a, b]), jnp.concatenate([b, a]))

    def tall(v):
        return jnp.concatenate([v[:48], v[48:]], axis=1)

    first = rows(keep[0], got[0])
    down_a, down_b = halves_of(keep[3], got[3], core)
    second = jnp.concatenate([rows(keep[1], got[1]), tall(down_a)], axis=1)
    third = jnp.concatenate([rows(keep[2], got[2]), tall(down_b)], axis=1)
    packs = []
    for own in (first, second, third):
        mine, other = gather_pack(own)
        packs.append(halves_of(to_full(mine, bits), to_full(other, bits), core))
    full_qkv = jnp.concatenate(
        [packs[0][s][:, :, p * 384 : p * 384 + 384].reshape(768, 384) for p in range(3) for s in range(2)], axis=1)
    full_out = jnp.concatenate([packs[0][s][:, :, 1152:].reshape(768, 384) for s in range(2)], axis=1)
    full_up = jnp.concatenate([packs[1 + f][s][:, :, :768].reshape(768, 768) for f in range(2) for s in range(2)], axis=1)

    def down_of(f):
        sides = []
        for s in range(2):
            v = packs[1 + f][s][:, :, 768:]
            sides.append(jnp.concatenate([v[:, :, :384], v[:, :, 384:]], axis=1).reshape(1536, 384))
        return jnp.concatenate(sides, axis=1)

    full_down = jnp.concatenate([down_of(0), down_of(1)], axis=0)

    allowed = attend_mask(segment_ids, pad_mask)
    inputs = tokens.astype(jnp.float32).reshape(total_rows, width)
    first_norm, first_pull = jax.vjp(layer_norm, inputs, gain_first, shift_first)
    normed = first_norm.astype(jnp.bfloat16)
    mixed = jnp.dot(normed, full_qkv, preferred_element_type=jnp.float32)
    query_part = (mixed[:, :width] + query_bias).astype(jnp.bfloat16).reshape(row_count, length, HEADS, HDIM)
    key_part = mixed[:, width : 2 * width].astype(jnp.bfloat16).reshape(row_count, length, HEADS, HDIM)
    value_part = (mixed[:, 2 * width :] + value_bias).astype(jnp.bfloat16).reshape(row_count, length, HEADS, HDIM)
    scores = score_block(query_part, key_part, allowed)
    highest = jnp.max(scores, axis=-1, keepdims=True)
    log_total = highest + jnp.log(jnp.sum(jnp.exp(scores - highest), axis=-1, keepdims=True))
    weights = jnp.exp(scores - log_total).astype(jnp.bfloat16)
    attended = jnp.einsum("rhqk,rkhe->rqhe", weights, value_part, preferred_element_type=jnp.float32)
    attended = attended.reshape(total_rows, width).astype(jnp.bfloat16)
    middle = inputs + jnp.dot(attended, full_out, preferred_element_type=jnp.float32) + out_bias
    second_norm, second_pull = jax.vjp(layer_norm, middle, gain_second, shift_second)
    normed_two = second_norm.astype(jnp.bfloat16)
    hidden = jnp.dot(normed_two, full_up, preferred_element_type=jnp.float32) + up_bias
    active, gate_pull = jax.vjp(smooth_gate, hidden)
    active_low = active.astype(jnp.bfloat16)
    result = middle + jnp.dot(active_low, full_down, preferred_element_type=jnp.float32) + down_bias
    output = result.astype(jnp.bfloat16).reshape(row_count, length, width)
    down_in = cotangent.reshape(total_rows, width)
    outer_grad = down_in.astype(jnp.float32)
    grad_bias_down = jnp.sum(outer_grad, axis=0)
    grad_w_down = outer_sum(active_low, down_in)
    active_grad = against(down_in, full_down)
    hidden_grad = gate_pull(active_grad)[0].astype(jnp.bfloat16)
    grad_bias_up = jnp.sum(hidden_grad.astype(jnp.float32), axis=0)
    grad_w_up = outer_sum(normed_two, hidden_grad)
    norm_two_grad = against(hidden_grad, full_up)
    middle_part, grad_gain_two, grad_shift_two = second_pull(norm_two_grad)
    middle_grad = outer_grad + middle_part
    branch_grad = middle_grad.astype(jnp.bfloat16)
    grad_bias_out = jnp.sum(branch_grad.astype(jnp.float32), axis=0)
    grad_w_out = outer_sum(attended, branch_grad)
    attended_grad = against(branch_grad, full_out).astype(jnp.bfloat16).reshape(row_count, length, HEADS, HDIM)
    probs = jnp.exp(score_block(query_part, key_part, allowed) - log_total)
    probs_low = probs.astype(jnp.bfloat16)
    value_grad = jnp.einsum("rhqk,rqhe->rkhe", probs_low, attended_grad, preferred_element_type=jnp.float32).astype(jnp.bfloat16)
    prob_grad = jnp.einsum("rqhe,rkhe->rhqk", attended_grad, value_part, preferred_element_type=jnp.float32)
    inner_term = jnp.sum(prob_grad * probs, axis=-1, keepdims=True)
    score_grad = (probs * (prob_grad - inner_term)).astype(jnp.bfloat16)
    score_scale = 1.0 / math.sqrt(HDIM)
    query_grad = (jnp.einsum("rhqk,rkhe->rqhe", score_grad, key_part, preferred_element_type=jnp.float32) * score_scale).astype(jnp.bfloat16).reshape(total_rows, width)
    key_grad = (jnp.einsum("rhqk,rqhe->rkhe", score_grad, query_part, preferred_element_type=jnp.float32) * score_scale).astype(jnp.bfloat16).reshape(total_rows, width)
    value_flat = value_grad.reshape(total_rows, width)
    mixed_grad = jnp.concatenate([query_grad, key_grad, value_flat], axis=1)
    grad_bias_query = jnp.sum(query_grad.astype(jnp.float32), axis=0)
    grad_bias_value = jnp.sum(value_flat.astype(jnp.float32), axis=0)
    grad_w_qkv = outer_sum(normed, mixed_grad)
    norm_one_grad = against(mixed_grad, full_qkv)
    input_part, grad_gain_one, grad_shift_one = first_pull(norm_one_grad)
    grad_tokens = (middle_grad + input_part).reshape(row_count, length, width)

    def sides(pick):
        a, b = to_relative(pick(0).astype(jnp.bfloat16), bits), to_relative(pick(1).astype(jnp.bfloat16), bits)
        return halves_of(a, b, core)

    def ff_pack(f):
        def pick(s):
            up = grad_w_up[:, f * 1536 + s * 768 : f * 1536 + s * 768 + 768].reshape(16, 48, 768)
            down = grad_w_down[f * 1536 : f * 1536 + 1536, s * 384 : s * 384 + 384].reshape(16, 2, 48, 384)
            return jnp.concatenate([up, down[:, 0], down[:, 1]], axis=2)

        return total_pack(*sides(pick))

    def attend_pack(s):
        at = s * 384
        return jnp.concatenate(
            [grad_w_qkv[:, at : at + 384], grad_w_qkv[:, 768 + at : 1152 + at],
             grad_w_qkv[:, 1536 + at : 1920 + at], grad_w_out[:, at : at + 384]], axis=1).reshape(16, 48, 1536)

    sum_a, sum_b = ff_pack(0), ff_pack(1)
    sum_one = total_pack(*sides(attend_pack))

    def finish(part):
        upper, lower = part[:24], part[24:]
        keep, give = halves_of(upper, lower, core)
        back = send(give, SWAP_C)
        return halves_of(keep, back, core)

    one0, one1 = finish(sum_one)
    share_qkv = jnp.concatenate([v[:, p * 384 : p * 384 + 384] for p in range(3) for v in (one0, one1)], axis=1)
    share_out = jnp.concatenate([one0[:, 1152:], one1[:, 1152:]], axis=1)
    ups = [jnp.concatenate(finish(v[:, :768]), axis=1) for v in (sum_a, sum_b)]
    share_up = jnp.stack([u.reshape(24, 16, 96) for u in ups], axis=2).reshape(24, 3072)

    def long(v):
        return jnp.concatenate([v[:, :384], v[:, 384:]], axis=0)

    keep, give = halves_of(long(sum_a[:, 768:]), long(sum_b[:, 768:]), core)
    back = send(give, SWAP_C)
    share_down = jnp.concatenate(halves_of(keep, back, core), axis=1)

    up_rows = grad_bias_up.reshape(2, 16, 96).transpose(1, 0, 2).reshape(32, 96)
    rows32 = jnp.concatenate(
        [v.reshape(32, 24) for v in (grad_gain_one, grad_shift_one, grad_bias_query, grad_bias_value,
                                     grad_bias_out, grad_gain_two, grad_shift_two)]
        + [up_rows, grad_bias_down.reshape(32, 24), jnp.zeros((32, 96), jnp.float32)], axis=1)
    mine = lax.psum_scatter(rows32, AXES, scatter_dimension=0, tiled=True).reshape(-1)
    pieces, at = [], 0
    for size in VECTOR_SIZES:
        pieces.append(mine[at : at + size])
        at += size
    return (output, grad_tokens, share_qkv, share_out, share_up, share_down, *pieces)


def solution(mesh):
    fits = dict(mesh.shape) == {"gx": 8, "gy": 4}
    device = on_device if fits else generic_device
    return jax.shard_map(
        device,
        mesh=mesh,
        in_specs=(
            P(("gx", "gy"), None, None),
            P(("gx", "gy"), None),
            P(("gx", "gy"), None),
            P(("gx", "gy"), None),
            P(("gx", "gy"), None),
            P(("gx", "gy"), None),
            P(("gx", "gy"), None),
            P(("gx", "gy")),
            P(("gx", "gy")),
            P(("gx", "gy")),
            P(("gx", "gy")),
            P(("gx", "gy")),
            P(("gx", "gy")),
            P(("gx", "gy")),
            P(("gx", "gy")),
            P(("gx", "gy")),
            P(("gx", "gy"), None, None),
        ),
        out_specs=(
            P(("gx", "gy"), None, None),
            P(("gx", "gy"), None, None),
            P(("gx", "gy"), None),
            P(("gx", "gy"), None),
            P(("gx", "gy"), None),
            P(("gx", "gy"), None),
            P(("gx", "gy")),
            P(("gx", "gy")),
            P(("gx", "gy")),
            P(("gx", "gy")),
            P(("gx", "gy")),
            P(("gx", "gy")),
            P(("gx", "gy")),
            P(("gx", "gy")),
            P(("gx", "gy")),
        ),
        check_vma=False,
    )
```

```python
import functools
import math

import jax
import jax.numpy as jnp
from jax import lax
from jax.experimental import pallas as pl
from jax.experimental.pallas import tpu as pltpu
from jax.sharding import Mesh
from jax.sharding import PartitionSpec as P

HEADS = 12
HDIM = 64


def layer_norm(values, gain, shift):
    centre = values - jnp.mean(values, axis=-1, keepdims=True)
    spread = jnp.mean(centre * centre, axis=-1, keepdims=True)
    return centre * lax.rsqrt(spread + 1e-06) * gain + shift


def smooth_gate(values):
    return jax.nn.gelu(values, approximate=True)


def attend_mask(segment_ids, pad_mask):
    length = segment_ids.shape[-1]
    positions = jnp.arange(length)
    same = segment_ids[:, :, None] == segment_ids[:, None, :]
    real = pad_mask[:, None, :] == 1
    itself = positions[:, None] == positions[None, :]
    return same & (real | itself[None])


def outer_sum(left, right):
    return lax.dot_general(
        left, right, (((0,), (0,)), ((), ())), preferred_element_type=jnp.float32
    )


def against(left, matrix):
    return lax.dot_general(
        left, matrix, (((1,), (1,)), ((), ())), preferred_element_type=jnp.float32
    )


def score_block(query_part, key_part, allowed):
    raw = jnp.einsum("rqhe,rkhe->rhqk", query_part, key_part, preferred_element_type=jnp.float32)
    raw = raw * (1.0 / math.sqrt(HDIM))
    return jnp.where(allowed[:, None], raw, -1e30)


def collect(
    w_qkv,
    w_out,
    w_up,
    w_down,
    gain_one,
    shift_one,
    bias_query,
    bias_value,
    bias_out,
    gain_two,
    shift_two,
    bias_up,
    bias_down,
):
    return (
        lax.all_gather(w_qkv, ("gx", "gy"), axis=0, tiled=True),
        lax.all_gather(w_out, ("gx", "gy"), axis=0, tiled=True),
        lax.all_gather(w_up, ("gx", "gy"), axis=0, tiled=True),
        lax.all_gather(w_down, ("gx", "gy"), axis=0, tiled=True),
        lax.all_gather(gain_one, ("gx", "gy"), axis=0, tiled=True),
        lax.all_gather(shift_one, ("gx", "gy"), axis=0, tiled=True),
        lax.all_gather(bias_query, ("gx", "gy"), axis=0, tiled=True),
        lax.all_gather(bias_value, ("gx", "gy"), axis=0, tiled=True),
        lax.all_gather(bias_out, ("gx", "gy"), axis=0, tiled=True),
        lax.all_gather(gain_two, ("gx", "gy"), axis=0, tiled=True),
        lax.all_gather(shift_two, ("gx", "gy"), axis=0, tiled=True),
        lax.all_gather(bias_up, ("gx", "gy"), axis=0, tiled=True),
        lax.all_gather(bias_down, ("gx", "gy"), axis=0, tiled=True),
    )


def generic_device(
    tokens,
    segment_ids,
    pad_mask,
    w_qkv,
    w_out,
    w_up,
    w_down,
    gain_one,
    shift_one,
    bias_query,
    bias_value,
    bias_out,
    gain_two,
    shift_two,
    bias_up,
    bias_down,
    cotangent,
):
    row_count, length, width = tokens.shape
    total_rows = row_count * length
    gathered = collect(
        w_qkv,
        w_out,
        w_up,
        w_down,
        gain_one,
        shift_one,
        bias_query,
        bias_value,
        bias_out,
        gain_two,
        shift_two,
        bias_up,
        bias_down,
    )
    full_qkv, full_out, full_up, full_down = (gathered[0], gathered[1], gathered[2], gathered[3])
    gain_first = gathered[4].astype(jnp.float32)
    shift_first = gathered[5].astype(jnp.float32)
    query_bias = gathered[6].astype(jnp.float32)
    value_bias = gathered[7].astype(jnp.float32)
    out_bias = gathered[8].astype(jnp.float32)
    gain_second = gathered[9].astype(jnp.float32)
    shift_second = gathered[10].astype(jnp.float32)
    up_bias = gathered[11].astype(jnp.float32)
    down_bias = gathered[12].astype(jnp.float32)
    allowed = attend_mask(segment_ids, pad_mask)
    inputs = tokens.astype(jnp.float32).reshape(total_rows, width)
    first_norm, first_pull = jax.vjp(layer_norm, inputs, gain_first, shift_first)
    normed = first_norm.astype(jnp.bfloat16)
    mixed = jnp.dot(normed, full_qkv, preferred_element_type=jnp.float32)
    query_part = (
        (mixed[:, :width] + query_bias).astype(jnp.bfloat16).reshape(row_count, length, HEADS, HDIM)
    )
    key_part = (
        mixed[:, width : 2 * width].astype(jnp.bfloat16).reshape(row_count, length, HEADS, HDIM)
    )
    value_part = (
        (mixed[:, 2 * width :] + value_bias)
        .astype(jnp.bfloat16)
        .reshape(row_count, length, HEADS, HDIM)
    )
    scores = score_block(query_part, key_part, allowed)
    highest = jnp.max(scores, axis=-1, keepdims=True)
    log_total = highest + jnp.log(jnp.sum(jnp.exp(scores - highest), axis=-1, keepdims=True))
    weights = jnp.exp(scores - log_total).astype(jnp.bfloat16)
    attended = jnp.einsum(
        "rhqk,rkhe->rqhe", weights, value_part, preferred_element_type=jnp.float32
    )
    attended = attended.reshape(total_rows, width).astype(jnp.bfloat16)
    middle = inputs + jnp.dot(attended, full_out, preferred_element_type=jnp.float32) + out_bias
    second_norm, second_pull = jax.vjp(layer_norm, middle, gain_second, shift_second)
    normed_two = second_norm.astype(jnp.bfloat16)
    hidden = jnp.dot(normed_two, full_up, preferred_element_type=jnp.float32) + up_bias
    active, gate_pull = jax.vjp(smooth_gate, hidden)
    active_low = active.astype(jnp.bfloat16)
    result = middle + jnp.dot(active_low, full_down, preferred_element_type=jnp.float32) + down_bias
    output = result.astype(jnp.bfloat16).reshape(row_count, length, width)
    again = collect(
        w_qkv,
        w_out,
        w_up,
        w_down,
        gain_one,
        shift_one,
        bias_query,
        bias_value,
        bias_out,
        gain_two,
        shift_two,
        bias_up,
        bias_down,
    )
    full_qkv, full_out, full_up, full_down = (again[0], again[1], again[2], again[3])
    down_in = cotangent.reshape(total_rows, width)
    outer_grad = down_in.astype(jnp.float32)
    grad_bias_down = jnp.sum(outer_grad, axis=0)
    grad_w_down = outer_sum(active_low, down_in)
    active_grad = against(down_in, full_down)
    hidden_grad = gate_pull(active_grad)[0].astype(jnp.bfloat16)
    grad_bias_up = jnp.sum(hidden_grad.astype(jnp.float32), axis=0)
    grad_w_up = outer_sum(normed_two, hidden_grad)
    norm_two_grad = against(hidden_grad, full_up)
    middle_part, grad_gain_two, grad_shift_two = second_pull(norm_two_grad)
    middle_grad = outer_grad + middle_part
    branch_grad = middle_grad.astype(jnp.bfloat16)
    grad_bias_out = jnp.sum(branch_grad.astype(jnp.float32), axis=0)
    grad_w_out = outer_sum(attended, branch_grad)
    attended_grad = (
        against(branch_grad, full_out).astype(jnp.bfloat16).reshape(row_count, length, HEADS, HDIM)
    )
    probs = jnp.exp(score_block(query_part, key_part, allowed) - log_total)
    probs_low = probs.astype(jnp.bfloat16)
    value_grad = jnp.einsum(
        "rhqk,rqhe->rkhe", probs_low, attended_grad, preferred_element_type=jnp.float32
    ).astype(jnp.bfloat16)
    prob_grad = jnp.einsum(
        "rqhe,rkhe->rhqk", attended_grad, value_part, preferred_element_type=jnp.float32
    )
    inner_term = jnp.sum(prob_grad * probs, axis=-1, keepdims=True)
    score_grad = (probs * (prob_grad - inner_term)).astype(jnp.bfloat16)
    score_scale = 1.0 / math.sqrt(HDIM)
    query_grad = (
        (
            jnp.einsum("rhqk,rkhe->rqhe", score_grad, key_part, preferred_element_type=jnp.float32)
            * score_scale
        )
        .astype(jnp.bfloat16)
        .reshape(total_rows, width)
    )
    key_grad = (
        (
            jnp.einsum(
                "rhqk,rqhe->rkhe", score_grad, query_part, preferred_element_type=jnp.float32
            )
            * score_scale
        )
        .astype(jnp.bfloat16)
        .reshape(total_rows, width)
    )
    value_flat = value_grad.reshape(total_rows, width)
    mixed_grad = jnp.concatenate([query_grad, key_grad, value_flat], axis=1)
    grad_bias_query = jnp.sum(query_grad.astype(jnp.float32), axis=0)
    grad_bias_value = jnp.sum(value_flat.astype(jnp.float32), axis=0)
    grad_w_qkv = outer_sum(normed, mixed_grad)
    norm_one_grad = against(mixed_grad, full_qkv)
    input_part, grad_gain_one, grad_shift_one = first_pull(norm_one_grad)
    grad_tokens = (middle_grad + input_part).reshape(row_count, length, width)
    shares = (
        lax.psum_scatter(grad_w_qkv, ("gx", "gy"), scatter_dimension=0, tiled=True),
        lax.psum_scatter(grad_w_out, ("gx", "gy"), scatter_dimension=0, tiled=True),
        lax.psum_scatter(grad_w_up, ("gx", "gy"), scatter_dimension=0, tiled=True),
        lax.psum_scatter(grad_w_down, ("gx", "gy"), scatter_dimension=0, tiled=True),
        lax.psum_scatter(grad_gain_one, ("gx", "gy"), scatter_dimension=0, tiled=True),
        lax.psum_scatter(grad_shift_one, ("gx", "gy"), scatter_dimension=0, tiled=True),
        lax.psum_scatter(grad_bias_query, ("gx", "gy"), scatter_dimension=0, tiled=True),
        lax.psum_scatter(grad_bias_value, ("gx", "gy"), scatter_dimension=0, tiled=True),
        lax.psum_scatter(grad_bias_out, ("gx", "gy"), scatter_dimension=0, tiled=True),
        lax.psum_scatter(grad_gain_two, ("gx", "gy"), scatter_dimension=0, tiled=True),
        lax.psum_scatter(grad_shift_two, ("gx", "gy"), scatter_dimension=0, tiled=True),
        lax.psum_scatter(grad_bias_up, ("gx", "gy"), scatter_dimension=0, tiled=True),
        lax.psum_scatter(grad_bias_down, ("gx", "gy"), scatter_dimension=0, tiled=True),
    )
    return (
        output,
        grad_tokens,
        shares[0],
        shares[1],
        shares[2],
        shares[3],
        shares[4],
        shares[5],
        shares[6],
        shares[7],
        shares[8],
        shares[9],
        shares[10],
        shares[11],
        shares[12],
    )


CHIPS = ("z", "y", "x")
AXES = CHIPS + ("core",)


def pairs(move):
    out = []
    for d in range(32):
        z, y, x, c = d // 8, (d // 4) % 2, (d // 2) % 2, d % 2
        z, y, x, c = move(z, y, x, c)
        out.append((d, ((z * 2 + y) * 2 + x) * 2 + c))
    return out


SWAP_C = pairs(lambda z, y, x, c: (z, y, x, 1 - c))
SWAP_X = pairs(lambda z, y, x, c: (z, y, 1 - x, c))
SWAP_Y = pairs(lambda z, y, x, c: (z, 1 - y, x, c))
SWAP_D = pairs(lambda z, y, x, c: (z, 1 - y, 1 - x, c))
SWAP_Z = [None] + [pairs(lambda z, y, x, c, k=k: (z ^ k, y, x, c)) for k in (1, 2, 3)]


def send(values, perm):
    return lax.ppermute(values, AXES, perm)


def place():
    return tuple(lax.axis_index(name) for name in AXES)


LOW = jnp.bfloat16
FULL = jnp.float32
ANY = pl.BlockSpec(memory_space=pl.ANY)
SMEM = pl.BlockSpec(memory_space=pltpu.SMEM)
MIB = 1024 * 1024


def whole(shape):
    zeros = (0,) * len(shape)
    return pl.BlockSpec(shape, lambda *_: zeros, pipeline_mode=pl.Buffered(1))


def params(limit=56):
    return pltpu.CompilerParams(vmem_limit_bytes=limit * MIB)


def cost(flops, read, exps=0, scale=10.0):
    return pl.CostEstimate(
        flops=int(scale * flops), bytes_accessed=int(scale * read), transcendentals=int(scale * exps)
    )


def mul(left, right):
    return lax.dot_general(left, right, (((1,), (0,)), ((), ())), preferred_element_type=FULL)


def mul_t(left, right):
    return lax.dot_general(left, right, (((1,), (1,)), ((), ())), preferred_element_type=FULL)


def t_mul(left, right):
    return lax.dot_general(left, right, (((0,), (0,)), ((), ())), preferred_element_type=FULL)


def first_kernel(qkv, v0, v1, v2, v3, v4, v5, v6, v7, up, out, tall):
    out[:, 0:2304] = qkv[...]
    tall[...] = jnp.zeros_like(tall)
    for row, vector in enumerate((v0, v1, v2, v3, v4, v5, v6, v7)):
        tall[row : row + 1, 0:24] = vector[...].astype(FULL).reshape(1, 24)
    turned = jnp.transpose(tall[...])[0:24]
    lane = lax.broadcasted_iota(jnp.int32, (24, 128), 1)
    row = lax.broadcasted_iota(jnp.int32, (24, 128), 0)
    tall[0:1, 16:112] = up[...].astype(FULL).reshape(1, 96)
    line = jnp.broadcast_to(tall[0:1, :], (24, 128))
    keep = (row == 0) & (lane >= 16) & (lane < 112)
    out[:, 2304:2432] = jnp.where(lane < 8, turned, jnp.where(keep, line, 0.0)).astype(LOW)


def first_call(qkv, vectors):
    return pl.pallas_call(
        first_kernel,
        out_shape=jax.ShapeDtypeStruct((24, 2432), LOW),
        in_specs=[pl.BlockSpec(memory_space=pltpu.VMEM)] * 10,
        out_specs=pl.BlockSpec(memory_space=pltpu.VMEM),
        scratch_shapes=[pltpu.VMEM((128, 128), FULL)],
        compiler_params=params(),
        cost_estimate=cost(1e5, 3e5),
        name="first",
    )(qkv, *vectors)


def prep_kernel(where, out_m, up_m, down_m, out_s, up_s, down_s, p2, p3):
    def build(core):
        pairs_of = lambda m, s: (m, s) if core == 0 else (s, m)

        def rows(m, s, at, width):
            both = [v[:, at : at + width].astype(FULL) for v in pairs_of(m, s)]
            return jnp.concatenate(both, axis=0).astype(LOW)

        p2[:, 0:1536] = rows(up_m, up_s, core * 1536, 1536)
        p2[:, 1536:1920] = rows(out_m, out_s, core * 384, 384)
        for k, down in enumerate(pairs_of(down_m, down_s)):
            p3[k * 96 : k * 96 + 96, :] = down[:, core * 384 : core * 384 + 384]

    for core in range(2):
        pl.when(where[3] == core)(functools.partial(build, core))


def prep(where, mine, theirs):
    return pl.pallas_call(
        prep_kernel,
        out_shape=[jax.ShapeDtypeStruct((48, 1920), LOW), jax.ShapeDtypeStruct((192, 384), LOW)],
        in_specs=[SMEM] + [pl.BlockSpec(memory_space=pltpu.VMEM)] * 6,
        out_specs=[pl.BlockSpec(memory_space=pltpu.VMEM)] * 2,
        compiler_params=params(),
        cost_estimate=cost(1e6, 2e6),
        name="prep",
    )(where, *mine, *theirs)


def chip_of(where, dz, dy, dx):
    return ((where[0] ^ dz) * 2 + (where[1] ^ dy)) * 2 + (where[2] ^ dx)


def load_pack(where, pieces, start):
    for side in range(2):
        owner = where[3] ^ side
        col, along_x, along_y, far0, far1 = pieces[side * 5 : side * 5 + 5]
        for dz in range(4):
            far = far0.at[dz] if dz < 2 else far1.at[dz - 2]
            for dy, dx, source in ((0, 0, col.at[dz]), (0, 1, along_x.at[dz]), (1, 0, along_y.at[dz]), (1, 1, far)):
                start(source, chip_of(where, dz, dy, dx), owner)


def wait_pack(target, sem):
    pltpu.make_async_copy(target, target, sem).wait()


def normalise(values):
    centre = values - jnp.mean(values, axis=1, keepdims=True)
    spread = lax.rsqrt(jnp.mean(centre * centre, axis=1, keepdims=True) + 1e-6)
    return centre * spread, spread


def qkv_kernel(where, tok, *refs):
    pieces, (qkv, normed, w1, vec, bias_up, buf, weights, sem) = refs[:10], refs[10:]
    half = pl.program_id(0)

    @pl.when(half == 0)
    def _():
        load_pack(
            where, pieces, lambda v, chip, core: pltpu.make_async_copy(v, buf.at[chip * 2 + core], sem).start()
        )
        wait_pack(buf, sem)
        lines = jnp.concatenate([buf[d, :, 2304:2432].astype(FULL) for d in range(32)], axis=0)
        lines = jnp.transpose(lines)
        vec[...] = lines[0:16]
        for chip in range(16):
            for s in range(2):
                line = buf[chip * 2 + s, 0:8, 2304:2432].astype(FULL)[0:1]
                at = (chip * 2 + s) * 96
                bias_up[0:1, at : at + 96] = line[:, 16:112]
        for t in range(4):
            at = slice(t * 256, t * 256 + 256)
            xhat, _ = normalise(tok[at, :].astype(FULL))
            normed[at, :] = (xhat * lines[0:1] + lines[1:2]).astype(LOW)

    def gather(h):
        for chip in range(16):
            rows = slice(chip * 48, chip * 48 + 48)
            for part in range(3):
                at = slice(part * 768 + h * 384, part * 768 + h * 384 + 384)
                both = [buf[chip * 2 + s, :, at].astype(FULL) for s in range(2)]
                weights[rows, part * 384 : part * 384 + 384] = jnp.concatenate(both, axis=0).astype(LOW)

    for h in range(2):
        pl.when(half == h)(functools.partial(gather, h))
    w1[0] = weights[...]
    at = pl.multiple_of(half * 384, 128)
    query_bias = vec[2:3, pl.ds(at, 384)]
    value_bias = vec[3:4, pl.ds(at, 384)]
    for t in range(4):
        at = slice(t * 256, t * 256 + 256)
        mixed = mul(normed[at, :], weights[...])
        qkv[0, at, 0:384] = (mixed[:, 0:384] + query_bias).astype(LOW) * 0.125
        qkv[0, at, 384:768] = mixed[:, 384:768].astype(LOW)
        qkv[0, at, 768:1152] = (mixed[:, 768:1152] + value_bias).astype(LOW)


def qkv_call(where, tokens, pieces):
    return pl.pallas_call(
        qkv_kernel,
        grid=(2,),
        out_shape=[
            jax.ShapeDtypeStruct((2, 1024, 1152), LOW),
            jax.ShapeDtypeStruct((1024, 768), LOW),
            jax.ShapeDtypeStruct((2, 768, 1152), LOW),
            jax.ShapeDtypeStruct((16, 768), FULL),
            jax.ShapeDtypeStruct((1, 3072), FULL),
        ],
        in_specs=[SMEM, whole((1024, 768))] + [ANY] * 10,
        out_specs=[
            pl.BlockSpec((1, 1024, 1152), lambda h: (h, 0, 0)),
            whole((1024, 768)),
            pl.BlockSpec((1, 768, 1152), lambda h: (h, 0, 0)),
            whole((16, 768)),
            whole((1, 3072)),
        ],
        scratch_shapes=[
            pltpu.VMEM((32, 24, 2432), LOW),
            pltpu.VMEM((768, 1152), LOW),
            pltpu.SemaphoreType.DMA,
        ],
        compiler_params=params(),
        cost_estimate=cost(2 * 1024 * 768 * 2304, 16e6, scale=0.1),
        name="qkv",
    )(where, tokens, *pieces)


def masked_pair(block):
    lane = lax.broadcasted_iota(jnp.int32, block.shape, 1)
    zero = jnp.zeros_like(block)
    return jnp.concatenate([jnp.where(lane < 64, block, zero), jnp.where(lane < 64, zero, block)], axis=0)


def unmask(both):
    return jnp.concatenate([both[0:64, 0:128], both[64:128, 128:256]], axis=0)


def attend_kernel(first, qkv, seg, pad, *refs):
    probs, att_t, bias, wide = refs[-4:]
    row = pl.program_id(0) + first
    seg_row, pad_row = seg[pl.ds(row, 1), :].astype(FULL), pad[pl.ds(row, 1), :].astype(FULL)
    seg_col = jnp.transpose(jnp.broadcast_to(seg_row, (128, 256)))
    pad_col = jnp.transpose(jnp.broadcast_to(pad_row, (128, 256)))
    for b in range(2):
        keys = slice(64 * b, 64 * b + 192)
        same = seg_col[keys] == jnp.broadcast_to(seg_row[:, 128 * b : 128 * b + 128], (192, 128))
        key_at = lax.broadcasted_iota(jnp.int32, (192, 128), 0) + 64 * b
        query_at = lax.broadcasted_iota(jnp.int32, (192, 128), 1) + 128 * b
        allowed = same & ((pad_col[keys] == 1.0) | (key_at == query_at))
        one = jnp.where(allowed, 0.0, -1e30)
        bias[b] = jnp.concatenate([one, one], axis=1)
    blocks = [(half, p, b) for half in range(2) for p in range(3) for b in range(2)]
    for i, (half, p, b) in enumerate(blocks):
        stack = masked_pair(qkv[half, 128 * b : 128 * b + 128, p * 128 : p * 128 + 128])
        keys = slice(64 * b, 64 * b + 192)
        wide[i] = mul_t(qkv[half, keys, 384 + p * 128 : 512 + p * 128], stack) + bias[b]
    for i, (half, p, b) in enumerate(blocks):
        scores = wide[i]
        power = jnp.exp(scores - jnp.max(scores, axis=0, keepdims=True))
        probs[0, p, half, b] = (power * (1.0 / jnp.sum(power, axis=0, keepdims=True))).astype(LOW)
    for half, p, b in blocks:
        keys = slice(64 * b, 64 * b + 192)
        both = t_mul(qkv[half, keys, 768 + p * 128 : 896 + p * 128], probs[0, p, half, b])
        at = half * 384 + p * 128
        att_t[at : at + 128, 128 * b : 128 * b + 128] = unmask(both).astype(LOW)


def attend_call(first, count, qkv, seg, pad, before):
    old = list(before or [])
    return pl.pallas_call(
        functools.partial(attend_kernel, first),
        grid=(count,),
        out_shape=[
            jax.ShapeDtypeStruct((4, 3, 2, 2, 192, 256), LOW),
            jax.ShapeDtypeStruct((768, 1024), LOW),
        ],
        in_specs=[pl.BlockSpec((2, 256, 1152), lambda r: (0, r + first, 0)), whole((4, 256)), whole((4, 256))]
        + [ANY] * len(old),
        out_specs=[
            pl.BlockSpec((1, 3, 2, 2, 192, 256), lambda r: (r + first, 0, 0, 0, 0, 0)),
            pl.BlockSpec((768, 256), lambda r: (0, r + first)),
        ],
        input_output_aliases={3: 0, 4: 1} if old else {},
        scratch_shapes=[pltpu.VMEM((2, 192, 256), FULL), pltpu.VMEM((12, 192, 256), FULL)],
        compiler_params=params(),
        cost_estimate=cost(count * 1.5e9, count * 3e6, 8e5, scale=0.1),
        name="attend%d" % first,
    )(qkv, seg, pad, *old)


GATE = math.sqrt(2.0 / math.pi)


def gate_pair(u):
    square = u * u
    factor = 0.5 + 0.5 * jnp.tanh(u * (GATE + GATE * 0.044715 * square))
    value = u * factor
    return value, factor + value * (1.0 - factor) * (2.0 * GATE + 6.0 * GATE * 0.044715 * square)


def load_up(where, pieces, up, w_out, sem):
    def start(block, chip, core):
        rows = pl.ds(pl.multiple_of(chip * 48, 16), 48)
        for source, target, width in ((slice(0, 1536), up, 1536), (slice(1536, 1920), w_out, 384)):
            columns = pl.ds(pl.multiple_of(core * width, 128), width)
            pltpu.make_async_copy(block.at[:, source], target.at[rows, columns], sem).start()

    load_pack(where, pieces, start)


def up_kernel(where, att_t, tok, bias, vec, *refs):
    pieces = refs[:10]
    middle, normed, act, slope, up, w_out, sem = refs[10:]

    @pl.when(pl.program_id(0) == 0)
    def _():
        load_up(where, pieces, up, w_out, sem)
        wait_pack(up, sem)
        wait_pack(w_out, sem)

    mid = tok[...].astype(FULL) + t_mul(att_t[...], w_out[...]) + vec[4:5, :]
    middle[...] = mid
    xhat, _ = normalise(mid)
    rows = (xhat * vec[5:6, :] + vec[6:7, :]).astype(LOW)
    normed[...] = rows
    for s in range(2):
        at = slice(s * 1536, s * 1536 + 1536)
        value, tilt = gate_pair(mul(rows, up[:, at]) + bias[:, at])
        act[:, at] = value.astype(LOW)
        slope[:, at] = tilt.astype(LOW)


def up_call(where, att_t, tokens, bias_up, vec, pieces):
    rows = lambda width: pl.BlockSpec((256, width), lambda t: (t, 0))
    return pl.pallas_call(
        up_kernel,
        grid=(4,),
        out_shape=[
            jax.ShapeDtypeStruct((1024, 768), FULL),
            jax.ShapeDtypeStruct((1024, 768), LOW),
            jax.ShapeDtypeStruct((1024, 3072), LOW),
            jax.ShapeDtypeStruct((1024, 3072), LOW),
        ],
        in_specs=[
            SMEM, pl.BlockSpec((768, 256), lambda t: (0, t)), rows(768), whole((1, 3072)), whole((16, 768)),
        ] + [ANY] * 10,
        out_specs=[rows(768), rows(768), rows(3072), rows(3072)],
        scratch_shapes=[
            pltpu.VMEM((768, 3072), LOW),
            pltpu.VMEM((768, 768), LOW),
            pltpu.SemaphoreType.DMA,
        ],
        compiler_params=params(),
        cost_estimate=cost(5 * 1024 * 768 * 768 * 2, 25e6, 3e6, scale=0.1),
        name="up",
    )(where, att_t, tokens, bias_up, vec, *pieces)


def down_kernel(where, middle, act, slope, cot, vec, own, other, output, hid, bias_grad, down, sem):
    step = pl.program_id(0)

    @pl.when(step == 0)
    def _():
        for side, source in ((0, own), (1, other)):
            at = pl.multiple_of((where[3] ^ side) * 384, 128)
            pltpu.make_async_copy(source, down.at[:, pl.ds(at, 384)], sem).start()
        wait_pack(down, sem)

    output[...] = (middle[...] + vec[7:8, :] + mul(act[...], down[...])).astype(LOW)
    for s in range(2):
        at = slice(s * 1536, s * 1536 + 1536)
        grad = (slope[:, at].astype(FULL) * mul_t(cot[...], down[at, :])).astype(LOW)
        hid[:, at] = grad
        line = jnp.sum(grad.astype(FULL), axis=0, keepdims=True)

        @pl.when(step == 0)
        def _():
            bias_grad[:, at] = line

        @pl.when(step > 0)
        def _():
            bias_grad[:, at] += line


def down_call(where, middle, act, slope, cot, vec, own, other):
    rows = lambda width: pl.BlockSpec((256, width), lambda t: (t, 0))
    return pl.pallas_call(
        down_kernel,
        grid=(4,),
        out_shape=[
            jax.ShapeDtypeStruct((1024, 768), LOW),
            jax.ShapeDtypeStruct((1024, 3072), LOW),
            jax.ShapeDtypeStruct((1, 3072), FULL),
        ],
        in_specs=[SMEM, rows(768), rows(3072), rows(3072), rows(768), whole((16, 768)), ANY, ANY],
        out_specs=[rows(768), rows(3072), whole((1, 3072))],
        scratch_shapes=[pltpu.VMEM((3072, 768), LOW), pltpu.SemaphoreType.DMA],
        compiler_params=params(),
        cost_estimate=cost(8 * 1024 * 768 * 768 * 2, 30e6),
        name="down",
    )(where, middle, act, slope, cot, vec, own, other)


def down_grads_kernel(where, act, cot, mine, theirs):
    grad = t_mul(act[...], cot[...]).astype(LOW)

    def put(side):
        for h, dest in ((side, mine), (1 - side, theirs)):
            for k in range(4):
                spot = ((k // 2) ^ where[1], (k % 2) ^ where[2], 0)
                dest[spot] = grad[k * 192 : k * 192 + 192, h * 384 : h * 384 + 384]

    for side in range(2):
        pl.when(where[3] == side)(functools.partial(put, side))


def down_grads_call(where, act, cot):
    shape = (2, 2, 4, 192, 384)
    block = pl.BlockSpec((2, 2, 1, 192, 384), lambda z, where: (0, 0, z ^ where[0], 0, 0))
    return pl.pallas_call(
        down_grads_kernel,
        grid_spec=pltpu.PrefetchScalarGridSpec(
            num_scalar_prefetch=1,
            grid=(4,),
            in_specs=[
                pl.BlockSpec((1024, 768), lambda z, where: (0, z)),
                pl.BlockSpec((1024, 768), lambda z, where: (0, 0), pipeline_mode=pl.Buffered(1)),
            ],
            out_specs=[block, block],
        ),
        out_shape=[jax.ShapeDtypeStruct(shape, LOW)] * 2,
        compiler_params=params(),
        cost_estimate=cost(4 * 1024 * 768 * 768 * 2, 13e6, scale=0.1),
        name="down_grads",
    )(where, act, cot)


def up_grads_kernel(where, normed, hid, mine, theirs):
    step = pl.program_id(0)
    grad = t_mul(normed[...], hid[...]).astype(LOW)

    def put(dest):
        for chip in range(16):
            spot = ((chip // 2 % 2) ^ where[1], (chip % 2) ^ where[2], (chip // 4) ^ where[0])
            dest[spot] = grad[chip * 48 : chip * 48 + 48]

    pl.when(step < 2)(functools.partial(put, theirs))
    pl.when(step >= 2)(functools.partial(put, mine))


def up_grads_call(where, normed, hid):
    shape = (2, 2, 4, 48, 1536)
    half = (2, 2, 4, 48, 768)
    return pl.pallas_call(
        up_grads_kernel,
        grid_spec=pltpu.PrefetchScalarGridSpec(
            num_scalar_prefetch=1,
            grid=(4,),
            in_specs=[
                pl.BlockSpec((1024, 768), lambda j, where: (0, 0), pipeline_mode=pl.Buffered(1)),
                pl.BlockSpec((1024, 768), lambda j, where: (0, ((j // 2) ^ where[3] ^ 1) * 2 + j % 2)),
            ],
            out_specs=[
                pl.BlockSpec(half, lambda j, where: (0, 0, 0, 0, jnp.maximum(j - 2, 0))),
                pl.BlockSpec(half, lambda j, where: (0, 0, 0, 0, jnp.minimum(j, 1))),
            ],
        ),
        out_shape=[jax.ShapeDtypeStruct(shape, LOW)] * 2,
        compiler_params=params(),
        cost_estimate=cost(4 * 1024 * 768 * 768 * 2, 13e6),
        name="up_grads",
    )(where, normed, hid)


def branch_kernel(where, hid, middle, cot, vec, *refs):
    pieces = refs[:10]
    middle_grad, branch_grad, att_grad, sums, up, w_out, sem = refs[10:]
    step = pl.program_id(0)

    @pl.when(step == 0)
    def _():
        load_up(where, pieces, up, w_out, sem)
        wait_pack(up, sem)
        wait_pack(w_out, sem)

    grad, outer = mul_t(hid[...], up[...]), cot[...].astype(FULL)
    xhat, spread = normalise(middle[...])
    mid_grad = outer + back_norm(grad, xhat, spread, vec[5:6, :])
    middle_grad[...] = mid_grad
    low = mid_grad.astype(LOW)
    branch_grad[...] = low
    add_rows(sums, 0, grad * xhat, step)
    add_rows(sums, 1, grad, step)
    add_rows(sums, 2, low.astype(FULL), step)
    add_rows(sums, 3, outer, step)
    att_grad[...] = mul_t(low, w_out[...]).astype(LOW)


def branch_call(where, hid, middle, cot, vec, pieces):
    rows = lambda width: pl.BlockSpec((256, width), lambda t: (t, 0))
    return pl.pallas_call(
        branch_kernel,
        grid=(4,),
        out_shape=[
            jax.ShapeDtypeStruct((1024, 768), FULL),
            jax.ShapeDtypeStruct((1024, 768), LOW),
            jax.ShapeDtypeStruct((1024, 768), LOW),
            jax.ShapeDtypeStruct((8, 768), FULL),
        ],
        in_specs=[SMEM, rows(3072), rows(768), rows(768), whole((16, 768))] + [ANY] * 10,
        out_specs=[rows(768), rows(768), rows(768), whole((8, 768))],
        scratch_shapes=[
            pltpu.VMEM((768, 3072), LOW),
            pltpu.VMEM((768, 768), LOW),
            pltpu.SemaphoreType.DMA,
        ],
        compiler_params=params(),
        cost_estimate=cost(5 * 1024 * 768 * 768 * 2, 25e6),
        name="branch",
    )(where, hid, middle, cot, vec, *pieces)


def back_norm(grad, xhat, spread, gain):
    scaled = grad * gain
    flat = jnp.mean(scaled, axis=1, keepdims=True)
    tilt = jnp.mean(scaled * xhat, axis=1, keepdims=True)
    return (scaled - flat - xhat * tilt) * spread


def add_rows(target, row, values, step):
    value = jnp.sum(values, axis=0, keepdims=True)

    @pl.when(step == 0)
    def _():
        target[row : row + 1, :] = value

    @pl.when(step > 0)
    def _():
        target[row : row + 1, :] += value


ROWS_STEP = 2


def unattend_kernel(groups, with_out, where, *refs):
    count = len(groups)
    parts = [refs[5 * g : 5 * g + 5] for g in range(count)]
    refs = refs[5 * count :]
    probs, normed = refs[:count], refs[count]
    refs = refs[count + 1 :]
    if with_out:
        att_t, branch_grad, refs = refs[0], refs[1], refs[2:]
        mixed, mine, theirs, sums, acc, wide, slim, stacks, out_acc = refs
    else:
        mixed, mine, theirs, sums, acc, wide, slim, stacks = refs
    step = pl.program_id(0)
    width = 128 * count
    blocks = [(r, g, h) for r in range(ROWS_STEP) for g in range(count) for h in range(2)]

    def keys_of(r, b):
        return slice(256 * r + 64 * b, 256 * r + 64 * b + 192)

    def queries_of(r, b):
        return slice(256 * r + 128 * b, 256 * r + 128 * b + 128)

    for i, (r, g, half) in enumerate(blocks):
        query, key, value = parts[g][:3]
        grads = parts[g][3 + half]
        for b in range(2):
            stacks[0, 2 * i + b] = masked_pair(query[half, queries_of(r, b), :])
            stack = masked_pair(grads[queries_of(r, b), :])
            stacks[1, 2 * i + b] = stack
            wide[2 * i + b] = mul_t(value[half, keys_of(r, b), :], stack)
    for i, (r, g, half) in enumerate(blocks):
        for b in range(2):
            weights = probs[g][r, 0, half, b].astype(FULL)
            prob_grad = wide[2 * i + b]
            inner = jnp.sum(prob_grad * weights, axis=0, keepdims=True)
            slim[2 * i + b] = (weights * (prob_grad - inner)).astype(LOW)

    def merge(first, second):
        return jnp.concatenate([first[0:64], first[64:192] + second[0:128], second[128:192]], axis=0)

    for i, (r, g, half) in enumerate(blocks):
        key = parts[g][1]
        rows = slice(256 * r, 256 * r + 256)
        value_grad = [mul(probs[g][r, 0, half, b], stacks[1, 2 * i + b]) for b in range(2)]
        key_grad = [mul(slim[2 * i + b], stacks[0, 2 * i + b]) for b in range(2)]
        turned = [unmask(t_mul(key[half, keys_of(r, b), :], slim[2 * i + b])) for b in range(2)]
        query_grad = jnp.transpose(jnp.concatenate(turned, axis=1)) * 0.125
        at = g * 128
        mixed[half, rows, at : at + 128] = query_grad.astype(LOW)
        mixed[half, rows, width + at : width + at + 128] = merge(*key_grad).astype(LOW)
        mixed[half, rows, 2 * width + at : 2 * width + at + 128] = merge(*value_grad).astype(LOW)

    def add(target, more):
        @pl.when(step == 0)
        def _():
            target[...] = more

        @pl.when(step > 0)
        def _():
            target[...] += more

    for half in range(2):
        add_rows(sums.at[half], 0, mixed[half].astype(FULL), step)
        add(acc.at[half], t_mul(normed[...], mixed[half]))
    if with_out:
        add(out_acc, mul(att_t[...], branch_grad[...]))

    def write(side):
        for half in range(2):
            dest = mine if half == side else theirs
            for chip in range(16):
                at = chip * 48
                spot = ((chip // 2 % 2) ^ where[1], (chip % 2) ^ where[2], (chip // 4) ^ where[0], slice(None))
                low = acc[half, at : at + 48, :].astype(LOW)
                if with_out:
                    dest[spot + (slice(0, 384),)] = out_acc[at : at + 48, half * 384 : half * 384 + 384].astype(LOW)
                    dest[spot + (slice(384, 384 + 3 * width),)] = low
                else:
                    dest[spot + (slice(None),)] = low

    for side in range(2):
        pl.when((step == 4 // ROWS_STEP - 1) & (where[3] == side))(functools.partial(write, side))


def unattend_call(groups, where, qkv, att_grad, probs, normed, att_t=None, branch_grad=None):
    with_out = att_t is not None
    count = len(groups)
    width = 384 * count
    tall = 256 * ROWS_STEP
    operands, specs = [], []
    for p in groups:
        for part in range(3):
            operands.append(qkv)
            specs.append(pl.BlockSpec((2, tall, 128), lambda r, c=part * 3 + p: (0, r, c)))
        for half in range(2):
            operands.append(att_grad)
            specs.append(pl.BlockSpec((tall, 128), lambda r, c=half * 3 + p: (r, c)))
    for p in groups:
        operands.append(probs)
        specs.append(pl.BlockSpec((ROWS_STEP, 1, 2, 2, 192, 256), lambda r, p=p: (r, p, 0, 0, 0, 0)))
    operands.append(normed)
    specs.append(pl.BlockSpec((tall, 768), lambda r: (r, 0)))
    if with_out:
        operands += [att_t, branch_grad]
        specs += [pl.BlockSpec((768, tall), lambda r: (0, r)), pl.BlockSpec((tall, 768), lambda r: (r, 0))]
    shape = (2, 2, 4, 48, width + (384 if with_out else 0))
    many = 4 * count * ROWS_STEP
    return pl.pallas_call(
        functools.partial(unattend_kernel, groups, with_out),
        grid=(4 // ROWS_STEP,),
        out_shape=[
            jax.ShapeDtypeStruct((2, 1024, width), LOW),
            jax.ShapeDtypeStruct(shape, LOW),
            jax.ShapeDtypeStruct(shape, LOW),
            jax.ShapeDtypeStruct((2, 8, width), FULL),
        ],
        in_specs=[SMEM] + specs,
        out_specs=[
            pl.BlockSpec((2, tall, width), lambda r: (0, r, 0)),
            whole(shape),
            whole(shape),
            whole((2, 8, width)),
        ],
        scratch_shapes=[
            pltpu.VMEM((2, 768, width), FULL),
            pltpu.VMEM((many, 192, 256), FULL),
            pltpu.VMEM((many, 192, 256), LOW),
            pltpu.VMEM((2, many, 256, 128), LOW),
        ] + ([pltpu.VMEM((768, 768), FULL)] if with_out else []),
        compiler_params=params(),
        cost_estimate=cost(count * 2.5e9, count * 8e6),
        name="unattend%d" % groups[0],
    )(where, *operands)


def tokens_kernel(m0, m1, w1, tok, vec, middle_grad, grad, lines):
    step = pl.program_id(0)
    total = None
    for half in range(2):
        joined = []
        for part in range(3):
            joined.append(m0[half, :, part * 128 : part * 128 + 128])
            joined.append(m1[half, :, part * 256 : part * 256 + 256])
        more = mul_t(jnp.concatenate(joined, axis=1), w1[half])
        total = more if total is None else total + more
    xhat, spread = normalise(tok[...].astype(FULL))
    grad[...] = middle_grad[...] + back_norm(total, xhat, spread, vec[0:1, :])
    add_rows(lines, 0, total * xhat, step)
    add_rows(lines, 1, total, step)

    @pl.when(step == 0)
    def _():
        lines[2:8, :] = jnp.zeros((6, 768), FULL)


def tokens_call(first, count, mixed0, mixed1, w1, tokens, vec, middle_grad, before):
    rows = pl.BlockSpec((256, 768), lambda r: (r + first, 0))
    old = list(before or [])
    return pl.pallas_call(
        lambda *refs: tokens_kernel(*refs[:6], *refs[6 + len(old) :]),
        grid=(count,),
        out_shape=[jax.ShapeDtypeStruct((1024, 768), FULL), jax.ShapeDtypeStruct((8, 768), FULL)],
        in_specs=[pl.BlockSpec((2, 256, w), lambda r: (0, r + first, 0)) for w in (384, 768)] + [
            whole((2, 768, 1152)), rows, whole((16, 768)), rows,
        ] + [ANY] * len(old),
        out_specs=[rows, whole((8, 768))],
        input_output_aliases={6: 0} if old else {},
        compiler_params=params(),
        cost_estimate=cost(count * 512 * 768 * 2304, count * 4e6),
        name="tokens%d" % first,
    )(mixed0, mixed1, w1, tokens, vec, middle_grad, *old)


def lines_kernel(first, second, sums, s0, s1, bias, lines):
    lines[0:2, :] = first[0:2, :] + second[0:2, :]
    for half in range(2):
        at = half * 384
        for row, part in ((2, 0), (3, 2)):
            lines[row : row + 1, at : at + 128] = s0[half, 0:1, part * 128 : part * 128 + 128]
            lines[row : row + 1, at + 128 : at + 384] = s1[half, 0:1, part * 256 : part * 256 + 256]
    lines[4:5, :] = sums[2:3, :]
    lines[5:6, :] = sums[0:1, :]
    lines[6:7, :] = sums[1:2, :]
    lines[7:8, :] = sums[3:4, :]
    for k in range(4):
        lines[8 + k : 9 + k, :] = bias[0:1, k * 768 : k * 768 + 768]
    lines[12:16, :] = jnp.zeros((4, 768), FULL)


def lines_call(*parts):
    return pl.pallas_call(
        lines_kernel,
        out_shape=jax.ShapeDtypeStruct((16, 768), FULL),
        in_specs=[pl.BlockSpec(memory_space=pltpu.VMEM)] * len(parts),
        out_specs=pl.BlockSpec(memory_space=pltpu.VMEM),
        compiler_params=params(),
        cost_estimate=cost(1e4, 2e5),
        name="lines",
    )(*parts)


def after(value, *before):
    return lax.optimization_barrier((value, before))[0]


class Total:
    def __init__(self, mine, theirs):
        self.mine = mine
        self.got = send(theirs, SWAP_C)

    def both(self, index):
        return self.mine[index].astype(FULL) + self.got[index].astype(FULL)

    def first(self, *before):
        self.mine = after(self.mine, *before)
        self.one = (
            self.both((slice(None), 1, slice(0, 2))).astype(LOW),
            self.both((1, slice(None), slice(2, 4))).astype(LOW),
        )
        return self.one

    def second(self, *before):
        self.mine = after(self.mine, *before)
        self.first_x, self.first_y = send(self.one[0], SWAP_X), send(self.one[1], SWAP_Y)
        self.two = (
            (self.both((1, 0, slice(0, 2))) + self.first_x[1]).astype(LOW),
            (self.both((0, 1, slice(2, 4))) + self.first_y[1]).astype(LOW),
        )
        return self.two

    def third(self, *before):
        self.mine = after(self.mine, *before)
        second_y, second_x = send(self.two[0], SWAP_Y), send(self.two[1], SWAP_X)
        near = self.both((0, 0, slice(0, 2))) + self.first_x[0] + second_y
        away = self.both((0, 0, slice(2, 4))) + self.first_y[0] + second_x
        self.own = near[0]
        self.three = (near[1].astype(LOW), away[0].astype(LOW), away[1].astype(LOW))
        return self.own, self.three

    def last(self, *before):
        total = after(self.own, *before)
        for k in (1, 2, 3):
            total = total + send(self.three[k - 1], SWAP_Z[k])
        return total


def halves_of(own, sibling, core):
    return jnp.where(core == 0, own, sibling), jnp.where(core == 0, sibling, own)


def on_device(
    tokens, segment_ids, pad_mask, w_qkv, w_out, w_up, w_down, gain_one, shift_one, bias_query,
    bias_value, bias_out, gain_two, shift_two, bias_up, bias_down, cotangent,
):
    z0, y0, x0, core = place()
    where = jnp.stack([z0, y0, x0, core]).astype(jnp.int32)
    row_count, length, width = tokens.shape
    total_rows = row_count * length
    flat = tokens.reshape(total_rows, width)
    cot = cotangent.reshape(total_rows, width)
    vectors = (gain_one, shift_one, bias_query, bias_value, bias_out, gain_two, shift_two, bias_down, bias_up)

    def along_z(own):
        return [send(own[None], SWAP_Z[k]) for k in (1, 2, 3)]

    def column(own, rest):
        return jnp.concatenate([own[None], *rest], axis=0)

    def plane(col):
        return send(col, SWAP_X), send(col, SWAP_Y)

    def corner(along_x, along_y):
        return send(along_x[0:2], SWAP_Y), send(along_y[2:4], SWAP_X)

    def across(blocks):
        return [send(v, SWAP_C) for v in blocks]

    p1 = first_call(w_qkv, vectors)
    rest1 = along_z(p1)
    mine = (w_out, w_up, w_down)
    p2, p3 = prep(where, after(mine, p1), across(mine))
    half3 = lax.all_gather(p3, CHIPS, axis=0, tiled=True)
    col1 = column(after(p1, p2), rest1)
    x1, y1 = plane(col1)
    rest2 = along_z(after(p2, col1))
    far1 = corner(x1, y1)
    own1 = [col1, x1, y1]
    pack1 = own1 + list(far1) + across(own1) + across(after(far1, *own1))
    qkv, normed_one, w1, vec, up_line = qkv_call(where, flat, pack1)
    col2 = column(after(p2, qkv), rest2)
    x2, y2 = plane(col2)
    held = attend_call(0, 2, after(qkv, col2), segment_ids, pad_mask, None)
    far2 = corner(after(x2, held), after(y2, held))
    own2 = [col2, x2, y2]
    other2 = across(after(own2, held))
    probs, att_t = attend_call(2, 2, after(qkv, x2, y2), segment_ids, pad_mask, held)
    pack2 = own2 + list(far2) + other2 + across(after(far2, att_t))
    middle, normed, act, slope = up_call(where, att_t, flat, up_line, vec, pack2)
    sum_a = Total(*down_grads_call(where, act, cot))
    other3 = send(after(half3, sum_a.mine), SWAP_C)
    output, hid, bias_grad = down_call(where, middle, act, slope, cot, vec, half3, other3)
    ready = sum_a.first(output)
    sum_b = Total(*up_grads_call(where, normed, after(hid, ready)))
    middle_grad, branch_grad, att_grad, sums = branch_call(where, hid, after(middle, sum_b.mine), cot, vec, pack2)
    ready = (sum_a.second(sums), sum_b.first(sums))
    mixed, line_sums = [], []

    def unattend(p, ready, *more):
        grads, mine, theirs, line = unattend_call(
            p, where, qkv, after(att_grad, ready), probs, normed_one, *more)
        mixed.append(grads)
        line_sums.append(line)
        return Total(mine, theirs)

    sum_c = unattend((0,), ready, att_t, branch_grad)
    ready = (sum_b.second(sum_c.mine), sum_a.third(sum_c.mine))
    sum_d = unattend((1, 2), ready)
    sum_a = sum_a.last(sum_d.mine)
    ready = (sum_b.third(sum_d.mine), sum_c.first(sum_d.mine), sum_a)
    held = tokens_call(0, 2, mixed[0], after(mixed[1], ready), w1, flat, vec, middle_grad, None)
    first_lines = held[1]
    ready = (sum_c.second(held), sum_d.first(held))
    sum_b = sum_b.last(held)
    grad_tokens, last_lines = tokens_call(
        2, 2, mixed[0], after(mixed[1], ready, sum_b), w1, flat, vec, middle_grad, held[:1])
    lines = lines_call(first_lines, last_lines, sums, *line_sums, bias_grad)
    ready = (sum_c.third(grad_tokens), sum_d.second(grad_tokens))
    lines = lines + send(lines, SWAP_C)
    sum_c = sum_c.last(ready)
    ready = sum_d.third(ready)
    lines = lines + (send(lines, SWAP_X) + (send(lines, SWAP_Y) + send(lines, SWAP_D)))
    sum_d = sum_d.last(ready)
    lines = lines + (send(lines, SWAP_Z[1]) + (send(lines, SWAP_Z[2]) + send(lines, SWAP_Z[3])))

    def finish(part):
        size = part.shape[0] // 2
        upper, lower = part[:size], part[size:]
        keep, give = halves_of(upper, lower, core)
        back = send(give, SWAP_C)
        return halves_of(keep, back, core)

    c0, c1 = finish(sum_c)
    d0, d1 = finish(sum_d)
    columns = []
    for part in range(3):
        for c, d in ((c0, d0), (c1, d1)):
            columns.append(c[:, 384 + part * 128 : 512 + part * 128])
            columns.append(d[:, part * 256 : part * 256 + 256])
    share_qkv = jnp.concatenate(columns, axis=1)
    share_out = jnp.concatenate([c0[:, 0:384], c1[:, 0:384]], axis=1)
    share_up = jnp.concatenate(finish(sum_b), axis=1)
    share_down = jnp.concatenate(finish(sum_a), axis=1)

    chip = (z0 * 2 + y0) * 2 + x0
    device = chip * 2 + core
    own = lax.dynamic_slice(lines, (0, device * 24), (8, 24))
    own_up = lax.dynamic_slice(lines, (8 + device // 8, device % 8 * 96), (1, 96))[0]
    return (
        output.reshape(row_count, length, width),
        grad_tokens.reshape(row_count, length, width),
        share_qkv, share_out, share_up, share_down,
        own[0], own[1], own[2], own[3], own[4], own[5], own[6], own_up, own[7],
    )


def solution(mesh):
    fits = dict(mesh.shape) == {"gx": 8, "gy": 4}
    device = on_device if fits else generic_device
    names = AXES if fits else ("gx", "gy")
    if fits:
        mesh = Mesh(mesh.devices.reshape(4, 2, 2, 2), AXES)
    return jax.shard_map(
        device,
        mesh=mesh,
        in_specs=(
            P(names, None, None),
            P(names, None),
            P(names, None),
            P(names, None),
            P(names, None),
            P(names, None),
            P(names, None),
            P(names),
            P(names),
            P(names),
            P(names),
            P(names),
            P(names),
            P(names),
            P(names),
            P(names),
            P(names, None, None),
        ),
        out_specs=(
            P(names, None, None),
            P(names, None, None),
            P(names, None),
            P(names, None),
            P(names, None),
            P(names, None),
            P(names),
            P(names),
            P(names),
            P(names),
            P(names),
            P(names),
            P(names),
            P(names),
            P(names),
        ),
        check_vma=False,
    )
```

```python
import functools
import math

import jax
import jax.numpy as jnp
from jax import lax
from jax.experimental import pallas as pl
from jax.experimental.pallas import tpu as pltpu
from jax.sharding import Mesh
from jax.sharding import PartitionSpec as P

HEADS = 12
HDIM = 64


def layer_norm(values, gain, shift):
    centre = values - jnp.mean(values, axis=-1, keepdims=True)
    spread = jnp.mean(centre * centre, axis=-1, keepdims=True)
    return centre * lax.rsqrt(spread + 1e-06) * gain + shift


def smooth_gate(values):
    return jax.nn.gelu(values, approximate=True)


def attend_mask(segment_ids, pad_mask):
    length = segment_ids.shape[-1]
    positions = jnp.arange(length)
    same = segment_ids[:, :, None] == segment_ids[:, None, :]
    real = pad_mask[:, None, :] == 1
    itself = positions[:, None] == positions[None, :]
    return same & (real | itself[None])


def outer_sum(left, right):
    return lax.dot_general(
        left, right, (((0,), (0,)), ((), ())), preferred_element_type=jnp.float32
    )


def against(left, matrix):
    return lax.dot_general(
        left, matrix, (((1,), (1,)), ((), ())), preferred_element_type=jnp.float32
    )


def score_block(query_part, key_part, allowed):
    raw = jnp.einsum("rqhe,rkhe->rhqk", query_part, key_part, preferred_element_type=jnp.float32)
    raw = raw * (1.0 / math.sqrt(HDIM))
    return jnp.where(allowed[:, None], raw, -1e30)


def collect(
    w_qkv,
    w_out,
    w_up,
    w_down,
    gain_one,
    shift_one,
    bias_query,
    bias_value,
    bias_out,
    gain_two,
    shift_two,
    bias_up,
    bias_down,
):
    return (
        lax.all_gather(w_qkv, ("gx", "gy"), axis=0, tiled=True),
        lax.all_gather(w_out, ("gx", "gy"), axis=0, tiled=True),
        lax.all_gather(w_up, ("gx", "gy"), axis=0, tiled=True),
        lax.all_gather(w_down, ("gx", "gy"), axis=0, tiled=True),
        lax.all_gather(gain_one, ("gx", "gy"), axis=0, tiled=True),
        lax.all_gather(shift_one, ("gx", "gy"), axis=0, tiled=True),
        lax.all_gather(bias_query, ("gx", "gy"), axis=0, tiled=True),
        lax.all_gather(bias_value, ("gx", "gy"), axis=0, tiled=True),
        lax.all_gather(bias_out, ("gx", "gy"), axis=0, tiled=True),
        lax.all_gather(gain_two, ("gx", "gy"), axis=0, tiled=True),
        lax.all_gather(shift_two, ("gx", "gy"), axis=0, tiled=True),
        lax.all_gather(bias_up, ("gx", "gy"), axis=0, tiled=True),
        lax.all_gather(bias_down, ("gx", "gy"), axis=0, tiled=True),
    )


def generic_device(
    tokens,
    segment_ids,
    pad_mask,
    w_qkv,
    w_out,
    w_up,
    w_down,
    gain_one,
    shift_one,
    bias_query,
    bias_value,
    bias_out,
    gain_two,
    shift_two,
    bias_up,
    bias_down,
    cotangent,
):
    row_count, length, width = tokens.shape
    total_rows = row_count * length
    gathered = collect(
        w_qkv,
        w_out,
        w_up,
        w_down,
        gain_one,
        shift_one,
        bias_query,
        bias_value,
        bias_out,
        gain_two,
        shift_two,
        bias_up,
        bias_down,
    )
    full_qkv, full_out, full_up, full_down = (gathered[0], gathered[1], gathered[2], gathered[3])
    gain_first = gathered[4].astype(jnp.float32)
    shift_first = gathered[5].astype(jnp.float32)
    query_bias = gathered[6].astype(jnp.float32)
    value_bias = gathered[7].astype(jnp.float32)
    out_bias = gathered[8].astype(jnp.float32)
    gain_second = gathered[9].astype(jnp.float32)
    shift_second = gathered[10].astype(jnp.float32)
    up_bias = gathered[11].astype(jnp.float32)
    down_bias = gathered[12].astype(jnp.float32)
    allowed = attend_mask(segment_ids, pad_mask)
    inputs = tokens.astype(jnp.float32).reshape(total_rows, width)
    first_norm, first_pull = jax.vjp(layer_norm, inputs, gain_first, shift_first)
    normed = first_norm.astype(jnp.bfloat16)
    mixed = jnp.dot(normed, full_qkv, preferred_element_type=jnp.float32)
    query_part = (
        (mixed[:, :width] + query_bias).astype(jnp.bfloat16).reshape(row_count, length, HEADS, HDIM)
    )
    key_part = (
        mixed[:, width : 2 * width].astype(jnp.bfloat16).reshape(row_count, length, HEADS, HDIM)
    )
    value_part = (
        (mixed[:, 2 * width :] + value_bias)
        .astype(jnp.bfloat16)
        .reshape(row_count, length, HEADS, HDIM)
    )
    scores = score_block(query_part, key_part, allowed)
    highest = jnp.max(scores, axis=-1, keepdims=True)
    log_total = highest + jnp.log(jnp.sum(jnp.exp(scores - highest), axis=-1, keepdims=True))
    weights = jnp.exp(scores - log_total).astype(jnp.bfloat16)
    attended = jnp.einsum(
        "rhqk,rkhe->rqhe", weights, value_part, preferred_element_type=jnp.float32
    )
    attended = attended.reshape(total_rows, width).astype(jnp.bfloat16)
    middle = inputs + jnp.dot(attended, full_out, preferred_element_type=jnp.float32) + out_bias
    second_norm, second_pull = jax.vjp(layer_norm, middle, gain_second, shift_second)
    normed_two = second_norm.astype(jnp.bfloat16)
    hidden = jnp.dot(normed_two, full_up, preferred_element_type=jnp.float32) + up_bias
    active, gate_pull = jax.vjp(smooth_gate, hidden)
    active_low = active.astype(jnp.bfloat16)
    result = middle + jnp.dot(active_low, full_down, preferred_element_type=jnp.float32) + down_bias
    output = result.astype(jnp.bfloat16).reshape(row_count, length, width)
    again = collect(
        w_qkv,
        w_out,
        w_up,
        w_down,
        gain_one,
        shift_one,
        bias_query,
        bias_value,
        bias_out,
        gain_two,
        shift_two,
        bias_up,
        bias_down,
    )
    full_qkv, full_out, full_up, full_down = (again[0], again[1], again[2], again[3])
    down_in = cotangent.reshape(total_rows, width)
    outer_grad = down_in.astype(jnp.float32)
    grad_bias_down = jnp.sum(outer_grad, axis=0)
    grad_w_down = outer_sum(active_low, down_in)
    active_grad = against(down_in, full_down)
    hidden_grad = gate_pull(active_grad)[0].astype(jnp.bfloat16)
    grad_bias_up = jnp.sum(hidden_grad.astype(jnp.float32), axis=0)
    grad_w_up = outer_sum(normed_two, hidden_grad)
    norm_two_grad = against(hidden_grad, full_up)
    middle_part, grad_gain_two, grad_shift_two = second_pull(norm_two_grad)
    middle_grad = outer_grad + middle_part
    branch_grad = middle_grad.astype(jnp.bfloat16)
    grad_bias_out = jnp.sum(branch_grad.astype(jnp.float32), axis=0)
    grad_w_out = outer_sum(attended, branch_grad)
    attended_grad = (
        against(branch_grad, full_out).astype(jnp.bfloat16).reshape(row_count, length, HEADS, HDIM)
    )
    probs = jnp.exp(score_block(query_part, key_part, allowed) - log_total)
    probs_low = probs.astype(jnp.bfloat16)
    value_grad = jnp.einsum(
        "rhqk,rqhe->rkhe", probs_low, attended_grad, preferred_element_type=jnp.float32
    ).astype(jnp.bfloat16)
    prob_grad = jnp.einsum(
        "rqhe,rkhe->rhqk", attended_grad, value_part, preferred_element_type=jnp.float32
    )
    inner_term = jnp.sum(prob_grad * probs, axis=-1, keepdims=True)
    score_grad = (probs * (prob_grad - inner_term)).astype(jnp.bfloat16)
    score_scale = 1.0 / math.sqrt(HDIM)
    query_grad = (
        (
            jnp.einsum("rhqk,rkhe->rqhe", score_grad, key_part, preferred_element_type=jnp.float32)
            * score_scale
        )
        .astype(jnp.bfloat16)
        .reshape(total_rows, width)
    )
    key_grad = (
        (
            jnp.einsum(
                "rhqk,rqhe->rkhe", score_grad, query_part, preferred_element_type=jnp.float32
            )
            * score_scale
        )
        .astype(jnp.bfloat16)
        .reshape(total_rows, width)
    )
    value_flat = value_grad.reshape(total_rows, width)
    mixed_grad = jnp.concatenate([query_grad, key_grad, value_flat], axis=1)
    grad_bias_query = jnp.sum(query_grad.astype(jnp.float32), axis=0)
    grad_bias_value = jnp.sum(value_flat.astype(jnp.float32), axis=0)
    grad_w_qkv = outer_sum(normed, mixed_grad)
    norm_one_grad = against(mixed_grad, full_qkv)
    input_part, grad_gain_one, grad_shift_one = first_pull(norm_one_grad)
    grad_tokens = (middle_grad + input_part).reshape(row_count, length, width)
    shares = (
        lax.psum_scatter(grad_w_qkv, ("gx", "gy"), scatter_dimension=0, tiled=True),
        lax.psum_scatter(grad_w_out, ("gx", "gy"), scatter_dimension=0, tiled=True),
        lax.psum_scatter(grad_w_up, ("gx", "gy"), scatter_dimension=0, tiled=True),
        lax.psum_scatter(grad_w_down, ("gx", "gy"), scatter_dimension=0, tiled=True),
        lax.psum_scatter(grad_gain_one, ("gx", "gy"), scatter_dimension=0, tiled=True),
        lax.psum_scatter(grad_shift_one, ("gx", "gy"), scatter_dimension=0, tiled=True),
        lax.psum_scatter(grad_bias_query, ("gx", "gy"), scatter_dimension=0, tiled=True),
        lax.psum_scatter(grad_bias_value, ("gx", "gy"), scatter_dimension=0, tiled=True),
        lax.psum_scatter(grad_bias_out, ("gx", "gy"), scatter_dimension=0, tiled=True),
        lax.psum_scatter(grad_gain_two, ("gx", "gy"), scatter_dimension=0, tiled=True),
        lax.psum_scatter(grad_shift_two, ("gx", "gy"), scatter_dimension=0, tiled=True),
        lax.psum_scatter(grad_bias_up, ("gx", "gy"), scatter_dimension=0, tiled=True),
        lax.psum_scatter(grad_bias_down, ("gx", "gy"), scatter_dimension=0, tiled=True),
    )
    return (
        output,
        grad_tokens,
        shares[0],
        shares[1],
        shares[2],
        shares[3],
        shares[4],
        shares[5],
        shares[6],
        shares[7],
        shares[8],
        shares[9],
        shares[10],
        shares[11],
        shares[12],
    )


CHIPS = ("z", "y", "x")
AXES = CHIPS + ("core",)


def pairs(move):
    out = []
    for d in range(32):
        z, y, x, c = d // 8, (d // 4) % 2, (d // 2) % 2, d % 2
        z, y, x, c = move(z, y, x, c)
        out.append((d, ((z * 2 + y) * 2 + x) * 2 + c))
    return out


SWAP_C = pairs(lambda z, y, x, c: (z, y, x, 1 - c))
SWAP_X = pairs(lambda z, y, x, c: (z, y, 1 - x, c))
SWAP_Y = pairs(lambda z, y, x, c: (z, 1 - y, x, c))
SWAP_D = pairs(lambda z, y, x, c: (z, 1 - y, 1 - x, c))
SWAP_Z = [None] + [pairs(lambda z, y, x, c, k=k: (z ^ k, y, x, c)) for k in (1, 2, 3)]


def send(values, perm):
    return lax.ppermute(values, AXES, perm)


def place():
    return tuple(lax.axis_index(name) for name in AXES)


LOW = jnp.bfloat16
FULL = jnp.float32
ANY = pl.BlockSpec(memory_space=pl.ANY)
SMEM = pl.BlockSpec(memory_space=pltpu.SMEM)
MIB = 1024 * 1024


def whole(shape):
    zeros = (0,) * len(shape)
    return pl.BlockSpec(shape, lambda *_: zeros, pipeline_mode=pl.Buffered(1))


def params(limit=64):
    return pltpu.CompilerParams(vmem_limit_bytes=limit * MIB)


def cost(flops, read, exps=0, scale=10.0):
    return pl.CostEstimate(
        flops=int(scale * flops), bytes_accessed=int(scale * read), transcendentals=int(scale * exps)
    )


def mul(left, right):
    return lax.dot_general(left, right, (((1,), (0,)), ((), ())), preferred_element_type=FULL)


def mul_t(left, right):
    return lax.dot_general(left, right, (((1,), (1,)), ((), ())), preferred_element_type=FULL)


def t_mul(left, right):
    return lax.dot_general(left, right, (((0,), (0,)), ((), ())), preferred_element_type=FULL)


def first_kernel(qkv, v0, v1, v2, v3, v4, v5, v6, v7, up, out, tall):
    out[:, 0:2304] = qkv[...]
    tall[...] = jnp.zeros_like(tall)
    for row, vector in enumerate((v0, v1, v2, v3, v4, v5, v6, v7)):
        tall[row : row + 1, 0:24] = vector[...].astype(FULL).reshape(1, 24)
    turned = jnp.transpose(tall[...])[0:24]
    lane = lax.broadcasted_iota(jnp.int32, (24, 128), 1)
    row = lax.broadcasted_iota(jnp.int32, (24, 128), 0)
    tall[0:1, 16:112] = up[...].astype(FULL).reshape(1, 96)
    line = jnp.broadcast_to(tall[0:1, :], (24, 128))
    keep = (row == 0) & (lane >= 16) & (lane < 112)
    out[:, 2304:2432] = jnp.where(lane < 8, turned, jnp.where(keep, line, 0.0)).astype(LOW)


def first_call(qkv, vectors):
    return pl.pallas_call(
        first_kernel,
        out_shape=jax.ShapeDtypeStruct((24, 2432), LOW),
        in_specs=[pl.BlockSpec(memory_space=pltpu.VMEM)] * 10,
        out_specs=pl.BlockSpec(memory_space=pltpu.VMEM),
        scratch_shapes=[pltpu.VMEM((128, 128), FULL)],
        compiler_params=params(),
        cost_estimate=cost(1e5, 3e5),
        name="first",
    )(qkv, *vectors)


def prep_kernel(where, out_m, up_m, down_m, out_s, up_s, down_s, p2, p3):
    def build(core):
        pairs_of = lambda m, s: (m, s) if core == 0 else (s, m)

        def rows(m, s, at, width):
            both = [v[:, at : at + width].astype(FULL) for v in pairs_of(m, s)]
            return jnp.concatenate(both, axis=0).astype(LOW)

        p2[:, 0:1536] = rows(up_m, up_s, core * 1536, 1536)
        p2[:, 1536:1920] = rows(out_m, out_s, core * 384, 384)
        for k, down in enumerate(pairs_of(down_m, down_s)):
            p3[k * 96 : k * 96 + 96, :] = down[:, core * 384 : core * 384 + 384]

    for core in range(2):
        pl.when(where[3] == core)(functools.partial(build, core))


def prep(where, mine, theirs):
    return pl.pallas_call(
        prep_kernel,
        out_shape=[jax.ShapeDtypeStruct((48, 1920), LOW), jax.ShapeDtypeStruct((192, 384), LOW)],
        in_specs=[SMEM] + [pl.BlockSpec(memory_space=pltpu.VMEM)] * 6,
        out_specs=[pl.BlockSpec(memory_space=pltpu.VMEM)] * 2,
        compiler_params=params(),
        cost_estimate=cost(1e6, 2e6),
        name="prep",
    )(where, *mine, *theirs)


def chip_of(where, dz, dy, dx):
    return ((where[0] ^ dz) * 2 + (where[1] ^ dy)) * 2 + (where[2] ^ dx)


def load_pack(where, pieces, start):
    for side in range(2):
        owner = where[3] ^ side
        col, along_x, along_y, far0, far1 = pieces[side * 5 : side * 5 + 5]
        for dz in range(4):
            far = far0.at[dz] if dz < 2 else far1.at[dz - 2]
            for dy, dx, source in ((0, 0, col.at[dz]), (0, 1, along_x.at[dz]), (1, 0, along_y.at[dz]), (1, 1, far)):
                start(source, chip_of(where, dz, dy, dx), owner)


def wait_pack(target, sem):
    pltpu.make_async_copy(target, target, sem).wait()


def normalise(values):
    centre = values - jnp.mean(values, axis=1, keepdims=True)
    spread = lax.rsqrt(jnp.mean(centre * centre, axis=1, keepdims=True) + 1e-6)
    return centre * spread, spread


def qkv_kernel(where, tok, *refs):
    pieces, (qkv, normed, w1, vec, bias_up, buf, weights, sem) = refs[:10], refs[10:]
    half = pl.program_id(0)

    @pl.when(half == 0)
    def _():
        load_pack(
            where, pieces, lambda v, chip, core: pltpu.make_async_copy(v, buf.at[chip * 2 + core], sem).start()
        )
        wait_pack(buf, sem)
        lines = jnp.concatenate([buf[d, :, 2304:2432].astype(FULL) for d in range(32)], axis=0)
        lines = jnp.transpose(lines)
        vec[...] = lines[0:16]
        for chip in range(16):
            for s in range(2):
                line = buf[chip * 2 + s, 0:8, 2304:2432].astype(FULL)[0:1]
                at = (chip * 2 + s) * 96
                bias_up[0:1, at : at + 96] = line[:, 16:112]
        for t in range(4):
            at = slice(t * 256, t * 256 + 256)
            xhat, _ = normalise(tok[at, :].astype(FULL))
            normed[at, :] = (xhat * lines[0:1] + lines[1:2]).astype(LOW)

    def gather(h):
        for chip in range(16):
            rows = slice(chip * 48, chip * 48 + 48)
            for part in range(3):
                at = slice(part * 768 + h * 384, part * 768 + h * 384 + 384)
                both = [buf[chip * 2 + s, :, at].astype(FULL) for s in range(2)]
                weights[rows, part * 384 : part * 384 + 384] = jnp.concatenate(both, axis=0).astype(LOW)

    for h in range(2):
        pl.when(half == h)(functools.partial(gather, h))
    w1[0] = weights[...]
    at = pl.multiple_of(half * 384, 128)
    query_bias = vec[2:3, pl.ds(at, 384)]
    value_bias = vec[3:4, pl.ds(at, 384)]
    for t in range(4):
        at = slice(t * 256, t * 256 + 256)
        mixed = mul(normed[at, :], weights[...])
        qkv[0, at, 0:384] = (mixed[:, 0:384] + query_bias).astype(LOW) * 0.125
        qkv[0, at, 384:768] = mixed[:, 384:768].astype(LOW)
        qkv[0, at, 768:1152] = (mixed[:, 768:1152] + value_bias).astype(LOW)


def qkv_call(where, tokens, pieces):
    return pl.pallas_call(
        qkv_kernel,
        grid=(2,),
        out_shape=[
            jax.ShapeDtypeStruct((2, 1024, 1152), LOW),
            jax.ShapeDtypeStruct((1024, 768), LOW),
            jax.ShapeDtypeStruct((2, 768, 1152), LOW),
            jax.ShapeDtypeStruct((16, 768), FULL),
            jax.ShapeDtypeStruct((1, 3072), FULL),
        ],
        in_specs=[SMEM, whole((1024, 768))] + [ANY] * 10,
        out_specs=[
            pl.BlockSpec((1, 1024, 1152), lambda h: (h, 0, 0)),
            whole((1024, 768)),
            pl.BlockSpec((1, 768, 1152), lambda h: (h, 0, 0)),
            whole((16, 768)),
            whole((1, 3072)),
        ],
        scratch_shapes=[
            pltpu.VMEM((32, 24, 2432), LOW),
            pltpu.VMEM((768, 1152), LOW),
            pltpu.SemaphoreType.DMA,
        ],
        compiler_params=params(),
        cost_estimate=cost(2 * 1024 * 768 * 2304, 16e6, scale=0.1),
        name="qkv",
    )(where, tokens, *pieces)


def masked_pair(block):
    lane = lax.broadcasted_iota(jnp.int32, block.shape, 1)
    zero = jnp.zeros_like(block)
    return jnp.concatenate([jnp.where(lane < 64, block, zero), jnp.where(lane < 64, zero, block)], axis=0)


def unmask(both):
    return jnp.concatenate([both[0:64, 0:128], both[64:128, 128:256]], axis=0)


def attend_kernel(first, qkv, seg, pad, *refs):
    probs, att_t, bias, wide = refs[-4:]
    row = pl.program_id(0) + first
    seg_row, pad_row = seg[pl.ds(row, 1), :].astype(FULL), pad[pl.ds(row, 1), :].astype(FULL)
    seg_col = jnp.transpose(jnp.broadcast_to(seg_row, (128, 256)))
    pad_col = jnp.transpose(jnp.broadcast_to(pad_row, (128, 256)))
    for b in range(2):
        keys = slice(64 * b, 64 * b + 192)
        same = seg_col[keys] == jnp.broadcast_to(seg_row[:, 128 * b : 128 * b + 128], (192, 128))
        key_at = lax.broadcasted_iota(jnp.int32, (192, 128), 0) + 64 * b
        query_at = lax.broadcasted_iota(jnp.int32, (192, 128), 1) + 128 * b
        allowed = same & ((pad_col[keys] == 1.0) | (key_at == query_at))
        one = jnp.where(allowed, 0.0, -1e30)
        bias[b] = jnp.concatenate([one, one], axis=1)
    blocks = [(half, p, b) for half in range(2) for p in range(3) for b in range(2)]
    for i, (half, p, b) in enumerate(blocks):
        stack = masked_pair(qkv[half, 128 * b : 128 * b + 128, p * 128 : p * 128 + 128])
        keys = slice(64 * b, 64 * b + 192)
        wide[i] = mul_t(qkv[half, keys, 384 + p * 128 : 512 + p * 128], stack) + bias[b]
    for i, (half, p, b) in enumerate(blocks):
        scores = wide[i]
        power = jnp.exp(scores - jnp.max(scores, axis=0, keepdims=True))
        probs[0, p, half, b] = (power * (1.0 / jnp.sum(power, axis=0, keepdims=True))).astype(LOW)
    for half, p, b in blocks:
        keys = slice(64 * b, 64 * b + 192)
        both = t_mul(qkv[half, keys, 768 + p * 128 : 896 + p * 128], probs[0, p, half, b])
        at = half * 384 + p * 128
        att_t[at : at + 128, 128 * b : 128 * b + 128] = unmask(both).astype(LOW)


def attend_call(first, count, qkv, seg, pad, before):
    old = list(before or [])
    return pl.pallas_call(
        functools.partial(attend_kernel, first),
        grid=(count,),
        out_shape=[
            jax.ShapeDtypeStruct((4, 3, 2, 2, 192, 256), LOW),
            jax.ShapeDtypeStruct((768, 1024), LOW),
        ],
        in_specs=[pl.BlockSpec((2, 256, 1152), lambda r: (0, r + first, 0)), whole((4, 256)), whole((4, 256))]
        + [ANY] * len(old),
        out_specs=[
            pl.BlockSpec((1, 3, 2, 2, 192, 256), lambda r: (r + first, 0, 0, 0, 0, 0)),
            pl.BlockSpec((768, 256), lambda r: (0, r + first)),
        ],
        input_output_aliases={3: 0, 4: 1} if old else {},
        scratch_shapes=[pltpu.VMEM((2, 192, 256), FULL), pltpu.VMEM((12, 192, 256), FULL)],
        compiler_params=params(),
        cost_estimate=cost(count * 1.5e9, count * 3e6, 8e5, scale=0.1),
        name="attend%d" % first,
    )(qkv, seg, pad, *old)


GATE = math.sqrt(2.0 / math.pi)


def gate_pair(u):
    square = u * u
    factor = 0.5 + 0.5 * jnp.tanh(u * (GATE + GATE * 0.044715 * square))
    value = u * factor
    return value, factor + value * (1.0 - factor) * (2.0 * GATE + 6.0 * GATE * 0.044715 * square)


FEED_SCALE = 0.1
CHUNK = 512
TILE = 256
TILES = 1024 // TILE


def load_up(where, pieces, up, w_out, sem, sem_out):
    def start(block, chip, core):
        rows = pl.ds(pl.multiple_of(chip * 48, 16), 48)
        for source, target, width, sem_of in (
            (slice(1536, 1920), w_out, 384, sem_out), (slice(0, 1536), up, 1536, sem)):
            columns = pl.ds(pl.multiple_of(core * width, 128), width)
            pltpu.make_async_copy(block.at[:, source], target.at[rows, columns], sem_of).start()

    load_pack(where, pieces, start)


def back_norm(grad, xhat, spread, gain):
    scaled = grad * gain
    flat = jnp.mean(scaled, axis=1, keepdims=True)
    tilt = jnp.mean(scaled * xhat, axis=1, keepdims=True)
    return (scaled - flat - xhat * tilt) * spread


def add_rows(target, row, values, step):
    value = jnp.sum(values, axis=0, keepdims=True)
    target[row : row + 1, :] = jnp.where(step == 0, value, target[row : row + 1, :] + value)


def feed_tile(step, att_t, tok, cot, bias, vec, weights, kept, outs, before):
    up, down, w_out = weights
    normed, act, hid = kept
    output, middle_grad, branch_grad, att_grad, sums, bias_grad = outs
    here = pl.ds(pl.multiple_of(step * TILE, TILE), TILE)
    before(0)
    mid = tok[...].astype(FULL) + t_mul(att_t[...], w_out[...]) + vec[4:5, :]
    xhat, spread = normalise(mid)
    rows = (xhat * vec[5:6, :] + vec[6:7, :]).astype(LOW)
    normed[here, :] = rows
    outer = cot[here, :]
    before(1)
    chunks = [slice(k * CHUNK, k * CHUNK + CHUNK) for k in range(3072 // CHUNK)]
    hidden = mul(rows, up[:, chunks[0]])
    for k, at in enumerate(chunks):
        following = mul(rows, up[:, chunks[k + 1]]) if k + 1 < len(chunks) else None
        if k == 0:
            before(2)
        active_grad = mul_t(outer, down[at, :])
        value, tilt = gate_pair(hidden + bias[:, at])
        act[here, at] = value.astype(LOW)
        grad = (tilt * active_grad).astype(LOW)
        hid[here, at] = grad
        line = jnp.sum(grad.astype(FULL), axis=0, keepdims=True)
        bias_grad[:, at] = jnp.where(step == 0, line, bias_grad[:, at] + line)
        hidden = following

    output[...] = (mid + vec[7:8, :] + mul(act[here, :], down[...])).astype(LOW)
    grad = mul_t(hid[here, :], up[...])
    outer = outer.astype(FULL)
    mid_grad = outer + back_norm(grad, xhat, spread, vec[5:6, :])
    middle_grad[...] = mid_grad
    low = mid_grad.astype(LOW)
    branch_grad[...] = low
    add_rows(sums, 0, grad * xhat, step)
    add_rows(sums, 1, grad, step)
    add_rows(sums, 2, low.astype(FULL), step)
    add_rows(sums, 3, outer, step)
    att_grad[...] = mul_t(low, w_out[...]).astype(LOW)


def feed_kernel(where, att_t, tok, cot, bias, vec, *refs):
    pieces, pieces_down = refs[:10], refs[10:20]
    outs = refs[20:26]
    down_packs, up_packs = refs[26:28], refs[28:30]
    up, down, w_out, normed, act, hid, sems = refs[30:]
    step = pl.program_id(0)
    core = where[3]

    def before(stage):
        @pl.when(step == 0)
        def _():
            if stage == 0:
                load_up(where, pieces, up, w_out, sems.at[1], sems.at[0])

                def start(block, chip, owner):
                    rows = pl.ds(pl.multiple_of(chip * 192, 16), 192)
                    columns = pl.ds(pl.multiple_of(owner * 384, 128), 384)
                    pltpu.make_async_copy(block, down.at[rows, columns], sems.at[2]).start()

                load_pack(where, pieces_down, start)
            target = (w_out, up, down)[stage]
            wait_pack(target, sems.at[stage])

    @pl.when(step < TILES)
    def _():
        feed_tile(step, att_t, tok, cot, bias, vec, (up, down, w_out), (normed, act, hid), outs, before)

    @pl.when(step >= TILES)
    def _():
        pair = step - TILES
        at = pl.multiple_of(pair * 1536, 1536)
        grad_down = t_mul(act[:, pl.ds(at, 1536)], cot[...]).astype(LOW)
        at = pl.multiple_of(pair * 384, 384)
        grad_up = t_mul(normed[:, pl.ds(at, 384)], hid[...])

        def put(side):
            for o in range(2):
                for k in range(8):
                    spot = ((k // 2 % 2) ^ where[1], (k % 2) ^ where[2], (k // 4) ^ (where[0] % 2))
                    at = k * 192 + o * 96
                    for h in range(2):
                        down_packs[o ^ side][spot + (slice(h * 96, h * 96 + 96),)] = grad_down[
                            at : at + 96, h * 384 : h * 384 + 384
                        ]
                    rows = grad_up[k * 48 + o * 24 : k * 48 + o * 24 + 24]
                    for j in range(4):
                        both = [rows[:, i * 384 : i * 384 + 384] for i in (2 * j, 2 * j + 1)]
                        up_packs[o ^ side][spot + (slice(j * 48, j * 48 + 48),)] = jnp.concatenate(
                            both, axis=0
                        ).astype(LOW)

        for side in range(2):
            pl.when(core == side)(functools.partial(put, side))


def feed_call(where, att_t, tokens, cot, bias_up, vec, pieces, pieces_down):
    tile = lambda step: jnp.minimum(step, TILES - 1)
    rows = pl.BlockSpec((TILE, 768), lambda s, where: (tile(s), 0))
    fixed = lambda shape: pl.BlockSpec(shape, lambda s, where: (0,) * len(shape), pipeline_mode=pl.Buffered(1))
    pack = (2, 2, 4, 192, 384)
    pack_block = pl.BlockSpec(
        (2, 2, 2, 192, 384), lambda s, where: (0, 0, jnp.clip(s - TILES, 0, 1) ^ (where[0] // 2), 0, 0))
    return pl.pallas_call(
        feed_kernel,
        grid_spec=pltpu.PrefetchScalarGridSpec(
            num_scalar_prefetch=1,
            grid=(TILES + 2,),
            in_specs=[
                pl.BlockSpec((768, TILE), lambda s, where: (0, tile(s))), rows, fixed((1024, 768)),
                fixed((1, 3072)), fixed((16, 768)),
            ] + [ANY] * 20,
            out_specs=[
                rows, rows, rows, rows, fixed((8, 768)), fixed((1, 3072)), *([pack_block] * 4),
            ],
            scratch_shapes=[
                pltpu.VMEM((768, 3072), LOW),
                pltpu.VMEM((3072, 768), LOW),
                pltpu.VMEM((768, 768), LOW),
                pltpu.VMEM((1024, 768), LOW),
                pltpu.VMEM((1024, 3072), LOW),
                pltpu.VMEM((1024, 3072), LOW),
                pltpu.SemaphoreType.DMA((3,)),
            ],
        ),
        out_shape=[
            jax.ShapeDtypeStruct((1024, 768), LOW),
            jax.ShapeDtypeStruct((1024, 768), FULL),
            jax.ShapeDtypeStruct((1024, 768), LOW),
            jax.ShapeDtypeStruct((1024, 768), LOW),
            jax.ShapeDtypeStruct((8, 768), FULL),
            jax.ShapeDtypeStruct((1, 3072), FULL),
        ] + [jax.ShapeDtypeStruct(pack, LOW)] * 4,
        compiler_params=params(),
        cost_estimate=cost(26 * 1024 * 768 * 768 * 2, 35e6, 3e6, scale=FEED_SCALE),
        name="feed",
    )(where, att_t, tokens, cot, bias_up, vec, *pieces, *pieces_down)


ROWS_STEP = 2


def unattend_kernel(groups, with_out, where, *refs):
    count = len(groups)
    parts = [refs[5 * g : 5 * g + 5] for g in range(count)]
    refs = refs[5 * count :]
    probs, normed = refs[:count], refs[count]
    refs = refs[count + 1 :]
    if with_out:
        att_t, branch_grad, refs = refs[0], refs[1], refs[2:]
        mixed, mine, theirs, sums, acc, wide, slim, stacks, out_acc = refs
    else:
        mixed, mine, theirs, sums, acc, wide, slim, stacks = refs
    step = pl.program_id(0)
    width = 128 * count
    blocks = [(r, g, h) for r in range(ROWS_STEP) for g in range(count) for h in range(2)]

    def keys_of(r, b):
        return slice(256 * r + 64 * b, 256 * r + 64 * b + 192)

    def queries_of(r, b):
        return slice(256 * r + 128 * b, 256 * r + 128 * b + 128)

    for i, (r, g, half) in enumerate(blocks):
        query, key, value = parts[g][:3]
        grads = parts[g][3 + half]
        for b in range(2):
            stacks[0, 2 * i + b] = masked_pair(query[half, queries_of(r, b), :])
            stack = masked_pair(grads[queries_of(r, b), :])
            stacks[1, 2 * i + b] = stack
            wide[2 * i + b] = mul_t(value[half, keys_of(r, b), :], stack)
    for i, (r, g, half) in enumerate(blocks):
        for b in range(2):
            weights = probs[g][r, 0, half, b].astype(FULL)
            prob_grad = wide[2 * i + b]
            inner = jnp.sum(prob_grad * weights, axis=0, keepdims=True)
            slim[2 * i + b] = (weights * (prob_grad - inner)).astype(LOW)

    def merge(first, second):
        return jnp.concatenate([first[0:64], first[64:192] + second[0:128], second[128:192]], axis=0)

    for i, (r, g, half) in enumerate(blocks):
        key = parts[g][1]
        rows = slice(256 * r, 256 * r + 256)
        value_grad = [mul(probs[g][r, 0, half, b], stacks[1, 2 * i + b]) for b in range(2)]
        key_grad = [mul(slim[2 * i + b], stacks[0, 2 * i + b]) for b in range(2)]
        turned = [unmask(t_mul(key[half, keys_of(r, b), :], slim[2 * i + b])) for b in range(2)]
        query_grad = jnp.transpose(jnp.concatenate(turned, axis=1)) * 0.125
        at = g * 128
        mixed[half, rows, at : at + 128] = query_grad.astype(LOW)
        mixed[half, rows, width + at : width + at + 128] = merge(*key_grad).astype(LOW)
        mixed[half, rows, 2 * width + at : 2 * width + at + 128] = merge(*value_grad).astype(LOW)

    def add(target, more):
        @pl.when(step == 0)
        def _():
            target[...] = more

        @pl.when(step > 0)
        def _():
            target[...] += more

    for half in range(2):
        add_rows(sums.at[half], 0, mixed[half].astype(FULL), step)
        add(acc.at[half], t_mul(normed[...], mixed[half]))
    if with_out:
        add(out_acc, mul(att_t[...], branch_grad[...]))

    def write(side):
        for owner in range(2):
            dest = mine if owner == side else theirs
            for chip in range(16):
                rows = slice(chip * 48 + owner * 24, chip * 48 + owner * 24 + 24)
                spot = ((chip // 2 % 2) ^ where[1], (chip % 2) ^ where[2], (chip // 4) ^ where[0], slice(None))
                if with_out:
                    lines = [out_acc[rows, :], jnp.concatenate([acc[0, rows, :], acc[1, rows, :]], axis=1)]
                else:
                    lines = [acc[0, rows, :], acc[1, rows, :]]
                dest[spot + (slice(0, 768),)] = jnp.concatenate(lines, axis=0).astype(LOW)

    for side in range(2):
        pl.when((step == 4 // ROWS_STEP - 1) & (where[3] == side))(functools.partial(write, side))


def unattend_call(groups, where, qkv, att_grad, probs, normed, att_t=None, branch_grad=None):
    with_out = att_t is not None
    count = len(groups)
    width = 384 * count
    tall = 256 * ROWS_STEP
    operands, specs = [], []
    for p in groups:
        for part in range(3):
            operands.append(qkv)
            specs.append(pl.BlockSpec((2, tall, 128), lambda r, c=part * 3 + p: (0, r, c)))
        for half in range(2):
            operands.append(att_grad)
            specs.append(pl.BlockSpec((tall, 128), lambda r, c=half * 3 + p: (r, c)))
    for p in groups:
        operands.append(probs)
        specs.append(pl.BlockSpec((ROWS_STEP, 1, 2, 2, 192, 256), lambda r, p=p: (r, p, 0, 0, 0, 0)))
    operands.append(normed)
    specs.append(pl.BlockSpec((tall, 768), lambda r: (r, 0)))
    if with_out:
        operands += [att_t, branch_grad]
        specs += [pl.BlockSpec((768, tall), lambda r: (0, r)), pl.BlockSpec((tall, 768), lambda r: (r, 0))]
    shape = (2, 2, 4, 48, 768 if with_out else 896)
    part_of = pl.BlockSpec((2, 2, 4, 48, 768), lambda r: (0, 0, 0, 0, 0), pipeline_mode=pl.Buffered(1))
    many = 4 * count * ROWS_STEP
    return pl.pallas_call(
        functools.partial(unattend_kernel, groups, with_out),
        grid=(4 // ROWS_STEP,),
        out_shape=[
            jax.ShapeDtypeStruct((2, 1024, width), LOW),
            jax.ShapeDtypeStruct(shape, LOW),
            jax.ShapeDtypeStruct(shape, LOW),
            jax.ShapeDtypeStruct((2, 8, width), FULL),
        ],
        in_specs=[SMEM] + specs,
        out_specs=[
            pl.BlockSpec((2, tall, width), lambda r: (0, r, 0)),
            part_of,
            part_of,
            whole((2, 8, width)),
        ],
        scratch_shapes=[
            pltpu.VMEM((2, 768, width), FULL),
            pltpu.VMEM((many, 192, 256), FULL),
            pltpu.VMEM((many, 192, 256), LOW),
            pltpu.VMEM((2, many, 256, 128), LOW),
        ] + ([pltpu.VMEM((768, 768), FULL)] if with_out else []),
        compiler_params=params(),
        cost_estimate=cost(count * 2.5e9, count * 8e6),
        name="unattend%d" % groups[0],
    )(where, *operands)


def tokens_kernel(
    where, m0, m1, w1, tok, vec, middle_grad, sums, sums0, sums1, bias, mine_in, theirs_in, grad, mine, theirs, lines, turned
):
    step = pl.program_id(0)
    total = None
    for half in range(2):
        joined = []
        for part in range(3):
            joined.append(m0[half, :, part * 128 : part * 128 + 128])
            joined.append(m1[half, :, part * 256 : part * 256 + 256])
        more = mul_t(jnp.concatenate(joined, axis=1), w1[half])
        total = more if total is None else total + more
    xhat, spread = normalise(tok[...].astype(FULL))
    grad[...] = middle_grad[...] + back_norm(total, xhat, spread, vec[0:1, :])
    add_rows(lines, 0, total * xhat, step)
    add_rows(lines, 1, total, step)

    @pl.when(step == 3)
    def _():
        for half in range(2):
            at = half * 384
            for row, part in ((2, 0), (3, 2)):
                lines[row : row + 1, at : at + 128] = sums0[half, 0:1, part * 128 : part * 128 + 128]
                lines[row : row + 1, at + 128 : at + 384] = sums1[half, 0:1, part * 256 : part * 256 + 256]
        lines[4:5, :] = sums[2:3, :]
        lines[5:6, :] = sums[0:1, :]
        lines[6:7, :] = sums[1:2, :]
        lines[7:8, :] = sums[3:4, :]
        lines[8:128, :] = jnp.zeros((120, 768), FULL)
        turned[...] = jnp.transpose(lines[...])
        for device in range(32):
            turned[device * 24 : device * 24 + 1, 16:112] = bias[0:1, device * 96 : device * 96 + 96]

        def write(side):
            for owner in range(2):
                dest = mine if owner == side else theirs
                for chip in range(16):
                    at = (chip * 2 + owner) * 24
                    spot = ((chip // 2 % 2) ^ where[1], (chip % 2) ^ where[2], (chip // 4) ^ where[0])
                    both = [turned[at : at + 24, :], jnp.zeros((24, 128), FULL)]
                    dest[spot] = jnp.concatenate(both, axis=0).astype(LOW)

        for side in range(2):
            pl.when(where[3] == side)(functools.partial(write, side))


def tokens_call(where, mixed0, mixed1, w1, tokens, vec, middle_grad, sums, sums0, sums1, bias, mine, theirs):
    rows = pl.BlockSpec((256, 768), lambda r: (r, 0))
    part_of = pl.BlockSpec((2, 2, 4, 48, 128), lambda r: (0, 0, 0, 0, 6), pipeline_mode=pl.Buffered(1))
    return pl.pallas_call(
        tokens_kernel,
        grid=(4,),
        out_shape=[jax.ShapeDtypeStruct((1024, 768), FULL)] + [jax.ShapeDtypeStruct(mine.shape, LOW)] * 2,
        in_specs=[SMEM] + [pl.BlockSpec((2, 256, w), lambda r: (0, r, 0)) for w in (384, 768)] + [
            whole((2, 768, 1152)), rows, whole((16, 768)), rows, whole((8, 768)), whole((2, 8, 384)),
            whole((2, 8, 768)), whole((1, 3072)), ANY, ANY,
        ],
        out_specs=[rows, part_of, part_of],
        input_output_aliases={11: 1, 12: 2},
        scratch_shapes=[pltpu.VMEM((128, 768), FULL), pltpu.VMEM((768, 128), FULL)],
        compiler_params=params(),
        cost_estimate=cost(2 * 1024 * 768 * 2304, 16e6),
        name="tokens",
    )(where, mixed0, mixed1, w1, tokens, vec, middle_grad, sums, sums0, sums1, bias, mine, theirs)


def after(value, *before):
    return lax.optimization_barrier((value, before))[0]


class Total:
    def __init__(self, mine, theirs):
        self.mine = mine
        self.block = mine.shape[3:]
        self.got = send(theirs, SWAP_C)

    def spec(self, size, place_of):
        return pl.BlockSpec(size + self.block, lambda i: place_of(i) + (0, 0))

    def low(self, *lead):
        return jax.ShapeDtypeStruct(lead + self.block, LOW)

    def first(self):
        def body(mine_x, got_x, mine_y, got_y, out_x, out_y):
            out_x[...] = (mine_x[...].astype(FULL) + got_x[...].astype(FULL)).reshape(out_x.shape).astype(LOW)
            out_y[...] = (mine_y[...].astype(FULL) + got_y[...].astype(FULL)).reshape(out_y.shape).astype(LOW)

        to_x = self.spec((1, 1, 2), lambda i: (i, 1, 0))
        to_y = self.spec((1, 1, 2), lambda i: (1, i, 1))
        out = self.spec((1, 2), lambda i: (i, 0))

        def keep(one_x, one_y):
            self.one_x, self.one_y = send(one_x, SWAP_X), send(one_y, SWAP_Y)

        return (body, [self.mine, self.got] * 2, [to_x, to_x, to_y, to_y], [self.low(2, 2)] * 2, [out] * 2, keep)

    def second(self):
        def body(mine_y, got_y, one_x, mine_x, got_x, one_y, out_y, out_x):
            add = lambda *refs: sum(r[...].astype(FULL).reshape(out_y.shape) for r in refs)
            out_y[...] = add(mine_y, got_y, one_x).astype(LOW)
            out_x[...] = add(mine_x, got_x, one_y).astype(LOW)

        to_y = self.spec((1, 1, 1), lambda i: (1, 0, i))
        to_x = self.spec((1, 1, 1), lambda i: (0, 1, 2 + i))
        came = self.spec((1, 1), lambda i: (1, i))
        out = self.spec((1,), lambda i: (i,))

        def keep(two_y, two_x):
            self.two_y, self.two_x = send(two_y, SWAP_Y), send(two_x, SWAP_X)

        operands = [self.mine, self.got, self.one_x, self.mine, self.got, self.one_y]
        return (body, operands, [to_y, to_y, came, to_x, to_x, came], [self.low(2)] * 2, [out] * 2, keep)

    def third(self):
        def body(mine, got, one_x, two_y, one_y, two_x, *outs):
            @pl.when(pl.program_id(0) == 0)
            def _():
                for k, target in enumerate(outs):
                    extra = (one_x[0, k], two_y[k]) if k < 2 else (one_y[0, k - 2], two_x[k - 2])
                    total = mine[0, 0, k].astype(FULL) + got[0, 0, k].astype(FULL)
                    total = total + extra[0].astype(FULL) + extra[1].astype(FULL)
                    target[...] = total.astype(target.dtype)

        near = self.spec((1, 1, 4), lambda i: (0, 0, 0))
        came = self.spec((1, 2), lambda i: (0, 0))
        two = self.spec((2,), lambda i: (0,))
        one = pl.BlockSpec(self.block, lambda i: (0, 0))
        out = [jax.ShapeDtypeStruct(self.block, FULL)] + [self.low()] * 3

        def keep(own, *three):
            self.own = own
            self.parts = [send(v, SWAP_Z[k + 1]) for k, v in enumerate(three)]

        operands = [self.mine, self.got, self.one_x, self.two_y, self.one_y, self.two_x]
        return (body, operands, [near, near, came, two, came, two], out, [one] * 4, keep)

    def last(self, write, shapes, more=()):
        def body(own, part1, part2, part3, *refs):
            @pl.when(pl.program_id(0) == 0)
            def _():
                total = own[...] + part1[...].astype(FULL) + part2[...].astype(FULL) + part3[...].astype(FULL)
                write(total, *refs)

        block = pl.BlockSpec(self.block, lambda i: (0, 0))
        same = lambda shape: pl.BlockSpec(shape, lambda i: (0,) * len(shape))

        def keep(*given):
            self.final = given

        return (
            body, [self.own, *self.parts, *more], [block] * 4 + [same(v.shape) for v in more],
            [jax.ShapeDtypeStruct(v, FULL) for v in shapes], [same(v) for v in shapes], keep,
        )


def write_down(total, share):
    share[...] = jnp.concatenate([total[0:96], total[96:192]], axis=1)


def write_up(total, share):
    share[...] = jnp.concatenate([total[j * 24 : j * 24 + 24] for j in range(8)], axis=1)


def write_out(total, share, rest):
    share[...] = total[0:24]
    rest[...] = total[24:48]


def write_qkv(total, first, share, *vectors):
    for half in range(2):
        for part in range(3):
            at = part * 768 + half * 384
            share[:, at : at + 128] = first[:, half * 384 + part * 128 : half * 384 + part * 128 + 128]
            share[:, at + 128 : at + 384] = total[half * 24 : half * 24 + 24, part * 256 : part * 256 + 256]
    columns = jnp.concatenate([total[0:24, 768:896], jnp.zeros((104, 128), FULL)], axis=0)
    lines = jnp.transpose(columns)
    for row in range(8):
        vectors[row][...] = lines[row : row + 1, 0:24].reshape(24)
    vectors[8][...] = total[0:1, 784:880].reshape(96)


def run_stages(stages, *before):
    ins = [len(s[1]) for s in stages]
    outs = [len(s[3]) for s in stages]

    def kernel(*refs):
        at_in, at_out = 0, sum(ins)
        for stage, n_in, n_out in zip(stages, ins, outs):
            stage[0](*refs[at_in : at_in + n_in], *refs[at_out : at_out + n_out])
            at_in, at_out = at_in + n_in, at_out + n_out

    operands = after([v for s in stages for v in s[1]], *before)
    results = pl.pallas_call(
        kernel,
        grid=(2,),
        out_shape=[v for s in stages for v in s[3]],
        in_specs=[v for s in stages for v in s[2]],
        out_specs=[v for s in stages for v in s[4]],
        compiler_params=params(),
        cost_estimate=cost(1e6, 4e6),
        name="sums",
    )(*operands)
    at = 0
    for stage, n_out in zip(stages, outs):
        stage[5](*results[at : at + n_out])
        at += n_out
    return results


def halves_of(own, sibling, core):
    return jnp.where(core == 0, own, sibling), jnp.where(core == 0, sibling, own)


def on_device(
    tokens, segment_ids, pad_mask, w_qkv, w_out, w_up, w_down, gain_one, shift_one, bias_query,
    bias_value, bias_out, gain_two, shift_two, bias_up, bias_down, cotangent,
):
    z0, y0, x0, core = place()
    where = jnp.stack([z0, y0, x0, core]).astype(jnp.int32)
    row_count, length, width = tokens.shape
    total_rows = row_count * length
    flat = tokens.reshape(total_rows, width)
    cot = cotangent.reshape(total_rows, width)
    vectors = (gain_one, shift_one, bias_query, bias_value, bias_out, gain_two, shift_two, bias_down, bias_up)

    def along_z(own):
        return [send(own[None], SWAP_Z[k]) for k in (1, 2, 3)]

    def column(own, rest):
        return jnp.concatenate([own[None], *rest], axis=0)

    def plane(col):
        return send(col, SWAP_X), send(col, SWAP_Y)

    def corner(along_x, along_y):
        return send(along_x[0:2], SWAP_Y), send(along_y[2:4], SWAP_X)

    def across(blocks):
        return [send(v, SWAP_C) for v in blocks]

    p1 = first_call(w_qkv, vectors)
    rest1 = along_z(p1)
    mine = (w_out, w_up, w_down)
    p2, p3 = prep(where, after(mine, p1), across(mine))
    col1 = column(after(p1, p2), rest1)
    x1, y1 = plane(col1)
    rest2 = along_z(after(p2, col1))
    col2 = column(p2, rest2)
    far1 = corner(after(x1, col2), after(y1, col2))
    own1 = [col1, x1, y1]
    pack1 = own1 + list(far1) + across(own1) + across(after(far1, *own1))
    x2, y2 = plane(col2)
    rest3 = along_z(after(p3, col2))
    qkv, normed_one, w1, vec, up_line = qkv_call(where, after(flat, col2), pack1)
    col3 = column(after(p3, qkv), rest3)
    far2 = corner(after(x2, qkv), after(y2, qkv))
    own2 = [col2, x2, y2]
    other2 = across(after(own2, qkv))
    x3, y3 = plane(col3)
    probs, att_t = attend_call(0, 4, after(qkv, col3), segment_ids, pad_mask, None)
    far2 = after(far2, att_t)
    far3 = corner(after(x3, att_t), after(y3, att_t))
    own3 = [col3, x3, y3]
    pack2 = own2 + list(far2) + other2 + across(far2)
    pack3 = own3 + list(far3) + across(after(own3, att_t)) + across(far3)
    output, middle_grad, branch_grad, att_grad, sums, bias_grad, *grads = feed_call(
        where, att_t, flat, cot, up_line, vec, pack2, pack3)

    sum_a, sum_b = Total(*grads[:2]), Total(*grads[2:])
    ready = run_stages([sum_a.first()])
    mixed0, mine, theirs, sums0 = unattend_call(
        (0,), where, qkv, after(att_grad, ready), probs, normed_one, att_t, branch_grad)
    sum_c = Total(mine, theirs)
    ready = run_stages([sum_a.second(), sum_b.first()], mixed0)
    mixed1, mine, theirs, sums1 = unattend_call((1, 2), where, qkv, after(att_grad, ready), probs, normed_one)
    ready = run_stages([sum_a.third(), sum_b.second(), sum_c.first()], mixed1)
    grad_tokens, mine, theirs = tokens_call(
        where, mixed0, after(mixed1, ready), w1, flat, vec, middle_grad, sums, sums0, sums1, bias_grad, mine, theirs)
    ready = run_stages([sum_b.third(), sum_c.second(), sum_a.last(write_down, [(96, 768)])], grad_tokens)
    sum_d = Total(mine, after(theirs, ready))
    ready = run_stages([sum_d.first(), sum_c.third()], ready)
    ready = run_stages([sum_d.second(), sum_b.last(write_up, [(24, 3072)])], ready)
    ready = run_stages([sum_d.third(), sum_c.last(write_out, [(24, 768)] * 2)], ready)
    run_stages(
        [sum_d.last(write_qkv, [(24, 2304)] + [(24,)] * 8 + [(96,)], sum_c.final[1:])], ready)
    share_qkv, *own = sum_d.final
    share_out, share_up, share_down = sum_c.final[0], sum_b.final[0], sum_a.final[0]
    return (
        output.reshape(row_count, length, width),
        grad_tokens.reshape(row_count, length, width),
        share_qkv, share_out, share_up, share_down,
        own[0], own[1], own[2], own[3], own[4], own[5], own[6], own[8], own[7],
    )


def solution(mesh):
    fits = dict(mesh.shape) == {"gx": 8, "gy": 4}
    device = on_device if fits else generic_device
    names = AXES if fits else ("gx", "gy")
    if fits:
        mesh = Mesh(mesh.devices.reshape(4, 2, 2, 2), AXES)
    return jax.shard_map(
        device,
        mesh=mesh,
        in_specs=(
            P(names, None, None),
            P(names, None),
            P(names, None),
            P(names, None),
            P(names, None),
            P(names, None),
            P(names, None),
            P(names),
            P(names),
            P(names),
            P(names),
            P(names),
            P(names),
            P(names),
            P(names),
            P(names),
            P(names, None, None),
        ),
        out_specs=(
            P(names, None, None),
            P(names, None, None),
            P(names, None),
            P(names, None),
            P(names, None),
            P(names, None),
            P(names),
            P(names),
            P(names),
            P(names),
            P(names),
            P(names),
            P(names),
            P(names),
            P(names),
        ),
        check_vma=False,
    )
```

```python
import functools
import math

import jax
import jax.numpy as jnp
from jax import lax
from jax.experimental import pallas as pl
from jax.experimental.pallas import tpu as pltpu
from jax.sharding import Mesh
from jax.sharding import PartitionSpec as P

HEADS = 12
HDIM = 64


def layer_norm(values, gain, shift):
    centre = values - jnp.mean(values, axis=-1, keepdims=True)
    spread = jnp.mean(centre * centre, axis=-1, keepdims=True)
    return centre * lax.rsqrt(spread + 1e-06) * gain + shift


def smooth_gate(values):
    return jax.nn.gelu(values, approximate=True)


def attend_mask(segment_ids, pad_mask):
    length = segment_ids.shape[-1]
    positions = jnp.arange(length)
    same = segment_ids[:, :, None] == segment_ids[:, None, :]
    real = pad_mask[:, None, :] == 1
    itself = positions[:, None] == positions[None, :]
    return same & (real | itself[None])


def outer_sum(left, right):
    return lax.dot_general(
        left, right, (((0,), (0,)), ((), ())), preferred_element_type=jnp.float32
    )


def against(left, matrix):
    return lax.dot_general(
        left, matrix, (((1,), (1,)), ((), ())), preferred_element_type=jnp.float32
    )


def score_block(query_part, key_part, allowed):
    raw = jnp.einsum("rqhe,rkhe->rhqk", query_part, key_part, preferred_element_type=jnp.float32)
    raw = raw * (1.0 / math.sqrt(HDIM))
    return jnp.where(allowed[:, None], raw, -1e30)


def collect(
    w_qkv,
    w_out,
    w_up,
    w_down,
    gain_one,
    shift_one,
    bias_query,
    bias_value,
    bias_out,
    gain_two,
    shift_two,
    bias_up,
    bias_down,
):
    return (
        lax.all_gather(w_qkv, ("gx", "gy"), axis=0, tiled=True),
        lax.all_gather(w_out, ("gx", "gy"), axis=0, tiled=True),
        lax.all_gather(w_up, ("gx", "gy"), axis=0, tiled=True),
        lax.all_gather(w_down, ("gx", "gy"), axis=0, tiled=True),
        lax.all_gather(gain_one, ("gx", "gy"), axis=0, tiled=True),
        lax.all_gather(shift_one, ("gx", "gy"), axis=0, tiled=True),
        lax.all_gather(bias_query, ("gx", "gy"), axis=0, tiled=True),
        lax.all_gather(bias_value, ("gx", "gy"), axis=0, tiled=True),
        lax.all_gather(bias_out, ("gx", "gy"), axis=0, tiled=True),
        lax.all_gather(gain_two, ("gx", "gy"), axis=0, tiled=True),
        lax.all_gather(shift_two, ("gx", "gy"), axis=0, tiled=True),
        lax.all_gather(bias_up, ("gx", "gy"), axis=0, tiled=True),
        lax.all_gather(bias_down, ("gx", "gy"), axis=0, tiled=True),
    )


def generic_device(
    tokens,
    segment_ids,
    pad_mask,
    w_qkv,
    w_out,
    w_up,
    w_down,
    gain_one,
    shift_one,
    bias_query,
    bias_value,
    bias_out,
    gain_two,
    shift_two,
    bias_up,
    bias_down,
    cotangent,
):
    row_count, length, width = tokens.shape
    total_rows = row_count * length
    gathered = collect(
        w_qkv,
        w_out,
        w_up,
        w_down,
        gain_one,
        shift_one,
        bias_query,
        bias_value,
        bias_out,
        gain_two,
        shift_two,
        bias_up,
        bias_down,
    )
    full_qkv, full_out, full_up, full_down = (gathered[0], gathered[1], gathered[2], gathered[3])
    gain_first = gathered[4].astype(jnp.float32)
    shift_first = gathered[5].astype(jnp.float32)
    query_bias = gathered[6].astype(jnp.float32)
    value_bias = gathered[7].astype(jnp.float32)
    out_bias = gathered[8].astype(jnp.float32)
    gain_second = gathered[9].astype(jnp.float32)
    shift_second = gathered[10].astype(jnp.float32)
    up_bias = gathered[11].astype(jnp.float32)
    down_bias = gathered[12].astype(jnp.float32)
    allowed = attend_mask(segment_ids, pad_mask)
    inputs = tokens.astype(jnp.float32).reshape(total_rows, width)
    first_norm, first_pull = jax.vjp(layer_norm, inputs, gain_first, shift_first)
    normed = first_norm.astype(jnp.bfloat16)
    mixed = jnp.dot(normed, full_qkv, preferred_element_type=jnp.float32)
    query_part = (
        (mixed[:, :width] + query_bias).astype(jnp.bfloat16).reshape(row_count, length, HEADS, HDIM)
    )
    key_part = (
        mixed[:, width : 2 * width].astype(jnp.bfloat16).reshape(row_count, length, HEADS, HDIM)
    )
    value_part = (
        (mixed[:, 2 * width :] + value_bias)
        .astype(jnp.bfloat16)
        .reshape(row_count, length, HEADS, HDIM)
    )
    scores = score_block(query_part, key_part, allowed)
    highest = jnp.max(scores, axis=-1, keepdims=True)
    log_total = highest + jnp.log(jnp.sum(jnp.exp(scores - highest), axis=-1, keepdims=True))
    weights = jnp.exp(scores - log_total).astype(jnp.bfloat16)
    attended = jnp.einsum(
        "rhqk,rkhe->rqhe", weights, value_part, preferred_element_type=jnp.float32
    )
    attended = attended.reshape(total_rows, width).astype(jnp.bfloat16)
    middle = inputs + jnp.dot(attended, full_out, preferred_element_type=jnp.float32) + out_bias
    second_norm, second_pull = jax.vjp(layer_norm, middle, gain_second, shift_second)
    normed_two = second_norm.astype(jnp.bfloat16)
    hidden = jnp.dot(normed_two, full_up, preferred_element_type=jnp.float32) + up_bias
    active, gate_pull = jax.vjp(smooth_gate, hidden)
    active_low = active.astype(jnp.bfloat16)
    result = middle + jnp.dot(active_low, full_down, preferred_element_type=jnp.float32) + down_bias
    output = result.astype(jnp.bfloat16).reshape(row_count, length, width)
    again = collect(
        w_qkv,
        w_out,
        w_up,
        w_down,
        gain_one,
        shift_one,
        bias_query,
        bias_value,
        bias_out,
        gain_two,
        shift_two,
        bias_up,
        bias_down,
    )
    full_qkv, full_out, full_up, full_down = (again[0], again[1], again[2], again[3])
    down_in = cotangent.reshape(total_rows, width)
    outer_grad = down_in.astype(jnp.float32)
    grad_bias_down = jnp.sum(outer_grad, axis=0)
    grad_w_down = outer_sum(active_low, down_in)
    active_grad = against(down_in, full_down)
    hidden_grad = gate_pull(active_grad)[0].astype(jnp.bfloat16)
    grad_bias_up = jnp.sum(hidden_grad.astype(jnp.float32), axis=0)
    grad_w_up = outer_sum(normed_two, hidden_grad)
    norm_two_grad = against(hidden_grad, full_up)
    middle_part, grad_gain_two, grad_shift_two = second_pull(norm_two_grad)
    middle_grad = outer_grad + middle_part
    branch_grad = middle_grad.astype(jnp.bfloat16)
    grad_bias_out = jnp.sum(branch_grad.astype(jnp.float32), axis=0)
    grad_w_out = outer_sum(attended, branch_grad)
    attended_grad = (
        against(branch_grad, full_out).astype(jnp.bfloat16).reshape(row_count, length, HEADS, HDIM)
    )
    probs = jnp.exp(score_block(query_part, key_part, allowed) - log_total)
    probs_low = probs.astype(jnp.bfloat16)
    value_grad = jnp.einsum(
        "rhqk,rqhe->rkhe", probs_low, attended_grad, preferred_element_type=jnp.float32
    ).astype(jnp.bfloat16)
    prob_grad = jnp.einsum(
        "rqhe,rkhe->rhqk", attended_grad, value_part, preferred_element_type=jnp.float32
    )
    inner_term = jnp.sum(prob_grad * probs, axis=-1, keepdims=True)
    score_grad = (probs * (prob_grad - inner_term)).astype(jnp.bfloat16)
    score_scale = 1.0 / math.sqrt(HDIM)
    query_grad = (
        (
            jnp.einsum("rhqk,rkhe->rqhe", score_grad, key_part, preferred_element_type=jnp.float32)
            * score_scale
        )
        .astype(jnp.bfloat16)
        .reshape(total_rows, width)
    )
    key_grad = (
        (
            jnp.einsum(
                "rhqk,rqhe->rkhe", score_grad, query_part, preferred_element_type=jnp.float32
            )
            * score_scale
        )
        .astype(jnp.bfloat16)
        .reshape(total_rows, width)
    )
    value_flat = value_grad.reshape(total_rows, width)
    mixed_grad = jnp.concatenate([query_grad, key_grad, value_flat], axis=1)
    grad_bias_query = jnp.sum(query_grad.astype(jnp.float32), axis=0)
    grad_bias_value = jnp.sum(value_flat.astype(jnp.float32), axis=0)
    grad_w_qkv = outer_sum(normed, mixed_grad)
    norm_one_grad = against(mixed_grad, full_qkv)
    input_part, grad_gain_one, grad_shift_one = first_pull(norm_one_grad)
    grad_tokens = (middle_grad + input_part).reshape(row_count, length, width)
    shares = (
        lax.psum_scatter(grad_w_qkv, ("gx", "gy"), scatter_dimension=0, tiled=True),
        lax.psum_scatter(grad_w_out, ("gx", "gy"), scatter_dimension=0, tiled=True),
        lax.psum_scatter(grad_w_up, ("gx", "gy"), scatter_dimension=0, tiled=True),
        lax.psum_scatter(grad_w_down, ("gx", "gy"), scatter_dimension=0, tiled=True),
        lax.psum_scatter(grad_gain_one, ("gx", "gy"), scatter_dimension=0, tiled=True),
        lax.psum_scatter(grad_shift_one, ("gx", "gy"), scatter_dimension=0, tiled=True),
        lax.psum_scatter(grad_bias_query, ("gx", "gy"), scatter_dimension=0, tiled=True),
        lax.psum_scatter(grad_bias_value, ("gx", "gy"), scatter_dimension=0, tiled=True),
        lax.psum_scatter(grad_bias_out, ("gx", "gy"), scatter_dimension=0, tiled=True),
        lax.psum_scatter(grad_gain_two, ("gx", "gy"), scatter_dimension=0, tiled=True),
        lax.psum_scatter(grad_shift_two, ("gx", "gy"), scatter_dimension=0, tiled=True),
        lax.psum_scatter(grad_bias_up, ("gx", "gy"), scatter_dimension=0, tiled=True),
        lax.psum_scatter(grad_bias_down, ("gx", "gy"), scatter_dimension=0, tiled=True),
    )
    return (
        output,
        grad_tokens,
        shares[0],
        shares[1],
        shares[2],
        shares[3],
        shares[4],
        shares[5],
        shares[6],
        shares[7],
        shares[8],
        shares[9],
        shares[10],
        shares[11],
        shares[12],
    )


CHIPS = ("z", "y", "x")
AXES = CHIPS + ("core",)


def pairs(move):
    out = []
    for d in range(32):
        z, y, x, c = d // 8, (d // 4) % 2, (d // 2) % 2, d % 2
        z, y, x, c = move(z, y, x, c)
        out.append((d, ((z * 2 + y) * 2 + x) * 2 + c))
    return out


SWAP_C = pairs(lambda z, y, x, c: (z, y, x, 1 - c))
SWAP_X = pairs(lambda z, y, x, c: (z, y, 1 - x, c))
SWAP_Y = pairs(lambda z, y, x, c: (z, 1 - y, x, c))
SWAP_D = pairs(lambda z, y, x, c: (z, 1 - y, 1 - x, c))
SWAP_Z = [None] + [pairs(lambda z, y, x, c, k=k: (z ^ k, y, x, c)) for k in (1, 2, 3)]


def send(values, perm):
    return lax.ppermute(values, AXES, perm)


def place():
    return tuple(lax.axis_index(name) for name in AXES)


LOW = jnp.bfloat16
FULL = jnp.float32
ANY = pl.BlockSpec(memory_space=pl.ANY)
SMEM = pl.BlockSpec(memory_space=pltpu.SMEM)
MIB = 1024 * 1024


def whole(shape):
    zeros = (0,) * len(shape)
    return pl.BlockSpec(shape, lambda *_: zeros, pipeline_mode=pl.Buffered(1))


def params(limit=64):
    return pltpu.CompilerParams(vmem_limit_bytes=limit * MIB)


def cost(flops, read, exps=0, scale=10.0):
    return pl.CostEstimate(
        flops=int(scale * flops), bytes_accessed=int(scale * read), transcendentals=int(scale * exps)
    )


def mul(left, right):
    return lax.dot_general(left, right, (((1,), (0,)), ((), ())), preferred_element_type=FULL)


def mul_t(left, right):
    return lax.dot_general(left, right, (((1,), (1,)), ((), ())), preferred_element_type=FULL)


def t_mul(left, right):
    return lax.dot_general(left, right, (((0,), (0,)), ((), ())), preferred_element_type=FULL)


def first_kernel(qkv, v0, v1, v2, v3, v4, v5, v6, v7, up, out, tall):
    out[:, 0:2304] = qkv[...]
    tall[...] = jnp.zeros_like(tall)
    for row, vector in enumerate((v0, v1, v2, v3, v4, v5, v6, v7)):
        tall[row : row + 1, 0:24] = vector[...].astype(FULL).reshape(1, 24)
    turned = jnp.transpose(tall[...])[0:24]
    lane = lax.broadcasted_iota(jnp.int32, (24, 128), 1)
    row = lax.broadcasted_iota(jnp.int32, (24, 128), 0)
    tall[0:1, 16:112] = up[...].astype(FULL).reshape(1, 96)
    line = jnp.broadcast_to(tall[0:1, :], (24, 128))
    keep = (row == 0) & (lane >= 16) & (lane < 112)
    out[:, 2304:2432] = jnp.where(lane < 8, turned, jnp.where(keep, line, 0.0)).astype(LOW)


def first_call(qkv, vectors):
    return pl.pallas_call(
        first_kernel,
        out_shape=jax.ShapeDtypeStruct((24, 2432), LOW),
        in_specs=[pl.BlockSpec(memory_space=pltpu.VMEM)] * 10,
        out_specs=pl.BlockSpec(memory_space=pltpu.VMEM),
        scratch_shapes=[pltpu.VMEM((128, 128), FULL)],
        compiler_params=params(),
        cost_estimate=cost(1e5, 3e5),
        name="first",
    )(qkv, *vectors)


def prep_kernel(where, out_m, up_m, down_m, out_s, up_s, down_s, p2, p3):
    def build(core):
        pairs_of = lambda m, s: (m, s) if core == 0 else (s, m)

        def rows(m, s, at, width):
            both = [v[:, at : at + width].astype(FULL) for v in pairs_of(m, s)]
            return jnp.concatenate(both, axis=0).astype(LOW)

        p2[:, 0:1536] = rows(up_m, up_s, core * 1536, 1536)
        p2[:, 1536:1920] = rows(out_m, out_s, core * 384, 384)
        for k, down in enumerate(pairs_of(down_m, down_s)):
            p3[k * 96 : k * 96 + 96, :] = down[:, core * 384 : core * 384 + 384]

    for core in range(2):
        pl.when(where[3] == core)(functools.partial(build, core))


def prep(where, mine, theirs):
    return pl.pallas_call(
        prep_kernel,
        out_shape=[jax.ShapeDtypeStruct((48, 1920), LOW), jax.ShapeDtypeStruct((192, 384), LOW)],
        in_specs=[SMEM] + [pl.BlockSpec(memory_space=pltpu.VMEM)] * 6,
        out_specs=[pl.BlockSpec(memory_space=pltpu.VMEM)] * 2,
        compiler_params=params(),
        cost_estimate=cost(1e6, 2e6),
        name="prep",
    )(where, *mine, *theirs)


def chip_of(where, dz, dy, dx):
    return ((where[0] ^ dz) * 2 + (where[1] ^ dy)) * 2 + (where[2] ^ dx)


def load_pack(where, pieces, start):
    for side in range(2):
        owner = where[3] ^ side
        col, along_x, along_y, far0, far1 = pieces[side * 5 : side * 5 + 5]
        for dz in range(4):
            far = far0.at[dz] if dz < 2 else far1.at[dz - 2]
            for dy, dx, source in ((0, 0, col.at[dz]), (0, 1, along_x.at[dz]), (1, 0, along_y.at[dz]), (1, 1, far)):
                start(source, chip_of(where, dz, dy, dx), owner)


def wait_pack(target, sem):
    pltpu.make_async_copy(target, target, sem).wait()


def normalise(values):
    centre = values - jnp.mean(values, axis=1, keepdims=True)
    spread = lax.rsqrt(jnp.mean(centre * centre, axis=1, keepdims=True) + 1e-6)
    return centre * spread, spread


def qkv_kernel(where, tok, *refs):
    pieces, (qkv, normed, w1, vec, bias_up, buf, weights, hats, sem) = refs[:10], refs[10:]
    half = pl.program_id(0)

    @pl.when(half == 0)
    def _():
        load_pack(
            where, pieces, lambda v, chip, core: pltpu.make_async_copy(v, buf.at[chip * 2 + core], sem).start()
        )
        for t in range(4):
            at = slice(t * 256, t * 256 + 256)
            hats[at, :], _ = normalise(tok[at, :].astype(FULL))
        wait_pack(buf, sem)
        lines = jnp.concatenate([buf[d, :, 2304:2432].astype(FULL) for d in range(32)], axis=0)
        lines = jnp.transpose(lines)
        vec[...] = lines[0:16]
        for chip in range(16):
            for s in range(2):
                line = buf[chip * 2 + s, 0:8, 2304:2432].astype(FULL)[0:1]
                at = (chip * 2 + s) * 96
                bias_up[0:1, at : at + 96] = line[:, 16:112]
        for t in range(4):
            at = slice(t * 256, t * 256 + 256)
            normed[at, :] = (hats[at, :] * lines[0:1] + lines[1:2]).astype(LOW)

    def gather(h):
        for chip in range(16):
            rows = slice(chip * 48, chip * 48 + 48)
            for part in range(3):
                at = slice(part * 768 + h * 384, part * 768 + h * 384 + 384)
                both = [buf[chip * 2 + s, :, at].astype(FULL) for s in range(2)]
                weights[rows, part * 384 : part * 384 + 384] = jnp.concatenate(both, axis=0).astype(LOW)

    for h in range(2):
        pl.when(half == h)(functools.partial(gather, h))
    w1[0] = weights[...]
    at = pl.multiple_of(half * 384, 128)
    query_bias = vec[2:3, pl.ds(at, 384)]
    value_bias = vec[3:4, pl.ds(at, 384)]
    for t in range(4):
        at = slice(t * 256, t * 256 + 256)
        mixed = mul(normed[at, :], weights[...])
        qkv[0, at, 0:384] = (mixed[:, 0:384] + query_bias).astype(LOW) * 0.125
        qkv[0, at, 384:768] = mixed[:, 384:768].astype(LOW)
        qkv[0, at, 768:1152] = (mixed[:, 768:1152] + value_bias).astype(LOW)


def qkv_call(where, tokens, pieces):
    return pl.pallas_call(
        qkv_kernel,
        grid=(2,),
        out_shape=[
            jax.ShapeDtypeStruct((2, 1024, 1152), LOW),
            jax.ShapeDtypeStruct((1024, 768), LOW),
            jax.ShapeDtypeStruct((2, 768, 1152), LOW),
            jax.ShapeDtypeStruct((16, 768), FULL),
            jax.ShapeDtypeStruct((1, 3072), FULL),
        ],
        in_specs=[SMEM, whole((1024, 768))] + [ANY] * 10,
        out_specs=[
            pl.BlockSpec((1, 1024, 1152), lambda h: (h, 0, 0)),
            whole((1024, 768)),
            pl.BlockSpec((1, 768, 1152), lambda h: (h, 0, 0)),
            whole((16, 768)),
            whole((1, 3072)),
        ],
        scratch_shapes=[
            pltpu.VMEM((32, 24, 2432), LOW),
            pltpu.VMEM((768, 1152), LOW),
            pltpu.VMEM((1024, 768), FULL),
            pltpu.SemaphoreType.DMA,
        ],
        compiler_params=params(),
        cost_estimate=cost(2 * 1024 * 768 * 2304, 16e6, scale=0.1),
        name="qkv",
    )(where, tokens, *pieces)


def masked_pair(block):
    lane = lax.broadcasted_iota(jnp.int32, block.shape, 1)
    zero = jnp.zeros_like(block)
    return jnp.concatenate([jnp.where(lane < 64, block, zero), jnp.where(lane < 64, zero, block)], axis=0)


def unmask(both):
    return jnp.concatenate([both[0:64, 0:128], both[64:128, 128:256]], axis=0)


def attend_kernel(first, qkv, seg, pad, *refs):
    probs, att_t, bias, wide = refs[-4:]
    row = pl.program_id(0) + first
    seg_row, pad_row = seg[pl.ds(row, 1), :].astype(FULL), pad[pl.ds(row, 1), :].astype(FULL)
    seg_col = jnp.transpose(jnp.broadcast_to(seg_row, (128, 256)))
    pad_col = jnp.transpose(jnp.broadcast_to(pad_row, (128, 256)))
    for b in range(2):
        keys = slice(64 * b, 64 * b + 192)
        same = seg_col[keys] == jnp.broadcast_to(seg_row[:, 128 * b : 128 * b + 128], (192, 128))
        key_at = lax.broadcasted_iota(jnp.int32, (192, 128), 0) + 64 * b
        query_at = lax.broadcasted_iota(jnp.int32, (192, 128), 1) + 128 * b
        allowed = same & ((pad_col[keys] == 1.0) | (key_at == query_at))
        one = jnp.where(allowed, 0.0, -1e30)
        bias[b] = jnp.concatenate([one, one], axis=1)
    blocks = [(half, p, b) for half in range(2) for p in range(3) for b in range(2)]
    for i, (half, p, b) in enumerate(blocks):
        stack = masked_pair(qkv[half, 128 * b : 128 * b + 128, p * 128 : p * 128 + 128])
        keys = slice(64 * b, 64 * b + 192)
        wide[i] = mul_t(qkv[half, keys, 384 + p * 128 : 512 + p * 128], stack) + bias[b]
    for i, (half, p, b) in enumerate(blocks):
        scores = wide[i]
        power = jnp.exp(scores - jnp.max(scores, axis=0, keepdims=True))
        probs[0, p, half, b] = (power * (1.0 / jnp.sum(power, axis=0, keepdims=True))).astype(LOW)
    for half, p, b in blocks:
        keys = slice(64 * b, 64 * b + 192)
        both = t_mul(qkv[half, keys, 768 + p * 128 : 896 + p * 128], probs[0, p, half, b])
        at = half * 384 + p * 128
        att_t[at : at + 128, 128 * b : 128 * b + 128] = unmask(both).astype(LOW)


def attend_call(first, count, qkv, seg, pad, before):
    old = list(before or [])
    return pl.pallas_call(
        functools.partial(attend_kernel, first),
        grid=(count,),
        out_shape=[
            jax.ShapeDtypeStruct((4, 3, 2, 2, 192, 256), LOW),
            jax.ShapeDtypeStruct((768, 1024), LOW),
        ],
        in_specs=[pl.BlockSpec((2, 256, 1152), lambda r: (0, r + first, 0)), whole((4, 256)), whole((4, 256))]
        + [ANY] * len(old),
        out_specs=[
            pl.BlockSpec((1, 3, 2, 2, 192, 256), lambda r: (r + first, 0, 0, 0, 0, 0)),
            pl.BlockSpec((768, 256), lambda r: (0, r + first)),
        ],
        input_output_aliases={3: 0, 4: 1} if old else {},
        scratch_shapes=[pltpu.VMEM((2, 192, 256), FULL), pltpu.VMEM((12, 192, 256), FULL)],
        compiler_params=params(),
        cost_estimate=cost(count * 1.5e9, count * 3e6, 8e5, scale=0.1),
        name="attend%d" % first,
    )(qkv, seg, pad, *old)


GATE = math.sqrt(2.0 / math.pi)


def gate_pair(u):
    square = u * u
    factor = 0.5 + 0.5 * jnp.tanh(u * (GATE + GATE * 0.044715 * square))
    value = u * factor
    return value, factor + value * (1.0 - factor) * (2.0 * GATE + 6.0 * GATE * 0.044715 * square)


FEED_SCALE = 0.1
CHUNK = 512
TILE = 256
TILES = 1024 // TILE


def load_up(where, pieces, up, w_out, sem, sem_out):
    def start(block, chip, core):
        rows = pl.ds(pl.multiple_of(chip * 48, 16), 48)
        for source, target, width, sem_of in (
            (slice(1536, 1920), w_out, 384, sem_out), (slice(0, 1536), up, 1536, sem)):
            columns = pl.ds(pl.multiple_of(core * width, 128), width)
            pltpu.make_async_copy(block.at[:, source], target.at[rows, columns], sem_of).start()

    load_pack(where, pieces, start)


def back_norm(grad, xhat, spread, gain):
    scaled = grad * gain
    flat = jnp.mean(scaled, axis=1, keepdims=True)
    tilt = jnp.mean(scaled * xhat, axis=1, keepdims=True)
    return (scaled - flat - xhat * tilt) * spread


def add_rows(target, row, values, step):
    value = jnp.sum(values, axis=0, keepdims=True)
    target[row : row + 1, :] = jnp.where(step == 0, value, target[row : row + 1, :] + value)


def feed_tile(step, att_t, tok, cot, bias, vec, weights, kept, outs, before):
    up, down, w_out = weights
    normed, act, hid = kept
    output, middle_grad, branch_grad, att_grad, sums, bias_grad = outs
    here = pl.ds(pl.multiple_of(step * TILE, TILE), TILE)
    before(0)
    mid = tok[...].astype(FULL) + t_mul(att_t[...], w_out[...]) + vec[4:5, :]
    xhat, spread = normalise(mid)
    rows = (xhat * vec[5:6, :] + vec[6:7, :]).astype(LOW)
    normed[here, :] = rows
    outer = cot[here, :]
    before(1)
    chunks = [slice(k * CHUNK, k * CHUNK + CHUNK) for k in range(3072 // CHUNK)]
    hidden = mul(rows, up[:, chunks[0]])
    for k, at in enumerate(chunks):
        following = mul(rows, up[:, chunks[k + 1]]) if k + 1 < len(chunks) else None
        if k == 0:
            before(2)
        active_grad = mul_t(outer, down[at, :])
        value, tilt = gate_pair(hidden + bias[:, at])
        act[here, at] = value.astype(LOW)
        grad = (tilt * active_grad).astype(LOW)
        hid[here, at] = grad
        line = jnp.sum(grad.astype(FULL), axis=0, keepdims=True)
        bias_grad[:, at] = jnp.where(step == 0, line, bias_grad[:, at] + line)
        hidden = following

    output[...] = (mid + vec[7:8, :] + mul(act[here, :], down[...])).astype(LOW)
    grad = mul_t(hid[here, :], up[...])
    outer = outer.astype(FULL)
    mid_grad = outer + back_norm(grad, xhat, spread, vec[5:6, :])
    middle_grad[...] = mid_grad
    low = mid_grad.astype(LOW)
    branch_grad[...] = low
    add_rows(sums, 0, grad * xhat, step)
    add_rows(sums, 1, grad, step)
    add_rows(sums, 2, low.astype(FULL), step)
    add_rows(sums, 3, outer, step)
    att_grad[...] = mul_t(low, w_out[...]).astype(LOW)


def feed_kernel(where, att_t, tok, cot, bias, vec, *refs):
    pieces, pieces_down = refs[:10], refs[10:20]
    outs = refs[20:26]
    down_packs, up_packs = refs[26:28], refs[28:30]
    up, down, w_out, normed, act, hid, sems = refs[30:]
    step = pl.program_id(0)
    core = where[3]

    def before(stage):
        @pl.when(step == 0)
        def _():
            if stage == 0:
                load_up(where, pieces, up, w_out, sems.at[1], sems.at[0])

                def start(block, chip, owner):
                    rows = pl.ds(pl.multiple_of(chip * 192, 16), 192)
                    columns = pl.ds(pl.multiple_of(owner * 384, 128), 384)
                    pltpu.make_async_copy(block, down.at[rows, columns], sems.at[2]).start()

                load_pack(where, pieces_down, start)
            target = (w_out, up, down)[stage]
            wait_pack(target, sems.at[stage])

    @pl.when(step < TILES)
    def _():
        feed_tile(step, att_t, tok, cot, bias, vec, (up, down, w_out), (normed, act, hid), outs, before)

    @pl.when(step >= TILES)
    def _():
        pair = step - TILES
        at = pl.multiple_of(pair * 1536, 1536)
        grad_down = t_mul(act[:, pl.ds(at, 1536)], cot[...]).astype(LOW)
        at = pl.multiple_of(pair * 384, 384)
        grad_up = t_mul(normed[:, pl.ds(at, 384)], hid[...])

        def put(side):
            for o in range(2):
                for k in range(8):
                    spot = ((k // 2 % 2) ^ where[1], (k % 2) ^ where[2], (k // 4) ^ (where[0] % 2))
                    at = k * 192 + o * 96
                    for h in range(2):
                        down_packs[o ^ side][spot + (slice(h * 96, h * 96 + 96),)] = grad_down[
                            at : at + 96, h * 384 : h * 384 + 384
                        ]
                    rows = grad_up[k * 48 + o * 24 : k * 48 + o * 24 + 24]
                    for j in range(4):
                        both = [rows[:, i * 384 : i * 384 + 384] for i in (2 * j, 2 * j + 1)]
                        up_packs[o ^ side][spot + (slice(j * 48, j * 48 + 48),)] = jnp.concatenate(
                            both, axis=0
                        ).astype(LOW)

        for side in range(2):
            pl.when(core == side)(functools.partial(put, side))


def feed_call(where, att_t, tokens, cot, bias_up, vec, pieces, pieces_down):
    tile = lambda step: jnp.minimum(step, TILES - 1)
    rows = pl.BlockSpec((TILE, 768), lambda s, where: (tile(s), 0))
    fixed = lambda shape: pl.BlockSpec(shape, lambda s, where: (0,) * len(shape), pipeline_mode=pl.Buffered(1))
    pack = (2, 2, 4, 192, 384)
    pack_block = pl.BlockSpec(
        (2, 2, 2, 192, 384), lambda s, where: (0, 0, jnp.clip(s - TILES, 0, 1) ^ (where[0] // 2), 0, 0))
    return pl.pallas_call(
        feed_kernel,
        grid_spec=pltpu.PrefetchScalarGridSpec(
            num_scalar_prefetch=1,
            grid=(TILES + 2,),
            in_specs=[
                pl.BlockSpec((768, TILE), lambda s, where: (0, tile(s))), rows, fixed((1024, 768)),
                fixed((1, 3072)), fixed((16, 768)),
            ] + [ANY] * 20,
            out_specs=[
                rows, rows, rows, rows, fixed((8, 768)), fixed((1, 3072)), *([pack_block] * 4),
            ],
            scratch_shapes=[
                pltpu.VMEM((768, 3072), LOW),
                pltpu.VMEM((3072, 768), LOW),
                pltpu.VMEM((768, 768), LOW),
                pltpu.VMEM((1024, 768), LOW),
                pltpu.VMEM((1024, 3072), LOW),
                pltpu.VMEM((1024, 3072), LOW),
                pltpu.SemaphoreType.DMA((3,)),
            ],
        ),
        out_shape=[
            jax.ShapeDtypeStruct((1024, 768), LOW),
            jax.ShapeDtypeStruct((1024, 768), FULL),
            jax.ShapeDtypeStruct((1024, 768), LOW),
            jax.ShapeDtypeStruct((1024, 768), LOW),
            jax.ShapeDtypeStruct((8, 768), FULL),
            jax.ShapeDtypeStruct((1, 3072), FULL),
        ] + [jax.ShapeDtypeStruct(pack, LOW)] * 4,
        compiler_params=params(),
        cost_estimate=cost(26 * 1024 * 768 * 768 * 2, 35e6, 3e6, scale=FEED_SCALE),
        name="feed",
    )(where, att_t, tokens, cot, bias_up, vec, *pieces, *pieces_down)


ROWS_STEP = 2


def unattend_kernel(groups, with_out, where, *refs):
    count = len(groups)
    parts = [refs[5 * g : 5 * g + 5] for g in range(count)]
    refs = refs[5 * count + (0 if with_out else 2) :]
    probs, normed = refs[:count], refs[count]
    refs = refs[count + 1 :]
    if with_out:
        att_t, branch_grad, refs = refs[0], refs[1], refs[2:]
        mixed, mine, theirs, sums, acc, wide, slim, stacks, out_acc = refs
    else:
        mixed, mine, theirs, sums, acc, wide, slim, stacks = refs
    step = pl.program_id(0)
    width = 128 * count
    blocks = [(r, g, h) for r in range(ROWS_STEP) for g in range(count) for h in range(2)]

    def keys_of(r, b):
        return slice(256 * r + 64 * b, 256 * r + 64 * b + 192)

    def queries_of(r, b):
        return slice(256 * r + 128 * b, 256 * r + 128 * b + 128)

    for i, (r, g, half) in enumerate(blocks):
        query, key, value = parts[g][:3]
        grads = parts[g][3 + half]
        for b in range(2):
            stacks[0, 2 * i + b] = masked_pair(query[half, queries_of(r, b), :])
            stack = masked_pair(grads[queries_of(r, b), :])
            stacks[1, 2 * i + b] = stack
            wide[2 * i + b] = mul_t(value[half, keys_of(r, b), :], stack)
    for i, (r, g, half) in enumerate(blocks):
        for b in range(2):
            weights = probs[g][r, 0, half, b].astype(FULL)
            prob_grad = wide[2 * i + b]
            inner = jnp.sum(prob_grad * weights, axis=0, keepdims=True)
            slim[2 * i + b] = (weights * (prob_grad - inner)).astype(LOW)

    def merge(first, second):
        return jnp.concatenate([first[0:64], first[64:192] + second[0:128], second[128:192]], axis=0)

    for i, (r, g, half) in enumerate(blocks):
        key = parts[g][1]
        rows = slice(256 * r, 256 * r + 256)
        value_grad = [mul(probs[g][r, 0, half, b], stacks[1, 2 * i + b]) for b in range(2)]
        key_grad = [mul(slim[2 * i + b], stacks[0, 2 * i + b]) for b in range(2)]
        turned = [unmask(t_mul(key[half, keys_of(r, b), :], slim[2 * i + b])) for b in range(2)]
        query_grad = jnp.transpose(jnp.concatenate(turned, axis=1)) * 0.125
        at = g * 128
        mixed[half, rows, at : at + 128] = query_grad.astype(LOW)
        mixed[half, rows, width + at : width + at + 128] = merge(*key_grad).astype(LOW)
        mixed[half, rows, 2 * width + at : 2 * width + at + 128] = merge(*value_grad).astype(LOW)

    def add(target, more):
        @pl.when(step == 0)
        def _():
            target[...] = more

        @pl.when(step > 0)
        def _():
            target[...] += more

    for half in range(2):
        add_rows(sums.at[half], 0, mixed[half].astype(FULL), step)
        add(acc.at[half], t_mul(normed[...], mixed[half]))
    if with_out:
        add(out_acc, mul(att_t[...], branch_grad[...]))

    def write(side):
        for owner in range(2):
            dest = mine if owner == side else theirs
            for chip in range(16):
                rows = slice(chip * 48 + owner * 24, chip * 48 + owner * 24 + 24)
                spot = ((chip // 2 % 2) ^ where[1], (chip % 2) ^ where[2], (chip // 4) ^ where[0], slice(None))
                if with_out:
                    lines = [out_acc[rows, :], jnp.concatenate([acc[0, rows, :], acc[1, rows, :]], axis=1)]
                else:
                    lines = [acc[0, rows, :], acc[1, rows, :]]
                dest[spot + (slice(0, 768),)] = jnp.concatenate(lines, axis=0).astype(LOW)

    for side in range(2):
        pl.when((step == 4 // ROWS_STEP - 1) & (where[3] == side))(functools.partial(write, side))


def unattend_call(groups, where, qkv, att_grad, probs, normed, packs=None, att_t=None, branch_grad=None):
    with_out = att_t is not None
    count = len(groups)
    width = 384 * count
    tall = 256 * ROWS_STEP
    operands, specs = [], []
    for p in groups:
        for part in range(3):
            operands.append(qkv)
            specs.append(pl.BlockSpec((2, tall, 128), lambda r, c=part * 3 + p: (0, r, c)))
        for half in range(2):
            operands.append(att_grad)
            specs.append(pl.BlockSpec((tall, 128), lambda r, c=half * 3 + p: (r, c)))
    if not with_out:
        operands += list(packs)
        specs += [ANY, ANY]
    for p in groups:
        operands.append(probs)
        specs.append(pl.BlockSpec((ROWS_STEP, 1, 2, 2, 192, 256), lambda r, p=p: (r, p, 0, 0, 0, 0)))
    operands.append(normed)
    specs.append(pl.BlockSpec((tall, 768), lambda r: (r, 0)))
    if with_out:
        operands += [att_t, branch_grad]
        specs += [pl.BlockSpec((768, tall), lambda r: (0, r)), pl.BlockSpec((tall, 768), lambda r: (r, 0))]
    shape = (2, 2, 4, 48, 1664)
    lanes = 0 if with_out else 1
    part_of = pl.BlockSpec((2, 2, 4, 48, 768), lambda r: (0, 0, 0, 0, lanes), pipeline_mode=pl.Buffered(1))
    many = 4 * count * ROWS_STEP
    return pl.pallas_call(
        functools.partial(unattend_kernel, groups, with_out),
        grid=(4 // ROWS_STEP,),
        out_shape=[
            jax.ShapeDtypeStruct((2, 1024, width), LOW),
            jax.ShapeDtypeStruct(shape, LOW),
            jax.ShapeDtypeStruct(shape, LOW),
            jax.ShapeDtypeStruct((2, 8, width), FULL),
        ],
        in_specs=[SMEM] + specs,
        out_specs=[
            pl.BlockSpec((2, tall, width), lambda r: (0, r, 0)),
            part_of,
            part_of,
            whole((2, 8, width)),
        ],
        input_output_aliases={} if with_out else {1 + 5 * count + k: 1 + k for k in range(2)},
        scratch_shapes=[
            pltpu.VMEM((2, 768, width), FULL),
            pltpu.VMEM((many, 192, 256), FULL),
            pltpu.VMEM((many, 192, 256), LOW),
            pltpu.VMEM((2, many, 256, 128), LOW),
        ] + ([pltpu.VMEM((768, 768), FULL)] if with_out else []),
        compiler_params=params(),
        cost_estimate=cost(count * 2.5e9, count * 8e6),
        name="unattend%d" % groups[0],
    )(where, *operands)


def tokens_kernel(
    where, m0, m1, w1, tok, vec, middle_grad, sums, sums0, sums1, bias, mine_in, theirs_in, grad, mine, theirs, lines, turned
):
    step = pl.program_id(0)
    total = None
    for half in range(2):
        joined = []
        for part in range(3):
            joined.append(m0[half, :, part * 128 : part * 128 + 128])
            joined.append(m1[half, :, part * 256 : part * 256 + 256])
        more = mul_t(jnp.concatenate(joined, axis=1), w1[half])
        total = more if total is None else total + more
    xhat, spread = normalise(tok[...].astype(FULL))
    grad[...] = middle_grad[...] + back_norm(total, xhat, spread, vec[0:1, :])
    add_rows(lines, 0, total * xhat, step)
    add_rows(lines, 1, total, step)

    @pl.when(step == 3)
    def _():
        for half in range(2):
            at = half * 384
            for row, part in ((2, 0), (3, 2)):
                lines[row : row + 1, at : at + 128] = sums0[half, 0:1, part * 128 : part * 128 + 128]
                lines[row : row + 1, at + 128 : at + 384] = sums1[half, 0:1, part * 256 : part * 256 + 256]
        lines[4:5, :] = sums[2:3, :]
        lines[5:6, :] = sums[0:1, :]
        lines[6:7, :] = sums[1:2, :]
        lines[7:8, :] = sums[3:4, :]
        lines[8:128, :] = jnp.zeros((120, 768), FULL)
        turned[...] = jnp.transpose(lines[...])
        for device in range(32):
            turned[device * 24 : device * 24 + 1, 16:112] = bias[0:1, device * 96 : device * 96 + 96]

        def write(side):
            for owner in range(2):
                dest = mine if owner == side else theirs
                for chip in range(16):
                    at = (chip * 2 + owner) * 24
                    spot = ((chip // 2 % 2) ^ where[1], (chip % 2) ^ where[2], (chip // 4) ^ where[0])
                    both = [turned[at : at + 24, :], jnp.zeros((24, 128), FULL)]
                    dest[spot] = jnp.concatenate(both, axis=0).astype(LOW)

        for side in range(2):
            pl.when(where[3] == side)(functools.partial(write, side))


def tokens_call(where, mixed0, mixed1, w1, tokens, vec, middle_grad, sums, sums0, sums1, bias, mine, theirs):
    rows = pl.BlockSpec((256, 768), lambda r: (r, 0))
    part_of = pl.BlockSpec((2, 2, 4, 48, 128), lambda r: (0, 0, 0, 0, 12), pipeline_mode=pl.Buffered(1))
    return pl.pallas_call(
        tokens_kernel,
        grid=(4,),
        out_shape=[jax.ShapeDtypeStruct((1024, 768), FULL)] + [jax.ShapeDtypeStruct(mine.shape, LOW)] * 2,
        in_specs=[SMEM] + [pl.BlockSpec((2, 256, w), lambda r: (0, r, 0)) for w in (384, 768)] + [
            whole((2, 768, 1152)), rows, whole((16, 768)), rows, whole((8, 768)), whole((2, 8, 384)),
            whole((2, 8, 768)), whole((1, 3072)), ANY, ANY,
        ],
        out_specs=[rows, part_of, part_of],
        input_output_aliases={11: 1, 12: 2},
        scratch_shapes=[pltpu.VMEM((128, 768), FULL), pltpu.VMEM((768, 128), FULL)],
        compiler_params=params(),
        cost_estimate=cost(2 * 1024 * 768 * 2304, 16e6),
        name="tokens",
    )(where, mixed0, mixed1, w1, tokens, vec, middle_grad, sums, sums0, sums1, bias, mine, theirs)


def after(value, *before):
    return lax.optimization_barrier((value, before))[0]


class Total:
    def __init__(self, mine, theirs):
        self.mine = mine
        self.block = mine.shape[3:]
        self.got = send(theirs, SWAP_C)

    def spec(self, size, place_of):
        return pl.BlockSpec(size + self.block, lambda i: place_of(i) + (0, 0))

    def low(self, *lead):
        return jax.ShapeDtypeStruct(lead + self.block, LOW)

    def first(self):
        def body(mine_x, got_x, mine_y, got_y, out_x, out_y):
            out_x[...] = (mine_x[...].astype(FULL) + got_x[...].astype(FULL)).reshape(out_x.shape).astype(LOW)
            out_y[...] = (mine_y[...].astype(FULL) + got_y[...].astype(FULL)).reshape(out_y.shape).astype(LOW)

        to_x = self.spec((1, 1, 2), lambda i: (i, 1, 0))
        to_y = self.spec((1, 1, 2), lambda i: (1, i, 1))
        out = self.spec((1, 2), lambda i: (i, 0))

        def keep(one_x, one_y):
            self.one_x, self.one_y = send(one_x, SWAP_X), send(one_y, SWAP_Y)

        return (body, [self.mine, self.got] * 2, [to_x, to_x, to_y, to_y], [self.low(2, 2)] * 2, [out] * 2, keep)

    def second(self):
        def body(mine_y, got_y, one_x, mine_x, got_x, one_y, out_y, out_x):
            add = lambda *refs: sum(r[...].astype(FULL).reshape(out_y.shape) for r in refs)
            out_y[...] = add(mine_y, got_y, one_x).astype(LOW)
            out_x[...] = add(mine_x, got_x, one_y).astype(LOW)

        to_y = self.spec((1, 1, 1), lambda i: (1, 0, i))
        to_x = self.spec((1, 1, 1), lambda i: (0, 1, 2 + i))
        came = self.spec((1, 1), lambda i: (1, i))
        out = self.spec((1,), lambda i: (i,))

        def keep(two_y, two_x):
            self.two_y, self.two_x = send(two_y, SWAP_Y), send(two_x, SWAP_X)

        operands = [self.mine, self.got, self.one_x, self.mine, self.got, self.one_y]
        return (body, operands, [to_y, to_y, came, to_x, to_x, came], [self.low(2)] * 2, [out] * 2, keep)

    def third(self):
        def body(mine, got, one_x, two_y, one_y, two_x, *outs):
            @pl.when(pl.program_id(0) == 0)
            def _():
                for k, target in enumerate(outs):
                    extra = (one_x[0, k], two_y[k]) if k < 2 else (one_y[0, k - 2], two_x[k - 2])
                    total = mine[0, 0, k].astype(FULL) + got[0, 0, k].astype(FULL)
                    total = total + extra[0].astype(FULL) + extra[1].astype(FULL)
                    target[...] = total.astype(target.dtype)

        near = self.spec((1, 1, 4), lambda i: (0, 0, 0))
        came = self.spec((1, 2), lambda i: (0, 0))
        two = self.spec((2,), lambda i: (0,))
        one = pl.BlockSpec(self.block, lambda i: (0, 0))
        out = [jax.ShapeDtypeStruct(self.block, FULL)] + [self.low()] * 3

        def keep(own, *three):
            self.own = own
            self.parts = [send(v, SWAP_Z[k + 1]) for k, v in enumerate(three)]

        operands = [self.mine, self.got, self.one_x, self.two_y, self.one_y, self.two_x]
        return (body, operands, [near, near, came, two, came, two], out, [one] * 4, keep)

    def last(self, write, shapes, more=()):
        def body(own, part1, part2, part3, *refs):
            @pl.when(pl.program_id(0) == 0)
            def _():
                total = own[...] + part1[...].astype(FULL) + part2[...].astype(FULL) + part3[...].astype(FULL)
                write(total, *refs)

        block = pl.BlockSpec(self.block, lambda i: (0, 0))
        same = lambda shape: pl.BlockSpec(shape, lambda i: (0,) * len(shape))

        def keep(*given):
            self.final = given

        return (
            body, [self.own, *self.parts, *more], [block] * 4 + [same(v.shape) for v in more],
            [jax.ShapeDtypeStruct(v, FULL) for v in shapes], [same(v) for v in shapes], keep,
        )


def write_down(total, share):
    share[...] = jnp.concatenate([total[0:96], total[96:192]], axis=1)


def write_up(total, share):
    share[...] = jnp.concatenate([total[j * 24 : j * 24 + 24] for j in range(8)], axis=1)


def write_head(total, share_out, share, *vectors):
    share_out[...] = total[0:24, 0:768]
    for half in range(2):
        for part in range(3):
            at = part * 768 + half * 384
            first = half * 384 + part * 128
            share[:, at : at + 128] = total[24:48, first : first + 128]
            rest = 768 + part * 256
            share[:, at + 128 : at + 384] = total[half * 24 : half * 24 + 24, rest : rest + 256]
    columns = jnp.concatenate([total[0:24, 1536:1664], jnp.zeros((104, 128), FULL)], axis=0)
    lines = jnp.transpose(columns)
    for row in range(8):
        vectors[row][...] = lines[row : row + 1, 0:24].reshape(24)
    vectors[8][...] = total[0:1, 1552:1648].reshape(96)


def run_stages(stages, *before):
    ins = [len(s[1]) for s in stages]
    outs = [len(s[3]) for s in stages]

    def kernel(*refs):
        at_in, at_out = 0, sum(ins)
        for stage, n_in, n_out in zip(stages, ins, outs):
            stage[0](*refs[at_in : at_in + n_in], *refs[at_out : at_out + n_out])
            at_in, at_out = at_in + n_in, at_out + n_out

    operands = after([v for s in stages for v in s[1]], *before)
    results = pl.pallas_call(
        kernel,
        grid=(2,),
        out_shape=[v for s in stages for v in s[3]],
        in_specs=[v for s in stages for v in s[2]],
        out_specs=[v for s in stages for v in s[4]],
        compiler_params=params(),
        cost_estimate=cost(1e6, 4e6),
        name="sums",
    )(*operands)
    at = 0
    for stage, n_out in zip(stages, outs):
        stage[5](*results[at : at + n_out])
        at += n_out
    return results


def halves_of(own, sibling, core):
    return jnp.where(core == 0, own, sibling), jnp.where(core == 0, sibling, own)


def on_device(
    tokens, segment_ids, pad_mask, w_qkv, w_out, w_up, w_down, gain_one, shift_one, bias_query,
    bias_value, bias_out, gain_two, shift_two, bias_up, bias_down, cotangent,
):
    z0, y0, x0, core = place()
    where = jnp.stack([z0, y0, x0, core]).astype(jnp.int32)
    row_count, length, width = tokens.shape
    total_rows = row_count * length
    flat = tokens.reshape(total_rows, width)
    cot = cotangent.reshape(total_rows, width)
    vectors = (gain_one, shift_one, bias_query, bias_value, bias_out, gain_two, shift_two, bias_down, bias_up)

    def along_z(own):
        return [send(own[None], SWAP_Z[k]) for k in (1, 2, 3)]

    def column(own, rest):
        return jnp.concatenate([own[None], *rest], axis=0)

    def plane(col):
        return send(col, SWAP_X), send(col, SWAP_Y)

    def corner(along_x, along_y):
        return send(along_x[0:2], SWAP_Y), send(along_y[2:4], SWAP_X)

    def across(blocks):
        return [send(v, SWAP_C) for v in blocks]

    p1 = first_call(w_qkv, vectors)
    rest1 = along_z(p1)
    mine = (w_out, w_up, w_down)
    p2, p3 = prep(where, after(mine, p1), across(mine))
    col1 = column(after(p1, p2), rest1)
    x1, y1 = plane(col1)
    rest2 = along_z(after(p2, col1))
    col2 = column(p2, rest2)
    far1 = corner(x1, y1)
    own1 = [col1, x1, y1]
    pack1 = own1 + list(far1) + across(own1) + across(far1)
    col2 = after(col2, far1)
    x2, y2 = plane(col2)
    rest3 = along_z(after(p3, col2))
    qkv, normed_one, w1, vec, up_line = qkv_call(where, after(flat, col2), pack1)
    col3 = column(after(p3, qkv), rest3)
    x3, y3 = plane(col3)
    held = attend_call(0, 2, after(qkv, col3), segment_ids, pad_mask, None)
    far2 = corner(x2, y2)
    other2 = across(after([col2, x2, y2], held))
    probs, att_t = attend_call(2, 2, after(qkv, x2, y2), segment_ids, pad_mask, held)
    pack2 = [col2, x2, y2, *far2] + other2 + across(after(far2, att_t))
    far3 = corner(after(x3, att_t), after(y3, att_t))
    own3 = [col3, x3, y3]
    pack3 = own3 + list(far3) + across(after(own3, att_t, other2)) + across(far3)
    output, middle_grad, branch_grad, att_grad, sums, bias_grad, *grads = feed_call(
        where, att_t, flat, cot, up_line, vec, pack2, pack3)

    sum_a, sum_b = Total(*grads[:2]), Total(*grads[2:])
    ready = run_stages([sum_a.first()])
    mixed0, mine, theirs, sums0 = unattend_call(
        (0,), where, qkv, after(att_grad, ready), probs, normed_one, None, att_t, branch_grad)
    ready = run_stages([sum_a.second(), sum_b.first()], mixed0)
    mixed1, mine, theirs, sums1 = unattend_call(
        (1, 2), where, qkv, after(att_grad, ready), probs, normed_one, (mine, theirs))
    ready = run_stages([sum_a.third(), sum_b.second()], mixed1)
    grad_tokens, mine, theirs = tokens_call(
        where, mixed0, after(mixed1, ready), w1, flat, vec, middle_grad, sums, sums0, sums1, bias_grad, mine, theirs)
    ready = run_stages([sum_b.third(), sum_a.last(write_down, [(96, 768)])], grad_tokens)
    head = Total(mine, after(theirs, ready))
    ready = run_stages([head.first()], ready)
    ready = run_stages([head.second(), sum_b.last(write_up, [(24, 3072)])], ready)
    ready = run_stages([head.third()], ready)
    run_stages([head.last(write_head, [(24, 768), (24, 2304)] + [(24,)] * 8 + [(96,)])], ready)
    share_out, share_qkv, *own = head.final
    share_up, share_down = sum_b.final[0], sum_a.final[0]
    return (
        output.reshape(row_count, length, width),
        grad_tokens.reshape(row_count, length, width),
        share_qkv, share_out, share_up, share_down,
        own[0], own[1], own[2], own[3], own[4], own[5], own[6], own[8], own[7],
    )


def solution(mesh):
    fits = dict(mesh.shape) == {"gx": 8, "gy": 4}
    device = on_device if fits else generic_device
    names = AXES if fits else ("gx", "gy")
    if fits:
        mesh = Mesh(mesh.devices.reshape(4, 2, 2, 2), AXES)
    return jax.shard_map(
        device,
        mesh=mesh,
        in_specs=(
            P(names, None, None),
            P(names, None),
            P(names, None),
            P(names, None),
            P(names, None),
            P(names, None),
            P(names, None),
            P(names),
            P(names),
            P(names),
            P(names),
            P(names),
            P(names),
            P(names),
            P(names),
            P(names),
            P(names, None, None),
        ),
        out_specs=(
            P(names, None, None),
            P(names, None, None),
            P(names, None),
            P(names, None),
            P(names, None),
            P(names, None),
            P(names),
            P(names),
            P(names),
            P(names),
            P(names),
            P(names),
            P(names),
            P(names),
            P(names),
        ),
        check_vma=False,
    )
```

```python
import functools
import math

import jax
import jax.numpy as jnp
from jax import lax
from jax.experimental import pallas as pl
from jax.experimental.pallas import tpu as pltpu
from jax.sharding import Mesh
from jax.sharding import PartitionSpec as P

HEADS = 12
HDIM = 64


def layer_norm(values, gain, shift):
    centre = values - jnp.mean(values, axis=-1, keepdims=True)
    spread = jnp.mean(centre * centre, axis=-1, keepdims=True)
    return centre * lax.rsqrt(spread + 1e-06) * gain + shift


def smooth_gate(values):
    return jax.nn.gelu(values, approximate=True)


def attend_mask(segment_ids, pad_mask):
    length = segment_ids.shape[-1]
    positions = jnp.arange(length)
    same = segment_ids[:, :, None] == segment_ids[:, None, :]
    real = pad_mask[:, None, :] == 1
    itself = positions[:, None] == positions[None, :]
    return same & (real | itself[None])


def outer_sum(left, right):
    return lax.dot_general(
        left, right, (((0,), (0,)), ((), ())), preferred_element_type=jnp.float32
    )


def against(left, matrix):
    return lax.dot_general(
        left, matrix, (((1,), (1,)), ((), ())), preferred_element_type=jnp.float32
    )


def score_block(query_part, key_part, allowed):
    raw = jnp.einsum("rqhe,rkhe->rhqk", query_part, key_part, preferred_element_type=jnp.float32)
    raw = raw * (1.0 / math.sqrt(HDIM))
    return jnp.where(allowed[:, None], raw, -1e30)


def collect(
    w_qkv,
    w_out,
    w_up,
    w_down,
    gain_one,
    shift_one,
    bias_query,
    bias_value,
    bias_out,
    gain_two,
    shift_two,
    bias_up,
    bias_down,
):
    return (
        lax.all_gather(w_qkv, ("gx", "gy"), axis=0, tiled=True),
        lax.all_gather(w_out, ("gx", "gy"), axis=0, tiled=True),
        lax.all_gather(w_up, ("gx", "gy"), axis=0, tiled=True),
        lax.all_gather(w_down, ("gx", "gy"), axis=0, tiled=True),
        lax.all_gather(gain_one, ("gx", "gy"), axis=0, tiled=True),
        lax.all_gather(shift_one, ("gx", "gy"), axis=0, tiled=True),
        lax.all_gather(bias_query, ("gx", "gy"), axis=0, tiled=True),
        lax.all_gather(bias_value, ("gx", "gy"), axis=0, tiled=True),
        lax.all_gather(bias_out, ("gx", "gy"), axis=0, tiled=True),
        lax.all_gather(gain_two, ("gx", "gy"), axis=0, tiled=True),
        lax.all_gather(shift_two, ("gx", "gy"), axis=0, tiled=True),
        lax.all_gather(bias_up, ("gx", "gy"), axis=0, tiled=True),
        lax.all_gather(bias_down, ("gx", "gy"), axis=0, tiled=True),
    )


def generic_device(
    tokens,
    segment_ids,
    pad_mask,
    w_qkv,
    w_out,
    w_up,
    w_down,
    gain_one,
    shift_one,
    bias_query,
    bias_value,
    bias_out,
    gain_two,
    shift_two,
    bias_up,
    bias_down,
    cotangent,
):
    row_count, length, width = tokens.shape
    total_rows = row_count * length
    gathered = collect(
        w_qkv,
        w_out,
        w_up,
        w_down,
        gain_one,
        shift_one,
        bias_query,
        bias_value,
        bias_out,
        gain_two,
        shift_two,
        bias_up,
        bias_down,
    )
    full_qkv, full_out, full_up, full_down = (gathered[0], gathered[1], gathered[2], gathered[3])
    gain_first = gathered[4].astype(jnp.float32)
    shift_first = gathered[5].astype(jnp.float32)
    query_bias = gathered[6].astype(jnp.float32)
    value_bias = gathered[7].astype(jnp.float32)
    out_bias = gathered[8].astype(jnp.float32)
    gain_second = gathered[9].astype(jnp.float32)
    shift_second = gathered[10].astype(jnp.float32)
    up_bias = gathered[11].astype(jnp.float32)
    down_bias = gathered[12].astype(jnp.float32)
    allowed = attend_mask(segment_ids, pad_mask)
    inputs = tokens.astype(jnp.float32).reshape(total_rows, width)
    first_norm, first_pull = jax.vjp(layer_norm, inputs, gain_first, shift_first)
    normed = first_norm.astype(jnp.bfloat16)
    mixed = jnp.dot(normed, full_qkv, preferred_element_type=jnp.float32)
    query_part = (
        (mixed[:, :width] + query_bias).astype(jnp.bfloat16).reshape(row_count, length, HEADS, HDIM)
    )
    key_part = (
        mixed[:, width : 2 * width].astype(jnp.bfloat16).reshape(row_count, length, HEADS, HDIM)
    )
    value_part = (
        (mixed[:, 2 * width :] + value_bias)
        .astype(jnp.bfloat16)
        .reshape(row_count, length, HEADS, HDIM)
    )
    scores = score_block(query_part, key_part, allowed)
    highest = jnp.max(scores, axis=-1, keepdims=True)
    log_total = highest + jnp.log(jnp.sum(jnp.exp(scores - highest), axis=-1, keepdims=True))
    weights = jnp.exp(scores - log_total).astype(jnp.bfloat16)
    attended = jnp.einsum(
        "rhqk,rkhe->rqhe", weights, value_part, preferred_element_type=jnp.float32
    )
    attended = attended.reshape(total_rows, width).astype(jnp.bfloat16)
    middle = inputs + jnp.dot(attended, full_out, preferred_element_type=jnp.float32) + out_bias
    second_norm, second_pull = jax.vjp(layer_norm, middle, gain_second, shift_second)
    normed_two = second_norm.astype(jnp.bfloat16)
    hidden = jnp.dot(normed_two, full_up, preferred_element_type=jnp.float32) + up_bias
    active, gate_pull = jax.vjp(smooth_gate, hidden)
    active_low = active.astype(jnp.bfloat16)
    result = middle + jnp.dot(active_low, full_down, preferred_element_type=jnp.float32) + down_bias
    output = result.astype(jnp.bfloat16).reshape(row_count, length, width)
    again = collect(
        w_qkv,
        w_out,
        w_up,
        w_down,
        gain_one,
        shift_one,
        bias_query,
        bias_value,
        bias_out,
        gain_two,
        shift_two,
        bias_up,
        bias_down,
    )
    full_qkv, full_out, full_up, full_down = (again[0], again[1], again[2], again[3])
    down_in = cotangent.reshape(total_rows, width)
    outer_grad = down_in.astype(jnp.float32)
    grad_bias_down = jnp.sum(outer_grad, axis=0)
    grad_w_down = outer_sum(active_low, down_in)
    active_grad = against(down_in, full_down)
    hidden_grad = gate_pull(active_grad)[0].astype(jnp.bfloat16)
    grad_bias_up = jnp.sum(hidden_grad.astype(jnp.float32), axis=0)
    grad_w_up = outer_sum(normed_two, hidden_grad)
    norm_two_grad = against(hidden_grad, full_up)
    middle_part, grad_gain_two, grad_shift_two = second_pull(norm_two_grad)
    middle_grad = outer_grad + middle_part
    branch_grad = middle_grad.astype(jnp.bfloat16)
    grad_bias_out = jnp.sum(branch_grad.astype(jnp.float32), axis=0)
    grad_w_out = outer_sum(attended, branch_grad)
    attended_grad = (
        against(branch_grad, full_out).astype(jnp.bfloat16).reshape(row_count, length, HEADS, HDIM)
    )
    probs = jnp.exp(score_block(query_part, key_part, allowed) - log_total)
    probs_low = probs.astype(jnp.bfloat16)
    value_grad = jnp.einsum(
        "rhqk,rqhe->rkhe", probs_low, attended_grad, preferred_element_type=jnp.float32
    ).astype(jnp.bfloat16)
    prob_grad = jnp.einsum(
        "rqhe,rkhe->rhqk", attended_grad, value_part, preferred_element_type=jnp.float32
    )
    inner_term = jnp.sum(prob_grad * probs, axis=-1, keepdims=True)
    score_grad = (probs * (prob_grad - inner_term)).astype(jnp.bfloat16)
    score_scale = 1.0 / math.sqrt(HDIM)
    query_grad = (
        (
            jnp.einsum("rhqk,rkhe->rqhe", score_grad, key_part, preferred_element_type=jnp.float32)
            * score_scale
        )
        .astype(jnp.bfloat16)
        .reshape(total_rows, width)
    )
    key_grad = (
        (
            jnp.einsum(
                "rhqk,rqhe->rkhe", score_grad, query_part, preferred_element_type=jnp.float32
            )
            * score_scale
        )
        .astype(jnp.bfloat16)
        .reshape(total_rows, width)
    )
    value_flat = value_grad.reshape(total_rows, width)
    mixed_grad = jnp.concatenate([query_grad, key_grad, value_flat], axis=1)
    grad_bias_query = jnp.sum(query_grad.astype(jnp.float32), axis=0)
    grad_bias_value = jnp.sum(value_flat.astype(jnp.float32), axis=0)
    grad_w_qkv = outer_sum(normed, mixed_grad)
    norm_one_grad = against(mixed_grad, full_qkv)
    input_part, grad_gain_one, grad_shift_one = first_pull(norm_one_grad)
    grad_tokens = (middle_grad + input_part).reshape(row_count, length, width)
    shares = (
        lax.psum_scatter(grad_w_qkv, ("gx", "gy"), scatter_dimension=0, tiled=True),
        lax.psum_scatter(grad_w_out, ("gx", "gy"), scatter_dimension=0, tiled=True),
        lax.psum_scatter(grad_w_up, ("gx", "gy"), scatter_dimension=0, tiled=True),
        lax.psum_scatter(grad_w_down, ("gx", "gy"), scatter_dimension=0, tiled=True),
        lax.psum_scatter(grad_gain_one, ("gx", "gy"), scatter_dimension=0, tiled=True),
        lax.psum_scatter(grad_shift_one, ("gx", "gy"), scatter_dimension=0, tiled=True),
        lax.psum_scatter(grad_bias_query, ("gx", "gy"), scatter_dimension=0, tiled=True),
        lax.psum_scatter(grad_bias_value, ("gx", "gy"), scatter_dimension=0, tiled=True),
        lax.psum_scatter(grad_bias_out, ("gx", "gy"), scatter_dimension=0, tiled=True),
        lax.psum_scatter(grad_gain_two, ("gx", "gy"), scatter_dimension=0, tiled=True),
        lax.psum_scatter(grad_shift_two, ("gx", "gy"), scatter_dimension=0, tiled=True),
        lax.psum_scatter(grad_bias_up, ("gx", "gy"), scatter_dimension=0, tiled=True),
        lax.psum_scatter(grad_bias_down, ("gx", "gy"), scatter_dimension=0, tiled=True),
    )
    return (
        output,
        grad_tokens,
        shares[0],
        shares[1],
        shares[2],
        shares[3],
        shares[4],
        shares[5],
        shares[6],
        shares[7],
        shares[8],
        shares[9],
        shares[10],
        shares[11],
        shares[12],
    )


CHIPS = ("z", "y", "x")
AXES = CHIPS + ("core",)


def pairs(move):
    out = []
    for d in range(32):
        z, y, x, c = d // 8, (d // 4) % 2, (d // 2) % 2, d % 2
        z, y, x, c = move(z, y, x, c)
        out.append((d, ((z * 2 + y) * 2 + x) * 2 + c))
    return out


SWAP_C = pairs(lambda z, y, x, c: (z, y, x, 1 - c))
SWAP_X = pairs(lambda z, y, x, c: (z, y, 1 - x, c))
SWAP_Y = pairs(lambda z, y, x, c: (z, 1 - y, x, c))
SWAP_D = pairs(lambda z, y, x, c: (z, 1 - y, 1 - x, c))
SWAP_Z = [None] + [pairs(lambda z, y, x, c, k=k: (z ^ k, y, x, c)) for k in (1, 2, 3)]


def send(values, perm):
    return lax.ppermute(values, AXES, perm)


def place():
    return tuple(lax.axis_index(name) for name in AXES)


LOW = jnp.bfloat16
FULL = jnp.float32
ANY = pl.BlockSpec(memory_space=pl.ANY)
SMEM = pl.BlockSpec(memory_space=pltpu.SMEM)
MIB = 1024 * 1024


def whole(shape):
    zeros = (0,) * len(shape)
    return pl.BlockSpec(shape, lambda *_: zeros, pipeline_mode=pl.Buffered(1))


def params(limit=64):
    return pltpu.CompilerParams(vmem_limit_bytes=limit * MIB)


def cost(flops, read, exps=0, scale=10.0):
    return pl.CostEstimate(
        flops=int(scale * flops), bytes_accessed=int(scale * read), transcendentals=int(scale * exps)
    )


def mul(left, right):
    return lax.dot_general(left, right, (((1,), (0,)), ((), ())), preferred_element_type=FULL)


def mul_t(left, right):
    return lax.dot_general(left, right, (((1,), (1,)), ((), ())), preferred_element_type=FULL)


def t_mul(left, right):
    return lax.dot_general(left, right, (((0,), (0,)), ((), ())), preferred_element_type=FULL)


def first_kernel(qkv, v0, v1, v2, v3, v4, v5, v6, v7, up, out, tall):
    out[:, 0:2304] = qkv[...]
    tall[...] = jnp.zeros_like(tall)
    for row, vector in enumerate((v0, v1, v2, v3, v4, v5, v6, v7)):
        tall[row : row + 1, 0:24] = vector[...].astype(FULL).reshape(1, 24)
    turned = jnp.transpose(tall[...])[0:24]
    lane = lax.broadcasted_iota(jnp.int32, (24, 128), 1)
    row = lax.broadcasted_iota(jnp.int32, (24, 128), 0)
    tall[0:1, 16:112] = up[...].astype(FULL).reshape(1, 96)
    line = jnp.broadcast_to(tall[0:1, :], (24, 128))
    keep = (row == 0) & (lane >= 16) & (lane < 112)
    out[:, 2304:2432] = jnp.where(lane < 8, turned, jnp.where(keep, line, 0.0)).astype(LOW)


def first_call(qkv, vectors):
    return pl.pallas_call(
        first_kernel,
        out_shape=jax.ShapeDtypeStruct((24, 2432), LOW),
        in_specs=[pl.BlockSpec(memory_space=pltpu.VMEM)] * 10,
        out_specs=pl.BlockSpec(memory_space=pltpu.VMEM),
        scratch_shapes=[pltpu.VMEM((128, 128), FULL)],
        compiler_params=params(),
        cost_estimate=cost(1e5, 3e5),
        name="first",
    )(qkv, *vectors)


def prep_kernel(where, out_m, up_m, down_m, out_s, up_s, down_s, p2, p3):
    def build(core):
        pairs_of = lambda m, s: (m, s) if core == 0 else (s, m)

        def rows(m, s, at, width):
            both = [v[:, at : at + width].astype(FULL) for v in pairs_of(m, s)]
            return jnp.concatenate(both, axis=0).astype(LOW)

        p2[:, 0:1536] = rows(up_m, up_s, core * 1536, 1536)
        p2[:, 1536:1920] = rows(out_m, out_s, core * 384, 384)
        for k, down in enumerate(pairs_of(down_m, down_s)):
            p3[k * 96 : k * 96 + 96, :] = down[:, core * 384 : core * 384 + 384]

    for core in range(2):
        pl.when(where[3] == core)(functools.partial(build, core))


def prep(where, mine, theirs):
    return pl.pallas_call(
        prep_kernel,
        out_shape=[jax.ShapeDtypeStruct((48, 1920), LOW), jax.ShapeDtypeStruct((192, 384), LOW)],
        in_specs=[SMEM] + [pl.BlockSpec(memory_space=pltpu.VMEM)] * 6,
        out_specs=[pl.BlockSpec(memory_space=pltpu.VMEM)] * 2,
        compiler_params=params(),
        cost_estimate=cost(1e6, 2e6),
        name="prep",
    )(where, *mine, *theirs)


def chip_of(where, dz, dy, dx):
    return ((where[0] ^ dz) * 2 + (where[1] ^ dy)) * 2 + (where[2] ^ dx)


def load_pack(where, pieces, start):
    for side in range(2):
        owner = where[3] ^ side
        col, along_x, along_y, far0, far1 = pieces[side * 5 : side * 5 + 5]
        for dz in range(4):
            far = far0.at[dz] if dz < 2 else far1.at[dz - 2]
            for dy, dx, source in ((0, 0, col.at[dz]), (0, 1, along_x.at[dz]), (1, 0, along_y.at[dz]), (1, 1, far)):
                start(source, chip_of(where, dz, dy, dx), owner)


def wait_pack(target, sem):
    pltpu.make_async_copy(target, target, sem).wait()


def normalise(values):
    centre = values - jnp.mean(values, axis=1, keepdims=True)
    spread = lax.rsqrt(jnp.mean(centre * centre, axis=1, keepdims=True) + 1e-6)
    return centre * spread, spread


def qkv_kernel(where, tok, *refs):
    pieces, (qkv, normed, w1, vec, bias_up, buf, weights, hats, sem) = refs[:10], refs[10:]
    half = pl.program_id(0)

    @pl.when(half == 0)
    def _():
        load_pack(
            where, pieces, lambda v, chip, core: pltpu.make_async_copy(v, buf.at[chip * 2 + core], sem).start()
        )
        for t in range(4):
            at = slice(t * 256, t * 256 + 256)
            hats[at, :], _ = normalise(tok[at, :].astype(FULL))
        wait_pack(buf, sem)
        lines = jnp.concatenate([buf[d, :, 2304:2432].astype(FULL) for d in range(32)], axis=0)
        lines = jnp.transpose(lines)
        vec[...] = lines[0:16]
        for chip in range(16):
            for s in range(2):
                line = buf[chip * 2 + s, 0:8, 2304:2432].astype(FULL)[0:1]
                at = (chip * 2 + s) * 96
                bias_up[0:1, at : at + 96] = line[:, 16:112]
        for t in range(4):
            at = slice(t * 256, t * 256 + 256)
            normed[at, :] = (hats[at, :] * lines[0:1] + lines[1:2]).astype(LOW)

    def gather(h):
        for chip in range(16):
            rows = slice(chip * 48, chip * 48 + 48)
            for part in range(3):
                at = slice(part * 768 + h * 384, part * 768 + h * 384 + 384)
                both = [buf[chip * 2 + s, :, at].astype(FULL) for s in range(2)]
                weights[rows, part * 384 : part * 384 + 384] = jnp.concatenate(both, axis=0).astype(LOW)

    for h in range(2):
        pl.when(half == h)(functools.partial(gather, h))
    w1[0] = weights[...]
    at = pl.multiple_of(half * 384, 128)
    query_bias = vec[2:3, pl.ds(at, 384)]
    value_bias = vec[3:4, pl.ds(at, 384)]
    for t in range(4):
        at = slice(t * 256, t * 256 + 256)
        mixed = mul(normed[at, :], weights[...])
        qkv[0, at, 0:384] = (mixed[:, 0:384] + query_bias).astype(LOW) * 0.125
        qkv[0, at, 384:768] = mixed[:, 384:768].astype(LOW)
        qkv[0, at, 768:1152] = (mixed[:, 768:1152] + value_bias).astype(LOW)


def qkv_call(where, tokens, pieces):
    return pl.pallas_call(
        qkv_kernel,
        grid=(2,),
        out_shape=[
            jax.ShapeDtypeStruct((2, 1024, 1152), LOW),
            jax.ShapeDtypeStruct((1024, 768), LOW),
            jax.ShapeDtypeStruct((2, 768, 1152), LOW),
            jax.ShapeDtypeStruct((16, 768), FULL),
            jax.ShapeDtypeStruct((1, 3072), FULL),
        ],
        in_specs=[SMEM, whole((1024, 768))] + [ANY] * 10,
        out_specs=[
            pl.BlockSpec((1, 1024, 1152), lambda h: (h, 0, 0)),
            whole((1024, 768)),
            pl.BlockSpec((1, 768, 1152), lambda h: (h, 0, 0)),
            whole((16, 768)),
            whole((1, 3072)),
        ],
        scratch_shapes=[
            pltpu.VMEM((32, 24, 2432), LOW),
            pltpu.VMEM((768, 1152), LOW),
            pltpu.VMEM((1024, 768), FULL),
            pltpu.SemaphoreType.DMA,
        ],
        compiler_params=params(),
        cost_estimate=cost(2 * 1024 * 768 * 2304, 16e6, scale=0.1),
        name="qkv",
    )(where, tokens, *pieces)


def masked_pair(block):
    lane = lax.broadcasted_iota(jnp.int32, block.shape, 1)
    zero = jnp.zeros_like(block)
    return jnp.concatenate([jnp.where(lane < 64, block, zero), jnp.where(lane < 64, zero, block)], axis=0)


def unmask(both):
    return jnp.concatenate([both[0:64, 0:128], both[64:128, 128:256]], axis=0)


def attend_kernel(first, qkv, seg, pad, *refs):
    probs, att_t, bias, wide = refs[-4:]
    row = pl.program_id(0) + first
    seg_row, pad_row = seg[pl.ds(row, 1), :].astype(FULL), pad[pl.ds(row, 1), :].astype(FULL)
    seg_col = jnp.transpose(jnp.broadcast_to(seg_row, (128, 256)))
    pad_col = jnp.transpose(jnp.broadcast_to(pad_row, (128, 256)))
    for b in range(2):
        keys = slice(64 * b, 64 * b + 192)
        same = seg_col[keys] == jnp.broadcast_to(seg_row[:, 128 * b : 128 * b + 128], (192, 128))
        key_at = lax.broadcasted_iota(jnp.int32, (192, 128), 0) + 64 * b
        query_at = lax.broadcasted_iota(jnp.int32, (192, 128), 1) + 128 * b
        allowed = same & ((pad_col[keys] == 1.0) | (key_at == query_at))
        one = jnp.where(allowed, 0.0, -1e30)
        bias[b] = jnp.concatenate([one, one], axis=1)
    blocks = [(half, p, b) for half in range(2) for p in range(3) for b in range(2)]
    for i, (half, p, b) in enumerate(blocks):
        stack = masked_pair(qkv[half, 128 * b : 128 * b + 128, p * 128 : p * 128 + 128])
        keys = slice(64 * b, 64 * b + 192)
        wide[i] = mul_t(qkv[half, keys, 384 + p * 128 : 512 + p * 128], stack) + bias[b]
    for i, (half, p, b) in enumerate(blocks):
        scores = wide[i]
        power = jnp.exp(scores - jnp.max(scores, axis=0, keepdims=True))
        probs[0, p, half, b] = (power * (1.0 / jnp.sum(power, axis=0, keepdims=True))).astype(LOW)
    for half, p, b in blocks:
        keys = slice(64 * b, 64 * b + 192)
        both = t_mul(qkv[half, keys, 768 + p * 128 : 896 + p * 128], probs[0, p, half, b])
        at = half * 384 + p * 128
        att_t[at : at + 128, 128 * b : 128 * b + 128] = unmask(both).astype(LOW)


def attend_call(first, count, qkv, seg, pad, before):
    old = list(before or [])
    return pl.pallas_call(
        functools.partial(attend_kernel, first),
        grid=(count,),
        out_shape=[
            jax.ShapeDtypeStruct((4, 3, 2, 2, 192, 256), LOW),
            jax.ShapeDtypeStruct((768, 1024), LOW),
        ],
        in_specs=[pl.BlockSpec((2, 256, 1152), lambda r: (0, r + first, 0)), whole((4, 256)), whole((4, 256))]
        + [ANY] * len(old),
        out_specs=[
            pl.BlockSpec((1, 3, 2, 2, 192, 256), lambda r: (r + first, 0, 0, 0, 0, 0)),
            pl.BlockSpec((768, 256), lambda r: (0, r + first)),
        ],
        input_output_aliases={3: 0, 4: 1} if old else {},
        scratch_shapes=[pltpu.VMEM((2, 192, 256), FULL), pltpu.VMEM((12, 192, 256), FULL)],
        compiler_params=params(),
        cost_estimate=cost(count * 1.5e9, count * 3e6, 8e5, scale=0.1),
        name="attend%d" % first,
    )(qkv, seg, pad, *old)


GATE = math.sqrt(2.0 / math.pi)


def gate_pair(u):
    square = u * u
    factor = 0.5 + 0.5 * jnp.tanh(u * (GATE + GATE * 0.044715 * square))
    value = u * factor
    return value, factor + value * (1.0 - factor) * (2.0 * GATE + 6.0 * GATE * 0.044715 * square)


FEED_SCALE = 0.1
CHUNK = 512
TILE = 256
TILES = 1024 // TILE


def load_up(where, pieces, up, w_out, sem, sem_out):
    def start(block, chip, core):
        rows = pl.ds(pl.multiple_of(chip * 48, 16), 48)
        for source, target, width, sem_of in (
            (slice(1536, 1920), w_out, 384, sem_out), (slice(0, 1536), up, 1536, sem)):
            columns = pl.ds(pl.multiple_of(core * width, 128), width)
            pltpu.make_async_copy(block.at[:, source], target.at[rows, columns], sem_of).start()

    load_pack(where, pieces, start)


def back_norm(grad, xhat, spread, gain):
    scaled = grad * gain
    flat = jnp.mean(scaled, axis=1, keepdims=True)
    tilt = jnp.mean(scaled * xhat, axis=1, keepdims=True)
    return (scaled - flat - xhat * tilt) * spread


def add_rows(target, row, values, step):
    value = jnp.sum(values, axis=0, keepdims=True)
    target[row : row + 1, :] = jnp.where(step == 0, value, target[row : row + 1, :] + value)


def feed_tile(step, att_t, tok, cot, bias, vec, weights, kept, outs, before):
    up, down, w_out = weights
    normed, act, hid = kept
    output, middle_grad, branch_grad, att_grad, sums, bias_grad = outs
    here = pl.ds(pl.multiple_of(step * TILE, TILE), TILE)
    before(0)
    mid = tok[...].astype(FULL) + t_mul(att_t[...], w_out[...]) + vec[4:5, :]
    xhat, spread = normalise(mid)
    rows = (xhat * vec[5:6, :] + vec[6:7, :]).astype(LOW)
    normed[here, :] = rows
    outer = cot[here, :]
    before(1)
    chunks = [slice(k * CHUNK, k * CHUNK + CHUNK) for k in range(3072 // CHUNK)]
    hidden = mul(rows, up[:, chunks[0]])
    for k, at in enumerate(chunks):
        following = mul(rows, up[:, chunks[k + 1]]) if k + 1 < len(chunks) else None
        if k == 0:
            before(2)
        active_grad = mul_t(outer, down[at, :])
        value, tilt = gate_pair(hidden + bias[:, at])
        act[here, at] = value.astype(LOW)
        grad = (tilt * active_grad).astype(LOW)
        hid[here, at] = grad
        line = jnp.sum(grad.astype(FULL), axis=0, keepdims=True)
        bias_grad[:, at] = jnp.where(step == 0, line, bias_grad[:, at] + line)
        hidden = following

    output[...] = (mid + vec[7:8, :] + mul(act[here, :], down[...])).astype(LOW)
    grad = mul_t(hid[here, :], up[...])
    outer = outer.astype(FULL)
    mid_grad = outer + back_norm(grad, xhat, spread, vec[5:6, :])
    middle_grad[...] = mid_grad
    low = mid_grad.astype(LOW)
    branch_grad[...] = low
    add_rows(sums, 0, grad * xhat, step)
    add_rows(sums, 1, grad, step)
    add_rows(sums, 2, low.astype(FULL), step)
    add_rows(sums, 3, outer, step)
    att_grad[...] = mul_t(low, w_out[...]).astype(LOW)


def feed_kernel(where, att_t, tok, cot, bias, vec, *refs):
    pieces, pieces_down = refs[:10], refs[10:20]
    outs = refs[20:26]
    down_packs, up_packs = refs[26:28], refs[28:30]
    up, down, w_out, normed, act, hid, sems = refs[30:]
    step = pl.program_id(0)
    core = where[3]

    def before(stage):
        @pl.when(step == 0)
        def _():
            if stage == 0:
                load_up(where, pieces, up, w_out, sems.at[1], sems.at[0])

                def start(block, chip, owner):
                    rows = pl.ds(pl.multiple_of(chip * 192, 16), 192)
                    columns = pl.ds(pl.multiple_of(owner * 384, 128), 384)
                    pltpu.make_async_copy(block, down.at[rows, columns], sems.at[2]).start()

                load_pack(where, pieces_down, start)
            target = (w_out, up, down)[stage]
            wait_pack(target, sems.at[stage])

    @pl.when(step < TILES)
    def _():
        feed_tile(step, att_t, tok, cot, bias, vec, (up, down, w_out), (normed, act, hid), outs, before)

    @pl.when(step >= TILES)
    def _():
        pair = step - TILES
        at = pl.multiple_of(pair * 1536, 1536)
        grad_down = t_mul(act[:, pl.ds(at, 1536)], cot[...]).astype(LOW)
        at = pl.multiple_of(pair * 384, 384)
        grad_up = t_mul(normed[:, pl.ds(at, 384)], hid[...])

        def put(side):
            for o in range(2):
                for k in range(8):
                    spot = ((k // 2 % 2) ^ where[1], (k % 2) ^ where[2], (k // 4) ^ (where[0] % 2))
                    at = k * 192 + o * 96
                    for h in range(2):
                        down_packs[o ^ side][spot + (slice(h * 96, h * 96 + 96),)] = grad_down[
                            at : at + 96, h * 384 : h * 384 + 384
                        ]
                    rows = grad_up[k * 48 + o * 24 : k * 48 + o * 24 + 24]
                    for j in range(4):
                        both = [rows[:, i * 384 : i * 384 + 384] for i in (2 * j, 2 * j + 1)]
                        up_packs[o ^ side][spot + (slice(j * 48, j * 48 + 48),)] = jnp.concatenate(
                            both, axis=0
                        ).astype(LOW)

        for side in range(2):
            pl.when(core == side)(functools.partial(put, side))


def feed_call(where, att_t, tokens, cot, bias_up, vec, pieces, pieces_down):
    tile = lambda step: jnp.minimum(step, TILES - 1)
    rows = pl.BlockSpec((TILE, 768), lambda s, where: (tile(s), 0))
    fixed = lambda shape: pl.BlockSpec(shape, lambda s, where: (0,) * len(shape), pipeline_mode=pl.Buffered(1))
    pack = (2, 2, 4, 192, 384)
    pack_block = pl.BlockSpec(
        (2, 2, 2, 192, 384), lambda s, where: (0, 0, jnp.clip(s - TILES, 0, 1) ^ (where[0] // 2), 0, 0))
    return pl.pallas_call(
        feed_kernel,
        grid_spec=pltpu.PrefetchScalarGridSpec(
            num_scalar_prefetch=1,
            grid=(TILES + 2,),
            in_specs=[
                pl.BlockSpec((768, TILE), lambda s, where: (0, tile(s))), rows, fixed((1024, 768)),
                fixed((1, 3072)), fixed((16, 768)),
            ] + [ANY] * 20,
            out_specs=[
                rows, rows, rows, rows, fixed((8, 768)), fixed((1, 3072)), *([pack_block] * 4),
            ],
            scratch_shapes=[
                pltpu.VMEM((768, 3072), LOW),
                pltpu.VMEM((3072, 768), LOW),
                pltpu.VMEM((768, 768), LOW),
                pltpu.VMEM((1024, 768), LOW),
                pltpu.VMEM((1024, 3072), LOW),
                pltpu.VMEM((1024, 3072), LOW),
                pltpu.SemaphoreType.DMA((3,)),
            ],
        ),
        out_shape=[
            jax.ShapeDtypeStruct((1024, 768), LOW),
            jax.ShapeDtypeStruct((1024, 768), FULL),
            jax.ShapeDtypeStruct((1024, 768), LOW),
            jax.ShapeDtypeStruct((1024, 768), LOW),
            jax.ShapeDtypeStruct((8, 768), FULL),
            jax.ShapeDtypeStruct((1, 3072), FULL),
        ] + [jax.ShapeDtypeStruct(pack, LOW)] * 4,
        compiler_params=params(),
        cost_estimate=cost(26 * 1024 * 768 * 768 * 2, 35e6, 3e6, scale=FEED_SCALE),
        name="feed",
    )(where, att_t, tokens, cot, bias_up, vec, *pieces, *pieces_down)


ROWS_STEP = 2


def unattend_kernel(groups, with_out, where, *refs):
    count = len(groups)
    parts = [refs[5 * g : 5 * g + 5] for g in range(count)]
    refs = refs[5 * count + (0 if with_out else 2) :]
    probs, normed = refs[:count], refs[count]
    refs = refs[count + 1 :]
    if with_out:
        att_t, branch_grad, refs = refs[0], refs[1], refs[2:]
        mixed, mine, theirs, sums, acc, wide, slim, stacks, out_acc = refs
    else:
        mixed, mine, theirs, sums, acc, wide, slim, stacks = refs
    step = pl.program_id(0)
    width = 128 * count
    blocks = [(r, g, h) for r in range(ROWS_STEP) for g in range(count) for h in range(2)]

    def keys_of(r, b):
        return slice(256 * r + 64 * b, 256 * r + 64 * b + 192)

    def queries_of(r, b):
        return slice(256 * r + 128 * b, 256 * r + 128 * b + 128)

    for i, (r, g, half) in enumerate(blocks):
        query, key, value = parts[g][:3]
        grads = parts[g][3 + half]
        for b in range(2):
            stacks[0, 2 * i + b] = masked_pair(query[half, queries_of(r, b), :])
            stack = masked_pair(grads[queries_of(r, b), :])
            stacks[1, 2 * i + b] = stack
            wide[2 * i + b] = mul_t(value[half, keys_of(r, b), :], stack)
    for i, (r, g, half) in enumerate(blocks):
        for b in range(2):
            weights = probs[g][r, 0, half, b].astype(FULL)
            prob_grad = wide[2 * i + b]
            inner = jnp.sum(prob_grad * weights, axis=0, keepdims=True)
            slim[2 * i + b] = (weights * (prob_grad - inner)).astype(LOW)

    def merge(first, second):
        return jnp.concatenate([first[0:64], first[64:192] + second[0:128], second[128:192]], axis=0)

    for i, (r, g, half) in enumerate(blocks):
        key = parts[g][1]
        rows = slice(256 * r, 256 * r + 256)
        value_grad = [mul(probs[g][r, 0, half, b], stacks[1, 2 * i + b]) for b in range(2)]
        key_grad = [mul(slim[2 * i + b], stacks[0, 2 * i + b]) for b in range(2)]
        turned = [unmask(t_mul(key[half, keys_of(r, b), :], slim[2 * i + b])) for b in range(2)]
        query_grad = jnp.transpose(jnp.concatenate(turned, axis=1)) * 0.125
        at = g * 128
        mixed[half, rows, at : at + 128] = query_grad.astype(LOW)
        mixed[half, rows, width + at : width + at + 128] = merge(*key_grad).astype(LOW)
        mixed[half, rows, 2 * width + at : 2 * width + at + 128] = merge(*value_grad).astype(LOW)

    def add(target, more):
        @pl.when(step == 0)
        def _():
            target[...] = more

        @pl.when(step > 0)
        def _():
            target[...] += more

    for half in range(2):
        add_rows(sums.at[half], 0, mixed[half].astype(FULL), step)
        add(acc.at[half], t_mul(normed[...], mixed[half]))
    if with_out:
        add(out_acc, mul(att_t[...], branch_grad[...]))

    def write(side):
        for owner in range(2):
            dest = mine if owner == side else theirs
            for chip in range(16):
                rows = slice(chip * 48 + owner * 24, chip * 48 + owner * 24 + 24)
                spot = ((chip // 2 % 2) ^ where[1], (chip % 2) ^ where[2], (chip // 4) ^ where[0], slice(None))
                if with_out:
                    lines = [out_acc[rows, :], jnp.concatenate([acc[0, rows, :], acc[1, rows, :]], axis=1)]
                else:
                    lines = [acc[0, rows, :], acc[1, rows, :]]
                dest[spot + (slice(0, 768),)] = jnp.concatenate(lines, axis=0).astype(LOW)

    for side in range(2):
        pl.when((step == 4 // ROWS_STEP - 1) & (where[3] == side))(functools.partial(write, side))


def unattend_call(groups, where, qkv, att_grad, probs, normed, packs=None, att_t=None, branch_grad=None):
    with_out = att_t is not None
    count = len(groups)
    width = 384 * count
    tall = 256 * ROWS_STEP
    operands, specs = [], []
    for p in groups:
        for part in range(3):
            operands.append(qkv)
            specs.append(pl.BlockSpec((2, tall, 128), lambda r, c=part * 3 + p: (0, r, c)))
        for half in range(2):
            operands.append(att_grad)
            specs.append(pl.BlockSpec((tall, 128), lambda r, c=half * 3 + p: (r, c)))
    if not with_out:
        operands += list(packs)
        specs += [ANY, ANY]
    for p in groups:
        operands.append(probs)
        specs.append(pl.BlockSpec((ROWS_STEP, 1, 2, 2, 192, 256), lambda r, p=p: (r, p, 0, 0, 0, 0)))
    operands.append(normed)
    specs.append(pl.BlockSpec((tall, 768), lambda r: (r, 0)))
    if with_out:
        operands += [att_t, branch_grad]
        specs += [pl.BlockSpec((768, tall), lambda r: (0, r)), pl.BlockSpec((tall, 768), lambda r: (r, 0))]
    shape = (2, 2, 4, 48, 1536)
    lanes = 0 if with_out else 1
    part_of = pl.BlockSpec((2, 2, 4, 48, 768), lambda r: (0, 0, 0, 0, lanes), pipeline_mode=pl.Buffered(1))
    many = 4 * count * ROWS_STEP
    return pl.pallas_call(
        functools.partial(unattend_kernel, groups, with_out),
        grid=(4 // ROWS_STEP,),
        out_shape=[
            jax.ShapeDtypeStruct((2, 1024, width), LOW),
            jax.ShapeDtypeStruct(shape, LOW),
            jax.ShapeDtypeStruct(shape, LOW),
            jax.ShapeDtypeStruct((2, 8, width), FULL),
        ],
        in_specs=[SMEM] + specs,
        out_specs=[
            pl.BlockSpec((2, tall, width), lambda r: (0, r, 0)),
            part_of,
            part_of,
            whole((2, 8, width)),
        ],
        input_output_aliases={} if with_out else {1 + 5 * count + k: 1 + k for k in range(2)},
        scratch_shapes=[
            pltpu.VMEM((2, 768, width), FULL),
            pltpu.VMEM((many, 192, 256), FULL),
            pltpu.VMEM((many, 192, 256), LOW),
            pltpu.VMEM((2, many, 256, 128), LOW),
        ] + ([pltpu.VMEM((768, 768), FULL)] if with_out else []),
        compiler_params=params(),
        cost_estimate=cost(count * 2.5e9, count * 8e6),
        name="unattend%d" % groups[0],
    )(where, *operands)


def tokens_kernel(m0, m1, w1, tok, vec, middle_grad, sums, sums0, sums1, bias, grad, lines):
    step = pl.program_id(0)
    total = None
    for half in range(2):
        joined = []
        for part in range(3):
            joined.append(m0[half, :, part * 128 : part * 128 + 128])
            joined.append(m1[half, :, part * 256 : part * 256 + 256])
        more = mul_t(jnp.concatenate(joined, axis=1), w1[half])
        total = more if total is None else total + more
    xhat, spread = normalise(tok[...].astype(FULL))
    grad[...] = middle_grad[...] + back_norm(total, xhat, spread, vec[0:1, :])
    add_rows(lines, 0, total * xhat, step)
    add_rows(lines, 1, total, step)

    @pl.when(step == 3)
    def _():
        for half in range(2):
            at = half * 384
            for row, part in ((2, 0), (3, 2)):
                lines[row : row + 1, at : at + 128] = sums0[half, 0:1, part * 128 : part * 128 + 128]
                lines[row : row + 1, at + 128 : at + 384] = sums1[half, 0:1, part * 256 : part * 256 + 256]
        lines[4:5, :] = sums[2:3, :]
        lines[5:6, :] = sums[0:1, :]
        lines[6:7, :] = sums[1:2, :]
        lines[7:8, :] = sums[3:4, :]
        for k in range(4):
            lines[8 + k : 9 + k, :] = bias[0:1, k * 768 : k * 768 + 768]
        lines[12:16, :] = jnp.zeros((4, 768), FULL)


def tokens_call(mixed0, mixed1, w1, tokens, vec, middle_grad, sums, sums0, sums1, bias):
    rows = pl.BlockSpec((256, 768), lambda r: (r, 0))
    return pl.pallas_call(
        tokens_kernel,
        grid=(4,),
        out_shape=[jax.ShapeDtypeStruct((1024, 768), FULL), jax.ShapeDtypeStruct((16, 768), FULL)],
        in_specs=[pl.BlockSpec((2, 256, w), lambda r: (0, r, 0)) for w in (384, 768)] + [
            whole((2, 768, 1152)), rows, whole((16, 768)), rows, whole((8, 768)), whole((2, 8, 384)),
            whole((2, 8, 768)), whole((1, 3072)),
        ],
        out_specs=[rows, whole((16, 768))],
        compiler_params=params(),
        cost_estimate=cost(2 * 1024 * 768 * 2304, 16e6),
        name="tokens",
    )(mixed0, mixed1, w1, tokens, vec, middle_grad, sums, sums0, sums1, bias)


def after(value, *before):
    return lax.optimization_barrier((value, before))[0]


class Total:
    def __init__(self, mine, theirs):
        self.mine = mine
        self.block = mine.shape[3:]
        self.got = send(theirs, SWAP_C)

    def spec(self, size, place_of):
        return pl.BlockSpec(size + self.block, lambda i: place_of(i) + (0, 0))

    def low(self, *lead):
        return jax.ShapeDtypeStruct(lead + self.block, LOW)

    def first(self):
        def body(mine_x, got_x, mine_y, got_y, out_x, out_y):
            out_x[...] = (mine_x[...].astype(FULL) + got_x[...].astype(FULL)).reshape(out_x.shape).astype(LOW)
            out_y[...] = (mine_y[...].astype(FULL) + got_y[...].astype(FULL)).reshape(out_y.shape).astype(LOW)

        to_x = self.spec((1, 1, 2), lambda i: (i, 1, 0))
        to_y = self.spec((1, 1, 2), lambda i: (1, i, 1))
        out = self.spec((1, 2), lambda i: (i, 0))

        def keep(one_x, one_y):
            self.one_x, self.one_y = send(one_x, SWAP_X), send(one_y, SWAP_Y)

        return (body, [self.mine, self.got] * 2, [to_x, to_x, to_y, to_y], [self.low(2, 2)] * 2, [out] * 2, keep)

    def second(self):
        def body(mine_y, got_y, one_x, mine_x, got_x, one_y, out_y, out_x):
            add = lambda *refs: sum(r[...].astype(FULL).reshape(out_y.shape) for r in refs)
            out_y[...] = add(mine_y, got_y, one_x).astype(LOW)
            out_x[...] = add(mine_x, got_x, one_y).astype(LOW)

        to_y = self.spec((1, 1, 1), lambda i: (1, 0, i))
        to_x = self.spec((1, 1, 1), lambda i: (0, 1, 2 + i))
        came = self.spec((1, 1), lambda i: (1, i))
        out = self.spec((1,), lambda i: (i,))

        def keep(two_y, two_x):
            self.two_y, self.two_x = send(two_y, SWAP_Y), send(two_x, SWAP_X)

        operands = [self.mine, self.got, self.one_x, self.mine, self.got, self.one_y]
        return (body, operands, [to_y, to_y, came, to_x, to_x, came], [self.low(2)] * 2, [out] * 2, keep)

    def third(self):
        def body(mine, got, one_x, two_y, one_y, two_x, *outs):
            @pl.when(pl.program_id(0) == 0)
            def _():
                for k, target in enumerate(outs):
                    extra = (one_x[0, k], two_y[k]) if k < 2 else (one_y[0, k - 2], two_x[k - 2])
                    total = mine[0, 0, k].astype(FULL) + got[0, 0, k].astype(FULL)
                    total = total + extra[0].astype(FULL) + extra[1].astype(FULL)
                    target[...] = total.astype(target.dtype)

        near = self.spec((1, 1, 4), lambda i: (0, 0, 0))
        came = self.spec((1, 2), lambda i: (0, 0))
        two = self.spec((2,), lambda i: (0,))
        one = pl.BlockSpec(self.block, lambda i: (0, 0))
        out = [jax.ShapeDtypeStruct(self.block, FULL)] + [self.low()] * 3

        def keep(own, *three):
            self.own = own
            self.parts = [send(v, SWAP_Z[k + 1]) for k, v in enumerate(three)]

        operands = [self.mine, self.got, self.one_x, self.two_y, self.one_y, self.two_x]
        return (body, operands, [near, near, came, two, came, two], out, [one] * 4, keep)

    def last(self, write, shapes, more=()):
        def body(own, part1, part2, part3, *refs):
            @pl.when(pl.program_id(0) == 0)
            def _():
                total = own[...] + part1[...].astype(FULL) + part2[...].astype(FULL) + part3[...].astype(FULL)
                write(total, *refs)

        block = pl.BlockSpec(self.block, lambda i: (0, 0))
        same = lambda shape: pl.BlockSpec(shape, lambda i: (0,) * len(shape))

        def keep(*given):
            self.final = given

        return (
            body, [self.own, *self.parts, *more], [block] * 4 + [same(v.shape) for v in more],
            [jax.ShapeDtypeStruct(v, FULL) for v in shapes], [same(v) for v in shapes], keep,
        )


def write_down(total, share):
    share[...] = jnp.concatenate([total[0:96], total[96:192]], axis=1)


def write_up(total, share):
    share[...] = jnp.concatenate([total[j * 24 : j * 24 + 24] for j in range(8)], axis=1)


def write_head(total, share_out, share):
    share_out[...] = total[0:24, 0:768]
    for half in range(2):
        for part in range(3):
            at = part * 768 + half * 384
            first = half * 384 + part * 128
            share[:, at : at + 128] = total[24:48, first : first + 128]
            rest = 768 + part * 256
            share[:, at + 128 : at + 384] = total[half * 24 : half * 24 + 24, rest : rest + 256]


def run_stages(stages, *before):
    ins = [len(s[1]) for s in stages]
    outs = [len(s[3]) for s in stages]

    def kernel(*refs):
        at_in, at_out = 0, sum(ins)
        for stage, n_in, n_out in zip(stages, ins, outs):
            stage[0](*refs[at_in : at_in + n_in], *refs[at_out : at_out + n_out])
            at_in, at_out = at_in + n_in, at_out + n_out

    operands = after([v for s in stages for v in s[1]], *before)
    results = pl.pallas_call(
        kernel,
        grid=(2,),
        out_shape=[v for s in stages for v in s[3]],
        in_specs=[v for s in stages for v in s[2]],
        out_specs=[v for s in stages for v in s[4]],
        compiler_params=params(),
        cost_estimate=cost(1e6, 4e6),
        name="sums",
    )(*operands)
    at = 0
    for stage, n_out in zip(stages, outs):
        stage[5](*results[at : at + n_out])
        at += n_out
    return results


def halves_of(own, sibling, core):
    return jnp.where(core == 0, own, sibling), jnp.where(core == 0, sibling, own)


def on_device(
    tokens, segment_ids, pad_mask, w_qkv, w_out, w_up, w_down, gain_one, shift_one, bias_query,
    bias_value, bias_out, gain_two, shift_two, bias_up, bias_down, cotangent,
):
    z0, y0, x0, core = place()
    where = jnp.stack([z0, y0, x0, core]).astype(jnp.int32)
    row_count, length, width = tokens.shape
    total_rows = row_count * length
    flat = tokens.reshape(total_rows, width)
    cot = cotangent.reshape(total_rows, width)
    vectors = (gain_one, shift_one, bias_query, bias_value, bias_out, gain_two, shift_two, bias_down, bias_up)

    def along_z(own):
        return [send(own[None], SWAP_Z[k]) for k in (1, 2, 3)]

    def column(own, rest):
        return jnp.concatenate([own[None], *rest], axis=0)

    def plane(col):
        return send(col, SWAP_X), send(col, SWAP_Y)

    def corner(along_x, along_y):
        return send(along_x[0:2], SWAP_Y), send(along_y[2:4], SWAP_X)

    def across(blocks):
        return [send(v, SWAP_C) for v in blocks]

    p1 = first_call(w_qkv, vectors)
    rest1 = along_z(p1)
    mine = (w_out, w_up, w_down)
    p2, p3 = prep(where, after(mine, p1), across(mine))
    col1 = column(after(p1, p2), rest1)
    x1, y1 = plane(col1)
    rest2 = along_z(after(p2, col1))
    col2 = column(p2, rest2)
    far1 = corner(x1, y1)
    own1 = [col1, x1, y1]
    pack1 = own1 + list(far1) + across(own1) + across(far1)
    col2 = after(col2, far1)
    x2, y2 = plane(col2)
    rest3 = along_z(after(p3, col2))
    qkv, normed_one, w1, vec, up_line = qkv_call(where, after(flat, col2), pack1)
    col3 = column(after(p3, qkv), rest3)
    x3, y3 = plane(col3)
    held = attend_call(0, 2, after(qkv, col3), segment_ids, pad_mask, None)
    far2 = corner(x2, y2)
    other2 = across(after([col2, x2, y2], held))
    probs, att_t = attend_call(2, 2, after(qkv, x2, y2), segment_ids, pad_mask, held)
    pack2 = [col2, x2, y2, *far2] + other2 + across(after(far2, att_t))
    far3 = corner(after(x3, att_t), after(y3, att_t))
    own3 = [col3, x3, y3]
    pack3 = own3 + list(far3) + across(after(own3, att_t, other2)) + across(far3)
    output, middle_grad, branch_grad, att_grad, sums, bias_grad, *grads = feed_call(
        where, att_t, flat, cot, up_line, vec, pack2, pack3)

    sum_a, sum_b = Total(*grads[:2]), Total(*grads[2:])
    ready = run_stages([sum_a.first()])
    mixed0, mine, theirs, sums0 = unattend_call(
        (0,), where, qkv, after(att_grad, ready), probs, normed_one, None, att_t, branch_grad)
    ready = run_stages([sum_a.second(), sum_b.first()], mixed0)
    mixed1, mine, theirs, sums1 = unattend_call(
        (1, 2), where, qkv, after(att_grad, ready), probs, normed_one, (mine, theirs))
    head = Total(mine, theirs)
    ready = run_stages([sum_a.third(), sum_b.second()], mixed1)
    grad_tokens, lines = tokens_call(
        mixed0, after(mixed1, ready), w1, flat, vec, middle_grad, sums, sums0, sums1, bias_grad)
    ready = run_stages([sum_b.third(), head.first(), sum_a.last(write_down, [(96, 768)])], grad_tokens)
    lines = after(lines, ready)
    got = send(lines, SWAP_C)
    ready = run_stages([head.second(), sum_b.last(write_up, [(24, 3072)])], ready)
    lines = after(lines, ready) + got
    got = [send(lines, move) for move in (SWAP_X, SWAP_Y, SWAP_D)]
    ready = run_stages([head.third()], ready)
    lines = after(lines, ready) + got[0] + (got[1] + got[2])
    got = [send(lines, move) for move in SWAP_Z[1:]]
    run_stages([head.last(write_head, [(24, 768), (24, 2304)])], ready)
    lines = lines + got[0] + (got[1] + got[2])
    share_out, share_qkv = head.final
    share_up, share_down = sum_b.final[0], sum_a.final[0]

    device = ((z0 * 2 + y0) * 2 + x0) * 2 + core
    own = lax.dynamic_slice(lines, (0, device * 24), (8, 24))
    own_up = lax.dynamic_slice(lines, (8 + device // 8, device % 8 * 96), (1, 96))[0]
    return (
        output.reshape(row_count, length, width),
        grad_tokens.reshape(row_count, length, width),
        share_qkv, share_out, share_up, share_down,
        own[0], own[1], own[2], own[3], own[4], own[5], own[6], own_up, own[7],
    )


def solution(mesh):
    fits = dict(mesh.shape) == {"gx": 8, "gy": 4}
    device = on_device if fits else generic_device
    names = AXES if fits else ("gx", "gy")
    if fits:
        mesh = Mesh(mesh.devices.reshape(4, 2, 2, 2), AXES)
    return jax.shard_map(
        device,
        mesh=mesh,
        in_specs=(
            P(names, None, None),
            P(names, None),
            P(names, None),
            P(names, None),
            P(names, None),
            P(names, None),
            P(names, None),
            P(names),
            P(names),
            P(names),
            P(names),
            P(names),
            P(names),
            P(names),
            P(names),
            P(names),
            P(names, None, None),
        ),
        out_specs=(
            P(names, None, None),
            P(names, None, None),
            P(names, None),
            P(names, None),
            P(names, None),
            P(names, None),
            P(names),
            P(names),
            P(names),
            P(names),
            P(names),
            P(names),
            P(names),
            P(names),
            P(names),
        ),
        check_vma=False,
    )
```

```python
import functools
import math

import jax
import jax.numpy as jnp
from jax import lax
from jax.experimental import pallas as pl
from jax.experimental.pallas import tpu as pltpu
from jax.sharding import Mesh
from jax.sharding import PartitionSpec as P

HEADS = 12
HDIM = 64


def layer_norm(values, gain, shift):
    centre = values - jnp.mean(values, axis=-1, keepdims=True)
    spread = jnp.mean(centre * centre, axis=-1, keepdims=True)
    return centre * lax.rsqrt(spread + 1e-06) * gain + shift


def smooth_gate(values):
    return jax.nn.gelu(values, approximate=True)


def attend_mask(segment_ids, pad_mask):
    length = segment_ids.shape[-1]
    positions = jnp.arange(length)
    same = segment_ids[:, :, None] == segment_ids[:, None, :]
    real = pad_mask[:, None, :] == 1
    itself = positions[:, None] == positions[None, :]
    return same & (real | itself[None])


def outer_sum(left, right):
    return lax.dot_general(
        left, right, (((0,), (0,)), ((), ())), preferred_element_type=jnp.float32
    )


def against(left, matrix):
    return lax.dot_general(
        left, matrix, (((1,), (1,)), ((), ())), preferred_element_type=jnp.float32
    )


def score_block(query_part, key_part, allowed):
    raw = jnp.einsum("rqhe,rkhe->rhqk", query_part, key_part, preferred_element_type=jnp.float32)
    raw = raw * (1.0 / math.sqrt(HDIM))
    return jnp.where(allowed[:, None], raw, -1e30)


def collect(
    w_qkv,
    w_out,
    w_up,
    w_down,
    gain_one,
    shift_one,
    bias_query,
    bias_value,
    bias_out,
    gain_two,
    shift_two,
    bias_up,
    bias_down,
):
    return (
        lax.all_gather(w_qkv, ("gx", "gy"), axis=0, tiled=True),
        lax.all_gather(w_out, ("gx", "gy"), axis=0, tiled=True),
        lax.all_gather(w_up, ("gx", "gy"), axis=0, tiled=True),
        lax.all_gather(w_down, ("gx", "gy"), axis=0, tiled=True),
        lax.all_gather(gain_one, ("gx", "gy"), axis=0, tiled=True),
        lax.all_gather(shift_one, ("gx", "gy"), axis=0, tiled=True),
        lax.all_gather(bias_query, ("gx", "gy"), axis=0, tiled=True),
        lax.all_gather(bias_value, ("gx", "gy"), axis=0, tiled=True),
        lax.all_gather(bias_out, ("gx", "gy"), axis=0, tiled=True),
        lax.all_gather(gain_two, ("gx", "gy"), axis=0, tiled=True),
        lax.all_gather(shift_two, ("gx", "gy"), axis=0, tiled=True),
        lax.all_gather(bias_up, ("gx", "gy"), axis=0, tiled=True),
        lax.all_gather(bias_down, ("gx", "gy"), axis=0, tiled=True),
    )


def generic_device(
    tokens,
    segment_ids,
    pad_mask,
    w_qkv,
    w_out,
    w_up,
    w_down,
    gain_one,
    shift_one,
    bias_query,
    bias_value,
    bias_out,
    gain_two,
    shift_two,
    bias_up,
    bias_down,
    cotangent,
):
    row_count, length, width = tokens.shape
    total_rows = row_count * length
    gathered = collect(
        w_qkv,
        w_out,
        w_up,
        w_down,
        gain_one,
        shift_one,
        bias_query,
        bias_value,
        bias_out,
        gain_two,
        shift_two,
        bias_up,
        bias_down,
    )
    full_qkv, full_out, full_up, full_down = (gathered[0], gathered[1], gathered[2], gathered[3])
    gain_first = gathered[4].astype(jnp.float32)
    shift_first = gathered[5].astype(jnp.float32)
    query_bias = gathered[6].astype(jnp.float32)
    value_bias = gathered[7].astype(jnp.float32)
    out_bias = gathered[8].astype(jnp.float32)
    gain_second = gathered[9].astype(jnp.float32)
    shift_second = gathered[10].astype(jnp.float32)
    up_bias = gathered[11].astype(jnp.float32)
    down_bias = gathered[12].astype(jnp.float32)
    allowed = attend_mask(segment_ids, pad_mask)
    inputs = tokens.astype(jnp.float32).reshape(total_rows, width)
    first_norm, first_pull = jax.vjp(layer_norm, inputs, gain_first, shift_first)
    normed = first_norm.astype(jnp.bfloat16)
    mixed = jnp.dot(normed, full_qkv, preferred_element_type=jnp.float32)
    query_part = (
        (mixed[:, :width] + query_bias).astype(jnp.bfloat16).reshape(row_count, length, HEADS, HDIM)
    )
    key_part = (
        mixed[:, width : 2 * width].astype(jnp.bfloat16).reshape(row_count, length, HEADS, HDIM)
    )
    value_part = (
        (mixed[:, 2 * width :] + value_bias)
        .astype(jnp.bfloat16)
        .reshape(row_count, length, HEADS, HDIM)
    )
    scores = score_block(query_part, key_part, allowed)
    highest = jnp.max(scores, axis=-1, keepdims=True)
    log_total = highest + jnp.log(jnp.sum(jnp.exp(scores - highest), axis=-1, keepdims=True))
    weights = jnp.exp(scores - log_total).astype(jnp.bfloat16)
    attended = jnp.einsum(
        "rhqk,rkhe->rqhe", weights, value_part, preferred_element_type=jnp.float32
    )
    attended = attended.reshape(total_rows, width).astype(jnp.bfloat16)
    middle = inputs + jnp.dot(attended, full_out, preferred_element_type=jnp.float32) + out_bias
    second_norm, second_pull = jax.vjp(layer_norm, middle, gain_second, shift_second)
    normed_two = second_norm.astype(jnp.bfloat16)
    hidden = jnp.dot(normed_two, full_up, preferred_element_type=jnp.float32) + up_bias
    active, gate_pull = jax.vjp(smooth_gate, hidden)
    active_low = active.astype(jnp.bfloat16)
    result = middle + jnp.dot(active_low, full_down, preferred_element_type=jnp.float32) + down_bias
    output = result.astype(jnp.bfloat16).reshape(row_count, length, width)
    again = collect(
        w_qkv,
        w_out,
        w_up,
        w_down,
        gain_one,
        shift_one,
        bias_query,
        bias_value,
        bias_out,
        gain_two,
        shift_two,
        bias_up,
        bias_down,
    )
    full_qkv, full_out, full_up, full_down = (again[0], again[1], again[2], again[3])
    down_in = cotangent.reshape(total_rows, width)
    outer_grad = down_in.astype(jnp.float32)
    grad_bias_down = jnp.sum(outer_grad, axis=0)
    grad_w_down = outer_sum(active_low, down_in)
    active_grad = against(down_in, full_down)
    hidden_grad = gate_pull(active_grad)[0].astype(jnp.bfloat16)
    grad_bias_up = jnp.sum(hidden_grad.astype(jnp.float32), axis=0)
    grad_w_up = outer_sum(normed_two, hidden_grad)
    norm_two_grad = against(hidden_grad, full_up)
    middle_part, grad_gain_two, grad_shift_two = second_pull(norm_two_grad)
    middle_grad = outer_grad + middle_part
    branch_grad = middle_grad.astype(jnp.bfloat16)
    grad_bias_out = jnp.sum(branch_grad.astype(jnp.float32), axis=0)
    grad_w_out = outer_sum(attended, branch_grad)
    attended_grad = (
        against(branch_grad, full_out).astype(jnp.bfloat16).reshape(row_count, length, HEADS, HDIM)
    )
    probs = jnp.exp(score_block(query_part, key_part, allowed) - log_total)
    probs_low = probs.astype(jnp.bfloat16)
    value_grad = jnp.einsum(
        "rhqk,rqhe->rkhe", probs_low, attended_grad, preferred_element_type=jnp.float32
    ).astype(jnp.bfloat16)
    prob_grad = jnp.einsum(
        "rqhe,rkhe->rhqk", attended_grad, value_part, preferred_element_type=jnp.float32
    )
    inner_term = jnp.sum(prob_grad * probs, axis=-1, keepdims=True)
    score_grad = (probs * (prob_grad - inner_term)).astype(jnp.bfloat16)
    score_scale = 1.0 / math.sqrt(HDIM)
    query_grad = (
        (
            jnp.einsum("rhqk,rkhe->rqhe", score_grad, key_part, preferred_element_type=jnp.float32)
            * score_scale
        )
        .astype(jnp.bfloat16)
        .reshape(total_rows, width)
    )
    key_grad = (
        (
            jnp.einsum(
                "rhqk,rqhe->rkhe", score_grad, query_part, preferred_element_type=jnp.float32
            )
            * score_scale
        )
        .astype(jnp.bfloat16)
        .reshape(total_rows, width)
    )
    value_flat = value_grad.reshape(total_rows, width)
    mixed_grad = jnp.concatenate([query_grad, key_grad, value_flat], axis=1)
    grad_bias_query = jnp.sum(query_grad.astype(jnp.float32), axis=0)
    grad_bias_value = jnp.sum(value_flat.astype(jnp.float32), axis=0)
    grad_w_qkv = outer_sum(normed, mixed_grad)
    norm_one_grad = against(mixed_grad, full_qkv)
    input_part, grad_gain_one, grad_shift_one = first_pull(norm_one_grad)
    grad_tokens = (middle_grad + input_part).reshape(row_count, length, width)
    shares = (
        lax.psum_scatter(grad_w_qkv, ("gx", "gy"), scatter_dimension=0, tiled=True),
        lax.psum_scatter(grad_w_out, ("gx", "gy"), scatter_dimension=0, tiled=True),
        lax.psum_scatter(grad_w_up, ("gx", "gy"), scatter_dimension=0, tiled=True),
        lax.psum_scatter(grad_w_down, ("gx", "gy"), scatter_dimension=0, tiled=True),
        lax.psum_scatter(grad_gain_one, ("gx", "gy"), scatter_dimension=0, tiled=True),
        lax.psum_scatter(grad_shift_one, ("gx", "gy"), scatter_dimension=0, tiled=True),
        lax.psum_scatter(grad_bias_query, ("gx", "gy"), scatter_dimension=0, tiled=True),
        lax.psum_scatter(grad_bias_value, ("gx", "gy"), scatter_dimension=0, tiled=True),
        lax.psum_scatter(grad_bias_out, ("gx", "gy"), scatter_dimension=0, tiled=True),
        lax.psum_scatter(grad_gain_two, ("gx", "gy"), scatter_dimension=0, tiled=True),
        lax.psum_scatter(grad_shift_two, ("gx", "gy"), scatter_dimension=0, tiled=True),
        lax.psum_scatter(grad_bias_up, ("gx", "gy"), scatter_dimension=0, tiled=True),
        lax.psum_scatter(grad_bias_down, ("gx", "gy"), scatter_dimension=0, tiled=True),
    )
    return (
        output,
        grad_tokens,
        shares[0],
        shares[1],
        shares[2],
        shares[3],
        shares[4],
        shares[5],
        shares[6],
        shares[7],
        shares[8],
        shares[9],
        shares[10],
        shares[11],
        shares[12],
    )


CHIPS = ("z", "y", "x")
AXES = CHIPS + ("core",)


def pairs(move):
    out = []
    for d in range(32):
        z, y, x, c = d // 8, (d // 4) % 2, (d // 2) % 2, d % 2
        z, y, x, c = move(z, y, x, c)
        out.append((d, ((z * 2 + y) * 2 + x) * 2 + c))
    return out


SWAP_C = pairs(lambda z, y, x, c: (z, y, x, 1 - c))
SWAP_X = pairs(lambda z, y, x, c: (z, y, 1 - x, c))
SWAP_Y = pairs(lambda z, y, x, c: (z, 1 - y, x, c))
SWAP_D = pairs(lambda z, y, x, c: (z, 1 - y, 1 - x, c))
SWAP_Z = [None] + [pairs(lambda z, y, x, c, k=k: (z ^ k, y, x, c)) for k in (1, 2, 3)]


def send(values, perm):
    return lax.ppermute(values, AXES, perm)


def place():
    return tuple(lax.axis_index(name) for name in AXES)


LOW = jnp.bfloat16
FULL = jnp.float32
ANY = pl.BlockSpec(memory_space=pl.ANY)
SMEM = pl.BlockSpec(memory_space=pltpu.SMEM)
MIB = 1024 * 1024


def whole(shape):
    zeros = (0,) * len(shape)
    return pl.BlockSpec(shape, lambda *_: zeros, pipeline_mode=pl.Buffered(1))


def params(limit=64):
    return pltpu.CompilerParams(vmem_limit_bytes=limit * MIB)


def cost(flops, read, exps=0, scale=10.0):
    return pl.CostEstimate(
        flops=int(scale * flops), bytes_accessed=int(scale * read), transcendentals=int(scale * exps)
    )


def mul(left, right):
    return lax.dot_general(left, right, (((1,), (0,)), ((), ())), preferred_element_type=FULL)


def mul_t(left, right):
    return lax.dot_general(left, right, (((1,), (1,)), ((), ())), preferred_element_type=FULL)


def t_mul(left, right):
    return lax.dot_general(left, right, (((0,), (0,)), ((), ())), preferred_element_type=FULL)


def first_kernel(qkv, v0, v1, v2, v3, v4, v5, v6, v7, up, out, tall):
    out[:, 0:2304] = qkv[...]
    tall[...] = jnp.zeros_like(tall)
    for row, vector in enumerate((v0, v1, v2, v3, v4, v5, v6, v7)):
        tall[row : row + 1, 0:24] = vector[...].astype(FULL).reshape(1, 24)
    turned = jnp.transpose(tall[...])[0:24]
    lane = lax.broadcasted_iota(jnp.int32, (24, 128), 1)
    row = lax.broadcasted_iota(jnp.int32, (24, 128), 0)
    tall[0:1, 16:112] = up[...].astype(FULL).reshape(1, 96)
    line = jnp.broadcast_to(tall[0:1, :], (24, 128))
    keep = (row == 0) & (lane >= 16) & (lane < 112)
    out[:, 2304:2432] = jnp.where(lane < 8, turned, jnp.where(keep, line, 0.0)).astype(LOW)


def first_call(qkv, vectors):
    return pl.pallas_call(
        first_kernel,
        out_shape=jax.ShapeDtypeStruct((24, 2432), LOW),
        in_specs=[pl.BlockSpec(memory_space=pltpu.VMEM)] * 10,
        out_specs=pl.BlockSpec(memory_space=pltpu.VMEM),
        scratch_shapes=[pltpu.VMEM((128, 128), FULL)],
        compiler_params=params(),
        cost_estimate=cost(1e5, 3e5),
        name="first",
    )(qkv, *vectors)


def prep_kernel(where, out_m, up_m, down_m, out_s, up_s, down_s, p2, p3):
    def build(core):
        pairs_of = lambda m, s: (m, s) if core == 0 else (s, m)

        def rows(m, s, at, width):
            both = [v[:, at : at + width].astype(FULL) for v in pairs_of(m, s)]
            return jnp.concatenate(both, axis=0).astype(LOW)

        p2[:, 0:1536] = rows(up_m, up_s, core * 1536, 1536)
        p2[:, 1536:1920] = rows(out_m, out_s, core * 384, 384)
        for k, down in enumerate(pairs_of(down_m, down_s)):
            p3[k * 96 : k * 96 + 96, :] = down[:, core * 384 : core * 384 + 384]

    for core in range(2):
        pl.when(where[3] == core)(functools.partial(build, core))


def prep(where, mine, theirs):
    return pl.pallas_call(
        prep_kernel,
        out_shape=[jax.ShapeDtypeStruct((48, 1920), LOW), jax.ShapeDtypeStruct((192, 384), LOW)],
        in_specs=[SMEM] + [pl.BlockSpec(memory_space=pltpu.VMEM)] * 6,
        out_specs=[pl.BlockSpec(memory_space=pltpu.VMEM)] * 2,
        compiler_params=params(),
        cost_estimate=cost(1e6, 2e6),
        name="prep",
    )(where, *mine, *theirs)


def chip_of(where, dz, dy, dx):
    return ((where[0] ^ dz) * 2 + (where[1] ^ dy)) * 2 + (where[2] ^ dx)


def load_pack(where, pieces, start):
    for side in range(2):
        owner = where[3] ^ side
        col, along_x, along_y, far0, far1 = pieces[side * 5 : side * 5 + 5]
        for dz in range(4):
            far = far0.at[dz] if dz < 2 else far1.at[dz - 2]
            for dy, dx, source in ((0, 0, col.at[dz]), (0, 1, along_x.at[dz]), (1, 0, along_y.at[dz]), (1, 1, far)):
                start(source, chip_of(where, dz, dy, dx), owner)


def wait_pack(target, sem):
    pltpu.make_async_copy(target, target, sem).wait()


def normalise(values):
    centre = values - jnp.mean(values, axis=1, keepdims=True)
    spread = lax.rsqrt(jnp.mean(centre * centre, axis=1, keepdims=True) + 1e-6)
    return centre * spread, spread


def qkv_kernel(where, tok, *refs):
    pieces, (qkv, normed, w1, vec, bias_up, buf, weights, hats, sem) = refs[:10], refs[10:]
    half = pl.program_id(0)

    @pl.when(half == 0)
    def _():
        load_pack(
            where, pieces, lambda v, chip, core: pltpu.make_async_copy(v, buf.at[chip * 2 + core], sem).start()
        )
        for t in range(4):
            at = slice(t * 256, t * 256 + 256)
            hats[at, :], _ = normalise(tok[at, :].astype(FULL))
        wait_pack(buf, sem)
        lines = jnp.concatenate([buf[d, :, 2304:2432].astype(FULL) for d in range(32)], axis=0)
        lines = jnp.transpose(lines)
        vec[...] = lines[0:16]
        for chip in range(16):
            for s in range(2):
                line = buf[chip * 2 + s, 0:8, 2304:2432].astype(FULL)[0:1]
                at = (chip * 2 + s) * 96
                bias_up[0:1, at : at + 96] = line[:, 16:112]
        for t in range(4):
            at = slice(t * 256, t * 256 + 256)
            normed[at, :] = (hats[at, :] * lines[0:1] + lines[1:2]).astype(LOW)

    def gather(h):
        for chip in range(16):
            rows = slice(chip * 48, chip * 48 + 48)
            for part in range(3):
                at = slice(part * 768 + h * 384, part * 768 + h * 384 + 384)
                both = [buf[chip * 2 + s, :, at].astype(FULL) for s in range(2)]
                weights[rows, part * 384 : part * 384 + 384] = jnp.concatenate(both, axis=0).astype(LOW)

    for h in range(2):
        pl.when(half == h)(functools.partial(gather, h))
    w1[0] = weights[...]
    at = pl.multiple_of(half * 384, 128)
    query_bias = vec[2:3, pl.ds(at, 384)]
    value_bias = vec[3:4, pl.ds(at, 384)]
    for t in range(4):
        at = slice(t * 256, t * 256 + 256)
        mixed = mul(normed[at, :], weights[...])
        qkv[0, at, 0:384] = (mixed[:, 0:384] + query_bias).astype(LOW) * 0.125
        qkv[0, at, 384:768] = mixed[:, 384:768].astype(LOW)
        qkv[0, at, 768:1152] = (mixed[:, 768:1152] + value_bias).astype(LOW)


def qkv_call(where, tokens, pieces):
    return pl.pallas_call(
        qkv_kernel,
        grid=(2,),
        out_shape=[
            jax.ShapeDtypeStruct((2, 1024, 1152), LOW),
            jax.ShapeDtypeStruct((1024, 768), LOW),
            jax.ShapeDtypeStruct((2, 768, 1152), LOW),
            jax.ShapeDtypeStruct((16, 768), FULL),
            jax.ShapeDtypeStruct((1, 3072), FULL),
        ],
        in_specs=[SMEM, whole((1024, 768))] + [ANY] * 10,
        out_specs=[
            pl.BlockSpec((1, 1024, 1152), lambda h: (h, 0, 0)),
            whole((1024, 768)),
            pl.BlockSpec((1, 768, 1152), lambda h: (h, 0, 0)),
            whole((16, 768)),
            whole((1, 3072)),
        ],
        scratch_shapes=[
            pltpu.VMEM((32, 24, 2432), LOW),
            pltpu.VMEM((768, 1152), LOW),
            pltpu.VMEM((1024, 768), FULL),
            pltpu.SemaphoreType.DMA,
        ],
        compiler_params=params(),
        cost_estimate=cost(2 * 1024 * 768 * 2304, 16e6, scale=0.1),
        name="qkv",
    )(where, tokens, *pieces)


def masked_pair(block):
    lane = lax.broadcasted_iota(jnp.int32, block.shape, 1)
    zero = jnp.zeros_like(block)
    return jnp.concatenate([jnp.where(lane < 64, block, zero), jnp.where(lane < 64, zero, block)], axis=0)


def unmask(both):
    return jnp.concatenate([both[0:64, 0:128], both[64:128, 128:256]], axis=0)


def attend_kernel(first, qkv, seg, pad, *refs):
    probs, att_t, bias, wide = refs[-4:]
    row = pl.program_id(0) + first
    seg_row, pad_row = seg[pl.ds(row, 1), :].astype(FULL), pad[pl.ds(row, 1), :].astype(FULL)
    seg_col = jnp.transpose(jnp.broadcast_to(seg_row, (128, 256)))
    pad_col = jnp.transpose(jnp.broadcast_to(pad_row, (128, 256)))
    for b in range(2):
        keys = slice(64 * b, 64 * b + 192)
        same = seg_col[keys] == jnp.broadcast_to(seg_row[:, 128 * b : 128 * b + 128], (192, 128))
        key_at = lax.broadcasted_iota(jnp.int32, (192, 128), 0) + 64 * b
        query_at = lax.broadcasted_iota(jnp.int32, (192, 128), 1) + 128 * b
        allowed = same & ((pad_col[keys] == 1.0) | (key_at == query_at))
        one = jnp.where(allowed, 0.0, -1e30)
        bias[b] = jnp.concatenate([one, one], axis=1)
    blocks = [(half, p, b) for half in range(2) for p in range(3) for b in range(2)]
    for i, (half, p, b) in enumerate(blocks):
        stack = masked_pair(qkv[half, 128 * b : 128 * b + 128, p * 128 : p * 128 + 128])
        keys = slice(64 * b, 64 * b + 192)
        wide[i] = mul_t(qkv[half, keys, 384 + p * 128 : 512 + p * 128], stack) + bias[b]
    for i, (half, p, b) in enumerate(blocks):
        scores = wide[i]
        power = jnp.exp(scores - jnp.max(scores, axis=0, keepdims=True))
        probs[0, p, half, b] = (power * (1.0 / jnp.sum(power, axis=0, keepdims=True))).astype(LOW)
    for half, p, b in blocks:
        keys = slice(64 * b, 64 * b + 192)
        both = t_mul(qkv[half, keys, 768 + p * 128 : 896 + p * 128], probs[0, p, half, b])
        at = half * 384 + p * 128
        att_t[at : at + 128, 128 * b : 128 * b + 128] = unmask(both).astype(LOW)


def attend_call(first, count, qkv, seg, pad, before):
    old = list(before or [])
    return pl.pallas_call(
        functools.partial(attend_kernel, first),
        grid=(count,),
        out_shape=[
            jax.ShapeDtypeStruct((4, 3, 2, 2, 192, 256), LOW),
            jax.ShapeDtypeStruct((768, 1024), LOW),
        ],
        in_specs=[pl.BlockSpec((2, 256, 1152), lambda r: (0, r + first, 0)), whole((4, 256)), whole((4, 256))]
        + [ANY] * len(old),
        out_specs=[
            pl.BlockSpec((1, 3, 2, 2, 192, 256), lambda r: (r + first, 0, 0, 0, 0, 0)),
            pl.BlockSpec((768, 256), lambda r: (0, r + first)),
        ],
        input_output_aliases={3: 0, 4: 1} if old else {},
        scratch_shapes=[pltpu.VMEM((2, 192, 256), FULL), pltpu.VMEM((12, 192, 256), FULL)],
        compiler_params=params(),
        cost_estimate=cost(count * 1.5e9, count * 3e6, 8e5, scale=0.1),
        name="attend%d" % first,
    )(qkv, seg, pad, *old)


GATE = math.sqrt(2.0 / math.pi)


def gate_pair(u):
    square = u * u
    factor = 0.5 + 0.5 * jnp.tanh(u * (GATE + GATE * 0.044715 * square))
    value = u * factor
    return value, factor + value * (1.0 - factor) * (2.0 * GATE + 6.0 * GATE * 0.044715 * square)


FEED_SCALE = 0.1
CHUNK = 256
TILE = 256
TILES = 1024 // TILE


def load_up(where, pieces, up, w_out, sem, sem_out):
    def start(block, chip, core):
        rows = pl.ds(pl.multiple_of(chip * 48, 16), 48)
        for source, target, width, sem_of in (
            (slice(1536, 1920), w_out, 384, sem_out), (slice(0, 1536), up, 1536, sem)):
            columns = pl.ds(pl.multiple_of(core * width, 128), width)
            pltpu.make_async_copy(block.at[:, source], target.at[rows, columns], sem_of).start()

    load_pack(where, pieces, start)


def back_norm(grad, xhat, spread, gain):
    scaled = grad * gain
    flat = jnp.mean(scaled, axis=1, keepdims=True)
    tilt = jnp.mean(scaled * xhat, axis=1, keepdims=True)
    return (scaled - flat - xhat * tilt) * spread


def add_rows(target, row, values, step):
    value = jnp.sum(values, axis=0, keepdims=True)
    target[row : row + 1, :] = jnp.where(step == 0, value, target[row : row + 1, :] + value)


def feed_tile(step, att_t, tok, cot, bias, vec, weights, kept, outs, before):
    up, down, w_out = weights
    normed, act, hid = kept
    output, middle_grad, branch_grad, att_grad, sums, bias_grad = outs
    here = pl.ds(pl.multiple_of(step * TILE, TILE), TILE)
    before(0)
    mid = tok[...].astype(FULL) + t_mul(att_t[...], w_out[...]) + vec[4:5, :]
    xhat, spread = normalise(mid)
    rows = (xhat * vec[5:6, :] + vec[6:7, :]).astype(LOW)
    normed[here, :] = rows
    outer = cot[here, :]
    before(1)
    chunks = [slice(k * CHUNK, k * CHUNK + CHUNK) for k in range(3072 // CHUNK)]
    hidden = mul(rows, up[:, chunks[0]])
    for k, at in enumerate(chunks):
        following = mul(rows, up[:, chunks[k + 1]]) if k + 1 < len(chunks) else None
        if k == 0:
            before(2)
        active_grad = mul_t(outer, down[at, :])
        value, tilt = gate_pair(hidden + bias[:, at])
        act[here, at] = value.astype(LOW)
        grad = (tilt * active_grad).astype(LOW)
        hid[here, at] = grad
        line = jnp.sum(grad.astype(FULL), axis=0, keepdims=True)
        bias_grad[:, at] = jnp.where(step == 0, line, bias_grad[:, at] + line)
        hidden = following

    output[...] = (mid + vec[7:8, :] + mul(act[here, :], down[...])).astype(LOW)
    grad = mul_t(hid[here, :], up[...])
    outer = outer.astype(FULL)
    mid_grad = outer + back_norm(grad, xhat, spread, vec[5:6, :])
    middle_grad[...] = mid_grad
    low = mid_grad.astype(LOW)
    branch_grad[...] = low
    add_rows(sums, 0, grad * xhat, step)
    add_rows(sums, 1, grad, step)
    add_rows(sums, 2, low.astype(FULL), step)
    add_rows(sums, 3, outer, step)
    att_grad[...] = mul_t(low, w_out[...]).astype(LOW)


def feed_kernel(where, att_t, tok, cot, bias, vec, *refs):
    pieces, pieces_down = refs[:10], refs[10:20]
    outs = refs[20:26]
    down_packs, up_packs = refs[26:28], refs[28:30]
    up, down, w_out, normed, act, hid, sems = refs[30:]
    step = pl.program_id(0)
    core = where[3]

    def before(stage):
        @pl.when(step == 0)
        def _():
            if stage == 0:
                load_up(where, pieces, up, w_out, sems.at[1], sems.at[0])

                def start(block, chip, owner):
                    rows = pl.ds(pl.multiple_of(chip * 192, 16), 192)
                    columns = pl.ds(pl.multiple_of(owner * 384, 128), 384)
                    pltpu.make_async_copy(block, down.at[rows, columns], sems.at[2]).start()

                load_pack(where, pieces_down, start)
            target = (w_out, up, down)[stage]
            wait_pack(target, sems.at[stage])

    @pl.when(step < TILES)
    def _():
        feed_tile(step, att_t, tok, cot, bias, vec, (up, down, w_out), (normed, act, hid), outs, before)

    @pl.when(step >= TILES)
    def _():
        pair = step - TILES
        at = pl.multiple_of(pair * 1536, 1536)
        grad_down = t_mul(act[:, pl.ds(at, 1536)], cot[...]).astype(LOW)
        at = pl.multiple_of(pair * 384, 384)
        grad_up = t_mul(normed[:, pl.ds(at, 384)], hid[...])

        def put(side):
            for o in range(2):
                for k in range(8):
                    spot = ((k // 2 % 2) ^ where[1], (k % 2) ^ where[2], (k // 4) ^ (where[0] % 2))
                    at = k * 192 + o * 96
                    for h in range(2):
                        down_packs[o ^ side][spot + (slice(h * 96, h * 96 + 96),)] = grad_down[
                            at : at + 96, h * 384 : h * 384 + 384
                        ]
                    rows = grad_up[k * 48 + o * 24 : k * 48 + o * 24 + 24]
                    for j in range(4):
                        both = [rows[:, i * 384 : i * 384 + 384] for i in (2 * j, 2 * j + 1)]
                        up_packs[o ^ side][spot + (slice(j * 48, j * 48 + 48),)] = jnp.concatenate(
                            both, axis=0
                        ).astype(LOW)

        for side in range(2):
            pl.when(core == side)(functools.partial(put, side))


def feed_call(where, att_t, tokens, cot, bias_up, vec, pieces, pieces_down):
    tile = lambda step: jnp.minimum(step, TILES - 1)
    rows = pl.BlockSpec((TILE, 768), lambda s, where: (tile(s), 0))
    fixed = lambda shape: pl.BlockSpec(shape, lambda s, where: (0,) * len(shape), pipeline_mode=pl.Buffered(1))
    pack = (2, 2, 4, 192, 384)
    pack_block = pl.BlockSpec(
        (2, 2, 2, 192, 384), lambda s, where: (0, 0, jnp.clip(s - TILES, 0, 1) ^ (where[0] // 2), 0, 0))
    return pl.pallas_call(
        feed_kernel,
        grid_spec=pltpu.PrefetchScalarGridSpec(
            num_scalar_prefetch=1,
            grid=(TILES + 2,),
            in_specs=[
                pl.BlockSpec((768, TILE), lambda s, where: (0, tile(s))), rows, fixed((1024, 768)),
                fixed((1, 3072)), fixed((16, 768)),
            ] + [ANY] * 20,
            out_specs=[
                rows, rows, rows, rows, fixed((8, 768)), fixed((1, 3072)), *([pack_block] * 4),
            ],
            scratch_shapes=[
                pltpu.VMEM((768, 3072), LOW),
                pltpu.VMEM((3072, 768), LOW),
                pltpu.VMEM((768, 768), LOW),
                pltpu.VMEM((1024, 768), LOW),
                pltpu.VMEM((1024, 3072), LOW),
                pltpu.VMEM((1024, 3072), LOW),
                pltpu.SemaphoreType.DMA((3,)),
            ],
        ),
        out_shape=[
            jax.ShapeDtypeStruct((1024, 768), LOW),
            jax.ShapeDtypeStruct((1024, 768), FULL),
            jax.ShapeDtypeStruct((1024, 768), LOW),
            jax.ShapeDtypeStruct((1024, 768), LOW),
            jax.ShapeDtypeStruct((8, 768), FULL),
            jax.ShapeDtypeStruct((1, 3072), FULL),
        ] + [jax.ShapeDtypeStruct(pack, LOW)] * 4,
        compiler_params=params(),
        cost_estimate=cost(26 * 1024 * 768 * 768 * 2, 35e6, 3e6, scale=FEED_SCALE),
        name="feed",
    )(where, att_t, tokens, cot, bias_up, vec, *pieces, *pieces_down)


ROWS_STEP = 2


def unattend_kernel(groups, with_out, where, *refs):
    count = len(groups)
    parts = [refs[5 * g : 5 * g + 5] for g in range(count)]
    refs = refs[5 * count + (0 if with_out else 2) :]
    probs, normed = refs[:count], refs[count]
    refs = refs[count + 1 :]
    if with_out:
        att_t, branch_grad, refs = refs[0], refs[1], refs[2:]
        mixed, mine, theirs, sums, acc, wide, slim, stacks, out_acc = refs
    else:
        mixed, mine, theirs, sums, acc, wide, slim, stacks = refs
    step = pl.program_id(0)
    width = 128 * count
    blocks = [(r, g, h) for r in range(ROWS_STEP) for g in range(count) for h in range(2)]

    def keys_of(r, b):
        return slice(256 * r + 64 * b, 256 * r + 64 * b + 192)

    def queries_of(r, b):
        return slice(256 * r + 128 * b, 256 * r + 128 * b + 128)

    for i, (r, g, half) in enumerate(blocks):
        query, key, value = parts[g][:3]
        grads = parts[g][3 + half]
        for b in range(2):
            stacks[0, 2 * i + b] = masked_pair(query[half, queries_of(r, b), :])
            stack = masked_pair(grads[queries_of(r, b), :])
            stacks[1, 2 * i + b] = stack
            wide[2 * i + b] = mul_t(value[half, keys_of(r, b), :], stack)
    for i, (r, g, half) in enumerate(blocks):
        for b in range(2):
            weights = probs[g][r, 0, half, b].astype(FULL)
            prob_grad = wide[2 * i + b]
            inner = jnp.sum(prob_grad * weights, axis=0, keepdims=True)
            slim[2 * i + b] = (weights * (prob_grad - inner)).astype(LOW)

    def merge(first, second):
        return jnp.concatenate([first[0:64], first[64:192] + second[0:128], second[128:192]], axis=0)

    for i, (r, g, half) in enumerate(blocks):
        key = parts[g][1]
        rows = slice(256 * r, 256 * r + 256)
        value_grad = [mul(probs[g][r, 0, half, b], stacks[1, 2 * i + b]) for b in range(2)]
        key_grad = [mul(slim[2 * i + b], stacks[0, 2 * i + b]) for b in range(2)]
        turned = [unmask(t_mul(key[half, keys_of(r, b), :], slim[2 * i + b])) for b in range(2)]
        query_grad = jnp.transpose(jnp.concatenate(turned, axis=1)) * 0.125
        at = g * 128
        mixed[half, rows, at : at + 128] = query_grad.astype(LOW)
        mixed[half, rows, width + at : width + at + 128] = merge(*key_grad).astype(LOW)
        mixed[half, rows, 2 * width + at : 2 * width + at + 128] = merge(*value_grad).astype(LOW)

    def add(target, more):
        @pl.when(step == 0)
        def _():
            target[...] = more

        @pl.when(step > 0)
        def _():
            target[...] += more

    for half in range(2):
        add_rows(sums.at[half], 0, mixed[half].astype(FULL), step)
        add(acc.at[half], t_mul(normed[...], mixed[half]))
    if with_out:
        add(out_acc, mul(att_t[...], branch_grad[...]))

    def write(side):
        for owner in range(2):
            dest = mine if owner == side else theirs
            for chip in range(16):
                rows = slice(chip * 48 + owner * 24, chip * 48 + owner * 24 + 24)
                spot = ((chip // 2 % 2) ^ where[1], (chip % 2) ^ where[2], (chip // 4) ^ where[0], slice(None))
                if with_out:
                    lines = [out_acc[rows, :], jnp.concatenate([acc[0, rows, :], acc[1, rows, :]], axis=1)]
                else:
                    lines = [acc[0, rows, :], acc[1, rows, :]]
                dest[spot + (slice(0, 768),)] = jnp.concatenate(lines, axis=0).astype(LOW)

    for side in range(2):
        pl.when((step == 4 // ROWS_STEP - 1) & (where[3] == side))(functools.partial(write, side))


def unattend_call(groups, where, qkv, att_grad, probs, normed, packs=None, att_t=None, branch_grad=None):
    with_out = att_t is not None
    count = len(groups)
    width = 384 * count
    tall = 256 * ROWS_STEP
    operands, specs = [], []
    for p in groups:
        for part in range(3):
            operands.append(qkv)
            specs.append(pl.BlockSpec((2, tall, 128), lambda r, c=part * 3 + p: (0, r, c)))
        for half in range(2):
            operands.append(att_grad)
            specs.append(pl.BlockSpec((tall, 128), lambda r, c=half * 3 + p: (r, c)))
    if not with_out:
        operands += list(packs)
        specs += [ANY, ANY]
    for p in groups:
        operands.append(probs)
        specs.append(pl.BlockSpec((ROWS_STEP, 1, 2, 2, 192, 256), lambda r, p=p: (r, p, 0, 0, 0, 0)))
    operands.append(normed)
    specs.append(pl.BlockSpec((tall, 768), lambda r: (r, 0)))
    if with_out:
        operands += [att_t, branch_grad]
        specs += [pl.BlockSpec((768, tall), lambda r: (0, r)), pl.BlockSpec((tall, 768), lambda r: (r, 0))]
    shape = (2, 2, 4, 48, 1536)
    lanes = 0 if with_out else 1
    part_of = pl.BlockSpec((2, 2, 4, 48, 768), lambda r: (0, 0, 0, 0, lanes), pipeline_mode=pl.Buffered(1))
    many = 4 * count * ROWS_STEP
    return pl.pallas_call(
        functools.partial(unattend_kernel, groups, with_out),
        grid=(4 // ROWS_STEP,),
        out_shape=[
            jax.ShapeDtypeStruct((2, 1024, width), LOW),
            jax.ShapeDtypeStruct(shape, LOW),
            jax.ShapeDtypeStruct(shape, LOW),
            jax.ShapeDtypeStruct((2, 8, width), FULL),
        ],
        in_specs=[SMEM] + specs,
        out_specs=[
            pl.BlockSpec((2, tall, width), lambda r: (0, r, 0)),
            part_of,
            part_of,
            whole((2, 8, width)),
        ],
        input_output_aliases={} if with_out else {1 + 5 * count + k: 1 + k for k in range(2)},
        scratch_shapes=[
            pltpu.VMEM((2, 768, width), FULL),
            pltpu.VMEM((many, 192, 256), FULL),
            pltpu.VMEM((many, 192, 256), LOW),
            pltpu.VMEM((2, many, 256, 128), LOW),
        ] + ([pltpu.VMEM((768, 768), FULL)] if with_out else []),
        compiler_params=params(),
        cost_estimate=cost(count * 2.5e9, count * 8e6),
        name="unattend%d" % groups[0],
    )(where, *operands)


def tokens_kernel(m0, m1, w1, tok, vec, middle_grad, sums, sums0, sums1, bias, grad, lines):
    step = pl.program_id(0)
    total = None
    for half in range(2):
        joined = []
        for part in range(3):
            joined.append(m0[half, :, part * 128 : part * 128 + 128])
            joined.append(m1[half, :, part * 256 : part * 256 + 256])
        more = mul_t(jnp.concatenate(joined, axis=1), w1[half])
        total = more if total is None else total + more
    xhat, spread = normalise(tok[...].astype(FULL))
    grad[...] = middle_grad[...] + back_norm(total, xhat, spread, vec[0:1, :])
    add_rows(lines, 0, total * xhat, step)
    add_rows(lines, 1, total, step)

    @pl.when(step == 3)
    def _():
        for half in range(2):
            at = half * 384
            for row, part in ((2, 0), (3, 2)):
                lines[row : row + 1, at : at + 128] = sums0[half, 0:1, part * 128 : part * 128 + 128]
                lines[row : row + 1, at + 128 : at + 384] = sums1[half, 0:1, part * 256 : part * 256 + 256]
        lines[4:5, :] = sums[2:3, :]
        lines[5:6, :] = sums[0:1, :]
        lines[6:7, :] = sums[1:2, :]
        lines[7:8, :] = sums[3:4, :]
        for k in range(4):
            lines[8 + k : 9 + k, :] = bias[0:1, k * 768 : k * 768 + 768]
        lines[12:16, :] = jnp.zeros((4, 768), FULL)


def tokens_call(mixed0, mixed1, w1, tokens, vec, middle_grad, sums, sums0, sums1, bias):
    rows = pl.BlockSpec((256, 768), lambda r: (r, 0))
    return pl.pallas_call(
        tokens_kernel,
        grid=(4,),
        out_shape=[jax.ShapeDtypeStruct((1024, 768), FULL), jax.ShapeDtypeStruct((16, 768), FULL)],
        in_specs=[pl.BlockSpec((2, 256, w), lambda r: (0, r, 0)) for w in (384, 768)] + [
            whole((2, 768, 1152)), rows, whole((16, 768)), rows, whole((8, 768)), whole((2, 8, 384)),
            whole((2, 8, 768)), whole((1, 3072)),
        ],
        out_specs=[rows, whole((16, 768))],
        compiler_params=params(),
        cost_estimate=cost(2 * 1024 * 768 * 2304, 16e6),
        name="tokens",
    )(mixed0, mixed1, w1, tokens, vec, middle_grad, sums, sums0, sums1, bias)


def after(value, *before):
    return lax.optimization_barrier((value, before))[0]


class Total:
    def __init__(self, mine, theirs):
        self.mine = mine
        self.block = mine.shape[3:]
        self.got = send(theirs, SWAP_C)

    def spec(self, size, place_of):
        return pl.BlockSpec(size + self.block, lambda i: place_of(i) + (0, 0))

    def low(self, *lead):
        return jax.ShapeDtypeStruct(lead + self.block, LOW)

    def first(self):
        def body(mine_x, got_x, mine_y, got_y, out_x, out_y):
            out_x[...] = (mine_x[...].astype(FULL) + got_x[...].astype(FULL)).reshape(out_x.shape).astype(LOW)
            out_y[...] = (mine_y[...].astype(FULL) + got_y[...].astype(FULL)).reshape(out_y.shape).astype(LOW)

        to_x = self.spec((1, 1, 2), lambda i: (i, 1, 0))
        to_y = self.spec((1, 1, 2), lambda i: (1, i, 1))
        out = self.spec((1, 2), lambda i: (i, 0))

        def keep(one_x, one_y):
            self.one_x, self.one_y = send(one_x, SWAP_X), send(one_y, SWAP_Y)

        return (body, [self.mine, self.got] * 2, [to_x, to_x, to_y, to_y], [self.low(2, 2)] * 2, [out] * 2, keep)

    def second(self):
        def body(mine_y, got_y, one_x, mine_x, got_x, one_y, out_y, out_x):
            add = lambda *refs: sum(r[...].astype(FULL).reshape(out_y.shape) for r in refs)
            out_y[...] = add(mine_y, got_y, one_x).astype(LOW)
            out_x[...] = add(mine_x, got_x, one_y).astype(LOW)

        to_y = self.spec((1, 1, 1), lambda i: (1, 0, i))
        to_x = self.spec((1, 1, 1), lambda i: (0, 1, 2 + i))
        came = self.spec((1, 1), lambda i: (1, i))
        out = self.spec((1,), lambda i: (i,))

        def keep(two_y, two_x):
            self.two_y, self.two_x = send(two_y, SWAP_Y), send(two_x, SWAP_X)

        operands = [self.mine, self.got, self.one_x, self.mine, self.got, self.one_y]
        return (body, operands, [to_y, to_y, came, to_x, to_x, came], [self.low(2)] * 2, [out] * 2, keep)

    def third(self):
        def body(mine, got, one_x, two_y, one_y, two_x, *outs):
            @pl.when(pl.program_id(0) == 0)
            def _():
                for k, target in enumerate(outs):
                    extra = (one_x[0, k], two_y[k]) if k < 2 else (one_y[0, k - 2], two_x[k - 2])
                    total = mine[0, 0, k].astype(FULL) + got[0, 0, k].astype(FULL)
                    total = total + extra[0].astype(FULL) + extra[1].astype(FULL)
                    target[...] = total.astype(target.dtype)

        near = self.spec((1, 1, 4), lambda i: (0, 0, 0))
        came = self.spec((1, 2), lambda i: (0, 0))
        two = self.spec((2,), lambda i: (0,))
        one = pl.BlockSpec(self.block, lambda i: (0, 0))
        out = [jax.ShapeDtypeStruct(self.block, FULL)] + [self.low()] * 3

        def keep(own, *three):
            self.own = own
            self.parts = [send(v, SWAP_Z[k + 1]) for k, v in enumerate(three)]

        operands = [self.mine, self.got, self.one_x, self.two_y, self.one_y, self.two_x]
        return (body, operands, [near, near, came, two, came, two], out, [one] * 4, keep)

    def last(self, write, shapes, more=()):
        def body(own, part1, part2, part3, *refs):
            @pl.when(pl.program_id(0) == 0)
            def _():
                total = own[...] + part1[...].astype(FULL) + part2[...].astype(FULL) + part3[...].astype(FULL)
                write(total, *refs)

        block = pl.BlockSpec(self.block, lambda i: (0, 0))
        same = lambda shape: pl.BlockSpec(shape, lambda i: (0,) * len(shape))

        def keep(*given):
            self.final = given

        return (
            body, [self.own, *self.parts, *more], [block] * 4 + [same(v.shape) for v in more],
            [jax.ShapeDtypeStruct(v, FULL) for v in shapes], [same(v) for v in shapes], keep,
        )


def write_down(total, share):
    share[...] = jnp.concatenate([total[0:96], total[96:192]], axis=1)


def write_up(total, share):
    share[...] = jnp.concatenate([total[j * 24 : j * 24 + 24] for j in range(8)], axis=1)


def write_head(total, share_out, share):
    share_out[...] = total[0:24, 0:768]
    for half in range(2):
        for part in range(3):
            at = part * 768 + half * 384
            first = half * 384 + part * 128
            share[:, at : at + 128] = total[24:48, first : first + 128]
            rest = 768 + part * 256
            share[:, at + 128 : at + 384] = total[half * 24 : half * 24 + 24, rest : rest + 256]


def run_stages(stages, *before):
    ins = [len(s[1]) for s in stages]
    outs = [len(s[3]) for s in stages]

    def kernel(*refs):
        at_in, at_out = 0, sum(ins)
        for stage, n_in, n_out in zip(stages, ins, outs):
            stage[0](*refs[at_in : at_in + n_in], *refs[at_out : at_out + n_out])
            at_in, at_out = at_in + n_in, at_out + n_out

    operands = after([v for s in stages for v in s[1]], *before)
    results = pl.pallas_call(
        kernel,
        grid=(2,),
        out_shape=[v for s in stages for v in s[3]],
        in_specs=[v for s in stages for v in s[2]],
        out_specs=[v for s in stages for v in s[4]],
        compiler_params=params(),
        cost_estimate=cost(1e6, 4e6),
        name="sums",
    )(*operands)
    at = 0
    for stage, n_out in zip(stages, outs):
        stage[5](*results[at : at + n_out])
        at += n_out
    return results


def halves_of(own, sibling, core):
    return jnp.where(core == 0, own, sibling), jnp.where(core == 0, sibling, own)


def on_device(
    tokens, segment_ids, pad_mask, w_qkv, w_out, w_up, w_down, gain_one, shift_one, bias_query,
    bias_value, bias_out, gain_two, shift_two, bias_up, bias_down, cotangent,
):
    z0, y0, x0, core = place()
    where = jnp.stack([z0, y0, x0, core]).astype(jnp.int32)
    row_count, length, width = tokens.shape
    total_rows = row_count * length
    flat = tokens.reshape(total_rows, width)
    cot = cotangent.reshape(total_rows, width)
    vectors = (gain_one, shift_one, bias_query, bias_value, bias_out, gain_two, shift_two, bias_down, bias_up)

    def along_z(own):
        return [send(own[None], SWAP_Z[k]) for k in (1, 2, 3)]

    def column(own, rest):
        return jnp.concatenate([own[None], *rest], axis=0)

    def plane(col):
        return send(col, SWAP_X), send(col, SWAP_Y)

    def corner(along_x, along_y):
        return send(along_x[0:2], SWAP_Y), send(along_y[2:4], SWAP_X)

    def across(blocks):
        return [send(v, SWAP_C) for v in blocks]

    p1 = first_call(w_qkv, vectors)
    rest1 = along_z(p1)
    mine = (w_out, w_up, w_down)
    p2, p3 = prep(where, after(mine, p1), across(mine))
    col1 = column(after(p1, p2), rest1)
    x1, y1 = plane(col1)
    rest2 = along_z(after(p2, col1))
    col2 = column(p2, rest2)
    far1 = corner(x1, y1)
    own1 = [col1, x1, y1]
    pack1 = own1 + list(far1) + across(own1) + across(far1)
    col2 = after(col2, far1)
    x2, y2 = plane(col2)
    rest3 = along_z(after(p3, col2))
    qkv, normed_one, w1, vec, up_line = qkv_call(where, after(flat, col2), pack1)
    col3 = column(after(p3, qkv), rest3)
    x3, y3 = plane(col3)
    held = attend_call(0, 2, after(qkv, col3), segment_ids, pad_mask, None)
    far2 = corner(x2, y2)
    other2 = across(after([col2, x2, y2], held))
    probs, att_t = attend_call(2, 2, after(qkv, x2, y2), segment_ids, pad_mask, held)
    pack2 = [col2, x2, y2, *far2] + other2 + across(after(far2, att_t))
    far3 = corner(after(x3, att_t), after(y3, att_t))
    own3 = [col3, x3, y3]
    pack3 = own3 + list(far3) + across(after(own3, att_t, other2)) + across(far3)
    output, middle_grad, branch_grad, att_grad, sums, bias_grad, *grads = feed_call(
        where, att_t, flat, cot, up_line, vec, pack2, pack3)

    sum_a, sum_b = Total(*grads[:2]), Total(*grads[2:])
    ready = run_stages([sum_a.first()])
    mixed0, mine, theirs, sums0 = unattend_call(
        (0,), where, qkv, after(att_grad, ready), probs, normed_one, None, att_t, branch_grad)
    ready = run_stages([sum_a.second(), sum_b.first()], mixed0)
    mixed1, mine, theirs, sums1 = unattend_call(
        (1, 2), where, qkv, after(att_grad, ready), probs, normed_one, (mine, theirs))
    head = Total(mine, theirs)
    ready = run_stages([sum_a.third(), sum_b.second()], mixed1)
    grad_tokens, lines = tokens_call(
        mixed0, after(mixed1, ready), w1, flat, vec, middle_grad, sums, sums0, sums1, bias_grad)
    ready = run_stages([sum_b.third(), head.first(), sum_a.last(write_down, [(96, 768)])], grad_tokens)
    lines = after(lines, ready)
    got = send(lines, SWAP_C)
    ready = run_stages([head.second(), sum_b.last(write_up, [(24, 3072)])], ready)
    lines = after(lines, ready) + got
    got = [send(lines, move) for move in (SWAP_X, SWAP_Y, SWAP_D)]
    ready = run_stages([head.third()], ready)
    lines = after(lines, ready) + got[0] + (got[1] + got[2])
    got = [send(lines, move) for move in SWAP_Z[1:]]
    run_stages([head.last(write_head, [(24, 768), (24, 2304)])], ready)
    lines = lines + got[0] + (got[1] + got[2])
    share_out, share_qkv = head.final
    share_up, share_down = sum_b.final[0], sum_a.final[0]

    device = ((z0 * 2 + y0) * 2 + x0) * 2 + core
    own = lax.dynamic_slice(lines, (0, device * 24), (8, 24))
    own_up = lax.dynamic_slice(lines, (8 + device // 8, device % 8 * 96), (1, 96))[0]
    return (
        output.reshape(row_count, length, width),
        grad_tokens.reshape(row_count, length, width),
        share_qkv, share_out, share_up, share_down,
        own[0], own[1], own[2], own[3], own[4], own[5], own[6], own_up, own[7],
    )


def solution(mesh):
    fits = dict(mesh.shape) == {"gx": 8, "gy": 4}
    device = on_device if fits else generic_device
    names = AXES if fits else ("gx", "gy")
    if fits:
        mesh = Mesh(mesh.devices.reshape(4, 2, 2, 2), AXES)
    return jax.shard_map(
        device,
        mesh=mesh,
        in_specs=(
            P(names, None, None),
            P(names, None),
            P(names, None),
            P(names, None),
            P(names, None),
            P(names, None),
            P(names, None),
            P(names),
            P(names),
            P(names),
            P(names),
            P(names),
            P(names),
            P(names),
            P(names),
            P(names),
            P(names, None, None),
        ),
        out_specs=(
            P(names, None, None),
            P(names, None, None),
            P(names, None),
            P(names, None),
            P(names, None),
            P(names, None),
            P(names),
            P(names),
            P(names),
            P(names),
            P(names),
            P(names),
            P(names),
            P(names),
            P(names),
        ),
        check_vma=False,
    )
```

```python
import functools
import math

import jax
import jax.numpy as jnp
from jax import lax
from jax.experimental import pallas as pl
from jax.experimental.pallas import tpu as pltpu
from jax.sharding import Mesh
from jax.sharding import PartitionSpec as P

HEADS = 12
HDIM = 64


def layer_norm(values, gain, shift):
    centre = values - jnp.mean(values, axis=-1, keepdims=True)
    spread = jnp.mean(centre * centre, axis=-1, keepdims=True)
    return centre * lax.rsqrt(spread + 1e-06) * gain + shift


def smooth_gate(values):
    return jax.nn.gelu(values, approximate=True)


def attend_mask(segment_ids, pad_mask):
    length = segment_ids.shape[-1]
    positions = jnp.arange(length)
    same = segment_ids[:, :, None] == segment_ids[:, None, :]
    real = pad_mask[:, None, :] == 1
    itself = positions[:, None] == positions[None, :]
    return same & (real | itself[None])


def outer_sum(left, right):
    return lax.dot_general(
        left, right, (((0,), (0,)), ((), ())), preferred_element_type=jnp.float32
    )


def against(left, matrix):
    return lax.dot_general(
        left, matrix, (((1,), (1,)), ((), ())), preferred_element_type=jnp.float32
    )


def score_block(query_part, key_part, allowed):
    raw = jnp.einsum("rqhe,rkhe->rhqk", query_part, key_part, preferred_element_type=jnp.float32)
    raw = raw * (1.0 / math.sqrt(HDIM))
    return jnp.where(allowed[:, None], raw, -1e30)


def collect(
    w_qkv,
    w_out,
    w_up,
    w_down,
    gain_one,
    shift_one,
    bias_query,
    bias_value,
    bias_out,
    gain_two,
    shift_two,
    bias_up,
    bias_down,
):
    return (
        lax.all_gather(w_qkv, ("gx", "gy"), axis=0, tiled=True),
        lax.all_gather(w_out, ("gx", "gy"), axis=0, tiled=True),
        lax.all_gather(w_up, ("gx", "gy"), axis=0, tiled=True),
        lax.all_gather(w_down, ("gx", "gy"), axis=0, tiled=True),
        lax.all_gather(gain_one, ("gx", "gy"), axis=0, tiled=True),
        lax.all_gather(shift_one, ("gx", "gy"), axis=0, tiled=True),
        lax.all_gather(bias_query, ("gx", "gy"), axis=0, tiled=True),
        lax.all_gather(bias_value, ("gx", "gy"), axis=0, tiled=True),
        lax.all_gather(bias_out, ("gx", "gy"), axis=0, tiled=True),
        lax.all_gather(gain_two, ("gx", "gy"), axis=0, tiled=True),
        lax.all_gather(shift_two, ("gx", "gy"), axis=0, tiled=True),
        lax.all_gather(bias_up, ("gx", "gy"), axis=0, tiled=True),
        lax.all_gather(bias_down, ("gx", "gy"), axis=0, tiled=True),
    )


def generic_device(
    tokens,
    segment_ids,
    pad_mask,
    w_qkv,
    w_out,
    w_up,
    w_down,
    gain_one,
    shift_one,
    bias_query,
    bias_value,
    bias_out,
    gain_two,
    shift_two,
    bias_up,
    bias_down,
    cotangent,
):
    row_count, length, width = tokens.shape
    total_rows = row_count * length
    gathered = collect(
        w_qkv,
        w_out,
        w_up,
        w_down,
        gain_one,
        shift_one,
        bias_query,
        bias_value,
        bias_out,
        gain_two,
        shift_two,
        bias_up,
        bias_down,
    )
    full_qkv, full_out, full_up, full_down = (gathered[0], gathered[1], gathered[2], gathered[3])
    gain_first = gathered[4].astype(jnp.float32)
    shift_first = gathered[5].astype(jnp.float32)
    query_bias = gathered[6].astype(jnp.float32)
    value_bias = gathered[7].astype(jnp.float32)
    out_bias = gathered[8].astype(jnp.float32)
    gain_second = gathered[9].astype(jnp.float32)
    shift_second = gathered[10].astype(jnp.float32)
    up_bias = gathered[11].astype(jnp.float32)
    down_bias = gathered[12].astype(jnp.float32)
    allowed = attend_mask(segment_ids, pad_mask)
    inputs = tokens.astype(jnp.float32).reshape(total_rows, width)
    first_norm, first_pull = jax.vjp(layer_norm, inputs, gain_first, shift_first)
    normed = first_norm.astype(jnp.bfloat16)
    mixed = jnp.dot(normed, full_qkv, preferred_element_type=jnp.float32)
    query_part = (
        (mixed[:, :width] + query_bias).astype(jnp.bfloat16).reshape(row_count, length, HEADS, HDIM)
    )
    key_part = (
        mixed[:, width : 2 * width].astype(jnp.bfloat16).reshape(row_count, length, HEADS, HDIM)
    )
    value_part = (
        (mixed[:, 2 * width :] + value_bias)
        .astype(jnp.bfloat16)
        .reshape(row_count, length, HEADS, HDIM)
    )
    scores = score_block(query_part, key_part, allowed)
    highest = jnp.max(scores, axis=-1, keepdims=True)
    log_total = highest + jnp.log(jnp.sum(jnp.exp(scores - highest), axis=-1, keepdims=True))
    weights = jnp.exp(scores - log_total).astype(jnp.bfloat16)
    attended = jnp.einsum(
        "rhqk,rkhe->rqhe", weights, value_part, preferred_element_type=jnp.float32
    )
    attended = attended.reshape(total_rows, width).astype(jnp.bfloat16)
    middle = inputs + jnp.dot(attended, full_out, preferred_element_type=jnp.float32) + out_bias
    second_norm, second_pull = jax.vjp(layer_norm, middle, gain_second, shift_second)
    normed_two = second_norm.astype(jnp.bfloat16)
    hidden = jnp.dot(normed_two, full_up, preferred_element_type=jnp.float32) + up_bias
    active, gate_pull = jax.vjp(smooth_gate, hidden)
    active_low = active.astype(jnp.bfloat16)
    result = middle + jnp.dot(active_low, full_down, preferred_element_type=jnp.float32) + down_bias
    output = result.astype(jnp.bfloat16).reshape(row_count, length, width)
    again = collect(
        w_qkv,
        w_out,
        w_up,
        w_down,
        gain_one,
        shift_one,
        bias_query,
        bias_value,
        bias_out,
        gain_two,
        shift_two,
        bias_up,
        bias_down,
    )
    full_qkv, full_out, full_up, full_down = (again[0], again[1], again[2], again[3])
    down_in = cotangent.reshape(total_rows, width)
    outer_grad = down_in.astype(jnp.float32)
    grad_bias_down = jnp.sum(outer_grad, axis=0)
    grad_w_down = outer_sum(active_low, down_in)
    active_grad = against(down_in, full_down)
    hidden_grad = gate_pull(active_grad)[0].astype(jnp.bfloat16)
    grad_bias_up = jnp.sum(hidden_grad.astype(jnp.float32), axis=0)
    grad_w_up = outer_sum(normed_two, hidden_grad)
    norm_two_grad = against(hidden_grad, full_up)
    middle_part, grad_gain_two, grad_shift_two = second_pull(norm_two_grad)
    middle_grad = outer_grad + middle_part
    branch_grad = middle_grad.astype(jnp.bfloat16)
    grad_bias_out = jnp.sum(branch_grad.astype(jnp.float32), axis=0)
    grad_w_out = outer_sum(attended, branch_grad)
    attended_grad = (
        against(branch_grad, full_out).astype(jnp.bfloat16).reshape(row_count, length, HEADS, HDIM)
    )
    probs = jnp.exp(score_block(query_part, key_part, allowed) - log_total)
    probs_low = probs.astype(jnp.bfloat16)
    value_grad = jnp.einsum(
        "rhqk,rqhe->rkhe", probs_low, attended_grad, preferred_element_type=jnp.float32
    ).astype(jnp.bfloat16)
    prob_grad = jnp.einsum(
        "rqhe,rkhe->rhqk", attended_grad, value_part, preferred_element_type=jnp.float32
    )
    inner_term = jnp.sum(prob_grad * probs, axis=-1, keepdims=True)
    score_grad = (probs * (prob_grad - inner_term)).astype(jnp.bfloat16)
    score_scale = 1.0 / math.sqrt(HDIM)
    query_grad = (
        (
            jnp.einsum("rhqk,rkhe->rqhe", score_grad, key_part, preferred_element_type=jnp.float32)
            * score_scale
        )
        .astype(jnp.bfloat16)
        .reshape(total_rows, width)
    )
    key_grad = (
        (
            jnp.einsum(
                "rhqk,rqhe->rkhe", score_grad, query_part, preferred_element_type=jnp.float32
            )
            * score_scale
        )
        .astype(jnp.bfloat16)
        .reshape(total_rows, width)
    )
    value_flat = value_grad.reshape(total_rows, width)
    mixed_grad = jnp.concatenate([query_grad, key_grad, value_flat], axis=1)
    grad_bias_query = jnp.sum(query_grad.astype(jnp.float32), axis=0)
    grad_bias_value = jnp.sum(value_flat.astype(jnp.float32), axis=0)
    grad_w_qkv = outer_sum(normed, mixed_grad)
    norm_one_grad = against(mixed_grad, full_qkv)
    input_part, grad_gain_one, grad_shift_one = first_pull(norm_one_grad)
    grad_tokens = (middle_grad + input_part).reshape(row_count, length, width)
    shares = (
        lax.psum_scatter(grad_w_qkv, ("gx", "gy"), scatter_dimension=0, tiled=True),
        lax.psum_scatter(grad_w_out, ("gx", "gy"), scatter_dimension=0, tiled=True),
        lax.psum_scatter(grad_w_up, ("gx", "gy"), scatter_dimension=0, tiled=True),
        lax.psum_scatter(grad_w_down, ("gx", "gy"), scatter_dimension=0, tiled=True),
        lax.psum_scatter(grad_gain_one, ("gx", "gy"), scatter_dimension=0, tiled=True),
        lax.psum_scatter(grad_shift_one, ("gx", "gy"), scatter_dimension=0, tiled=True),
        lax.psum_scatter(grad_bias_query, ("gx", "gy"), scatter_dimension=0, tiled=True),
        lax.psum_scatter(grad_bias_value, ("gx", "gy"), scatter_dimension=0, tiled=True),
        lax.psum_scatter(grad_bias_out, ("gx", "gy"), scatter_dimension=0, tiled=True),
        lax.psum_scatter(grad_gain_two, ("gx", "gy"), scatter_dimension=0, tiled=True),
        lax.psum_scatter(grad_shift_two, ("gx", "gy"), scatter_dimension=0, tiled=True),
        lax.psum_scatter(grad_bias_up, ("gx", "gy"), scatter_dimension=0, tiled=True),
        lax.psum_scatter(grad_bias_down, ("gx", "gy"), scatter_dimension=0, tiled=True),
    )
    return (
        output,
        grad_tokens,
        shares[0],
        shares[1],
        shares[2],
        shares[3],
        shares[4],
        shares[5],
        shares[6],
        shares[7],
        shares[8],
        shares[9],
        shares[10],
        shares[11],
        shares[12],
    )


CHIPS = ("z", "y", "x")
AXES = CHIPS + ("core",)


def pairs(move):
    out = []
    for d in range(32):
        z, y, x, c = d // 8, (d // 4) % 2, (d // 2) % 2, d % 2
        z, y, x, c = move(z, y, x, c)
        out.append((d, ((z * 2 + y) * 2 + x) * 2 + c))
    return out


SWAP_C = pairs(lambda z, y, x, c: (z, y, x, 1 - c))
SWAP_X = pairs(lambda z, y, x, c: (z, y, 1 - x, c))
SWAP_Y = pairs(lambda z, y, x, c: (z, 1 - y, x, c))
SWAP_D = pairs(lambda z, y, x, c: (z, 1 - y, 1 - x, c))
SWAP_Z = [None] + [pairs(lambda z, y, x, c, k=k: (z ^ k, y, x, c)) for k in (1, 2, 3)]


def send(values, perm):
    return lax.ppermute(values, AXES, perm)


def place():
    return tuple(lax.axis_index(name) for name in AXES)


LOW = jnp.bfloat16
FULL = jnp.float32
ANY = pl.BlockSpec(memory_space=pl.ANY)
SMEM = pl.BlockSpec(memory_space=pltpu.SMEM)
MIB = 1024 * 1024


def whole(shape):
    zeros = (0,) * len(shape)
    return pl.BlockSpec(shape, lambda *_: zeros, pipeline_mode=pl.Buffered(1))


def params(limit=64):
    return pltpu.CompilerParams(vmem_limit_bytes=limit * MIB)


def cost(flops, read, exps=0, scale=10.0):
    return pl.CostEstimate(
        flops=int(scale * flops), bytes_accessed=int(scale * read), transcendentals=int(scale * exps)
    )


def mul(left, right):
    return lax.dot_general(left, right, (((1,), (0,)), ((), ())), preferred_element_type=FULL)


def mul_t(left, right):
    return lax.dot_general(left, right, (((1,), (1,)), ((), ())), preferred_element_type=FULL)


def t_mul(left, right):
    return lax.dot_general(left, right, (((0,), (0,)), ((), ())), preferred_element_type=FULL)


def first_kernel(qkv, v0, v1, v2, v3, v4, v5, v6, v7, up, out, tall):
    out[:, 0:2304] = qkv[...]
    tall[...] = jnp.zeros_like(tall)
    for row, vector in enumerate((v0, v1, v2, v3, v4, v5, v6, v7)):
        tall[row : row + 1, 0:24] = vector[...].astype(FULL).reshape(1, 24)
    turned = jnp.transpose(tall[...])[0:24]
    lane = lax.broadcasted_iota(jnp.int32, (24, 128), 1)
    row = lax.broadcasted_iota(jnp.int32, (24, 128), 0)
    tall[0:1, 16:112] = up[...].astype(FULL).reshape(1, 96)
    line = jnp.broadcast_to(tall[0:1, :], (24, 128))
    keep = (row == 0) & (lane >= 16) & (lane < 112)
    out[:, 2304:2432] = jnp.where(lane < 8, turned, jnp.where(keep, line, 0.0)).astype(LOW)


def first_call(qkv, vectors):
    return pl.pallas_call(
        first_kernel,
        out_shape=jax.ShapeDtypeStruct((24, 2432), LOW),
        in_specs=[pl.BlockSpec(memory_space=pltpu.VMEM)] * 10,
        out_specs=pl.BlockSpec(memory_space=pltpu.VMEM),
        scratch_shapes=[pltpu.VMEM((128, 128), FULL)],
        compiler_params=params(),
        cost_estimate=cost(1e5, 3e5),
        name="first",
    )(qkv, *vectors)


def prep_kernel(where, out_m, up_m, down_m, out_s, up_s, down_s, p2, p3):
    def build(core):
        pairs_of = lambda m, s: (m, s) if core == 0 else (s, m)

        def rows(m, s, at, width):
            both = [v[:, at : at + width].astype(FULL) for v in pairs_of(m, s)]
            return jnp.concatenate(both, axis=0).astype(LOW)

        p2[:, 0:1536] = rows(up_m, up_s, core * 1536, 1536)
        p2[:, 1536:1920] = rows(out_m, out_s, core * 384, 384)
        for k, down in enumerate(pairs_of(down_m, down_s)):
            p3[k * 96 : k * 96 + 96, :] = down[:, core * 384 : core * 384 + 384]

    for core in range(2):
        pl.when(where[3] == core)(functools.partial(build, core))


def prep(where, mine, theirs):
    return pl.pallas_call(
        prep_kernel,
        out_shape=[jax.ShapeDtypeStruct((48, 1920), LOW), jax.ShapeDtypeStruct((192, 384), LOW)],
        in_specs=[SMEM] + [pl.BlockSpec(memory_space=pltpu.VMEM)] * 6,
        out_specs=[pl.BlockSpec(memory_space=pltpu.VMEM)] * 2,
        compiler_params=params(),
        cost_estimate=cost(1e6, 2e6),
        name="prep",
    )(where, *mine, *theirs)


def chip_of(where, dz, dy, dx):
    return ((where[0] ^ dz) * 2 + (where[1] ^ dy)) * 2 + (where[2] ^ dx)


def load_pack(where, pieces, start):
    for side in range(2):
        owner = where[3] ^ side
        col, along_x, along_y, far0, far1 = pieces[side * 5 : side * 5 + 5]
        for dz in range(4):
            far = far0.at[dz] if dz < 2 else far1.at[dz - 2]
            for dy, dx, source in ((0, 0, col.at[dz]), (0, 1, along_x.at[dz]), (1, 0, along_y.at[dz]), (1, 1, far)):
                start(source, chip_of(where, dz, dy, dx), owner)


def wait_pack(target, sem):
    pltpu.make_async_copy(target, target, sem).wait()


def normalise(values):
    centre = values - jnp.mean(values, axis=1, keepdims=True)
    spread = lax.rsqrt(jnp.mean(centre * centre, axis=1, keepdims=True) + 1e-6)
    return centre * spread, spread


def qkv_kernel(where, tok, *refs):
    pieces, (qkv, normed, w1, vec, bias_up, buf, weights, hats, sem) = refs[:10], refs[10:]
    half = pl.program_id(0)

    @pl.when(half == 0)
    def _():
        load_pack(
            where, pieces, lambda v, chip, core: pltpu.make_async_copy(v, buf.at[chip * 2 + core], sem).start()
        )
        for t in range(4):
            at = slice(t * 256, t * 256 + 256)
            hats[at, :], _ = normalise(tok[at, :].astype(FULL))
        wait_pack(buf, sem)
        lines = jnp.concatenate([buf[d, :, 2304:2432].astype(FULL) for d in range(32)], axis=0)
        lines = jnp.transpose(lines)
        vec[...] = lines[0:16]
        for chip in range(16):
            for s in range(2):
                line = buf[chip * 2 + s, 0:8, 2304:2432].astype(FULL)[0:1]
                at = (chip * 2 + s) * 96
                bias_up[0:1, at : at + 96] = line[:, 16:112]
        for t in range(4):
            at = slice(t * 256, t * 256 + 256)
            normed[at, :] = (hats[at, :] * lines[0:1] + lines[1:2]).astype(LOW)

    def gather(h):
        for chip in range(16):
            rows = slice(chip * 48, chip * 48 + 48)
            for part in range(3):
                at = slice(part * 768 + h * 384, part * 768 + h * 384 + 384)
                both = [buf[chip * 2 + s, :, at].astype(FULL) for s in range(2)]
                weights[rows, part * 384 : part * 384 + 384] = jnp.concatenate(both, axis=0).astype(LOW)

    for h in range(2):
        pl.when(half == h)(functools.partial(gather, h))
    w1[0] = weights[...]
    at = pl.multiple_of(half * 384, 128)
    query_bias = vec[2:3, pl.ds(at, 384)]
    value_bias = vec[3:4, pl.ds(at, 384)]
    for t in range(4):
        at = slice(t * 256, t * 256 + 256)
        mixed = mul(normed[at, :], weights[...])
        qkv[0, at, 0:384] = (mixed[:, 0:384] + query_bias).astype(LOW) * 0.125
        qkv[0, at, 384:768] = mixed[:, 384:768].astype(LOW)
        qkv[0, at, 768:1152] = (mixed[:, 768:1152] + value_bias).astype(LOW)


def qkv_call(where, tokens, pieces):
    return pl.pallas_call(
        qkv_kernel,
        grid=(2,),
        out_shape=[
            jax.ShapeDtypeStruct((2, 1024, 1152), LOW),
            jax.ShapeDtypeStruct((1024, 768), LOW),
            jax.ShapeDtypeStruct((2, 768, 1152), LOW),
            jax.ShapeDtypeStruct((16, 768), FULL),
            jax.ShapeDtypeStruct((1, 3072), FULL),
        ],
        in_specs=[SMEM, whole((1024, 768))] + [ANY] * 10,
        out_specs=[
            pl.BlockSpec((1, 1024, 1152), lambda h: (h, 0, 0)),
            whole((1024, 768)),
            pl.BlockSpec((1, 768, 1152), lambda h: (h, 0, 0)),
            whole((16, 768)),
            whole((1, 3072)),
        ],
        scratch_shapes=[
            pltpu.VMEM((32, 24, 2432), LOW),
            pltpu.VMEM((768, 1152), LOW),
            pltpu.VMEM((1024, 768), FULL),
            pltpu.SemaphoreType.DMA,
        ],
        compiler_params=params(),
        cost_estimate=cost(2 * 1024 * 768 * 2304, 16e6, scale=0.1),
        name="qkv",
    )(where, tokens, *pieces)


def masked_pair(block):
    lane = lax.broadcasted_iota(jnp.int32, block.shape, 1)
    zero = jnp.zeros_like(block)
    return jnp.concatenate([jnp.where(lane < 64, block, zero), jnp.where(lane < 64, zero, block)], axis=0)


def unmask(both):
    return jnp.concatenate([both[0:64, 0:128], both[64:128, 128:256]], axis=0)


def attend_kernel(first, qkv, seg, pad, *refs):
    probs, att_t, bias, wide = refs[-4:]
    row = pl.program_id(0) + first
    seg_row, pad_row = seg[pl.ds(row, 1), :].astype(FULL), pad[pl.ds(row, 1), :].astype(FULL)
    seg_col = jnp.transpose(jnp.broadcast_to(seg_row, (128, 256)))
    pad_col = jnp.transpose(jnp.broadcast_to(pad_row, (128, 256)))
    for b in range(2):
        keys = slice(64 * b, 64 * b + 192)
        same = seg_col[keys] == jnp.broadcast_to(seg_row[:, 128 * b : 128 * b + 128], (192, 128))
        key_at = lax.broadcasted_iota(jnp.int32, (192, 128), 0) + 64 * b
        query_at = lax.broadcasted_iota(jnp.int32, (192, 128), 1) + 128 * b
        allowed = same & ((pad_col[keys] == 1.0) | (key_at == query_at))
        one = jnp.where(allowed, 0.0, -1e30)
        bias[b] = jnp.concatenate([one, one], axis=1)
    blocks = [(half, p, b) for half in range(2) for p in range(3) for b in range(2)]
    for i, (half, p, b) in enumerate(blocks):
        stack = masked_pair(qkv[half, 128 * b : 128 * b + 128, p * 128 : p * 128 + 128])
        keys = slice(64 * b, 64 * b + 192)
        wide[i] = mul_t(qkv[half, keys, 384 + p * 128 : 512 + p * 128], stack) + bias[b]
    for i, (half, p, b) in enumerate(blocks):
        scores = wide[i]
        power = jnp.exp(scores - jnp.max(scores, axis=0, keepdims=True))
        probs[0, p, half, b] = (power * (1.0 / jnp.sum(power, axis=0, keepdims=True))).astype(LOW)
    for half, p, b in blocks:
        keys = slice(64 * b, 64 * b + 192)
        both = t_mul(qkv[half, keys, 768 + p * 128 : 896 + p * 128], probs[0, p, half, b])
        at = half * 384 + p * 128
        att_t[at : at + 128, 128 * b : 128 * b + 128] = unmask(both).astype(LOW)


def attend_call(first, count, qkv, seg, pad, before):
    old = list(before or [])
    return pl.pallas_call(
        functools.partial(attend_kernel, first),
        grid=(count,),
        out_shape=[
            jax.ShapeDtypeStruct((4, 3, 2, 2, 192, 256), LOW),
            jax.ShapeDtypeStruct((768, 1024), LOW),
        ],
        in_specs=[pl.BlockSpec((2, 256, 1152), lambda r: (0, r + first, 0)), whole((4, 256)), whole((4, 256))]
        + [ANY] * len(old),
        out_specs=[
            pl.BlockSpec((1, 3, 2, 2, 192, 256), lambda r: (r + first, 0, 0, 0, 0, 0)),
            pl.BlockSpec((768, 256), lambda r: (0, r + first)),
        ],
        input_output_aliases={3: 0, 4: 1} if old else {},
        scratch_shapes=[pltpu.VMEM((2, 192, 256), FULL), pltpu.VMEM((12, 192, 256), FULL)],
        compiler_params=params(),
        cost_estimate=cost(count * 1.5e9, count * 3e6, 8e5, scale=0.1),
        name="attend%d" % first,
    )(qkv, seg, pad, *old)


GATE = math.sqrt(2.0 / math.pi)


def gate_pair(u):
    square = u * u
    factor = 0.5 + 0.5 * jnp.tanh(u * (GATE + GATE * 0.044715 * square))
    value = u * factor
    return value, factor + value * (1.0 - factor) * (2.0 * GATE + 6.0 * GATE * 0.044715 * square)


FEED_SCALE = 0.1
CHUNK = 256
TILE = 256
TILES = 1024 // TILE


def load_up(where, pieces, up, w_out, sem, sem_out):
    def start(block, chip, core):
        rows = pl.ds(pl.multiple_of(chip * 48, 16), 48)
        for source, target, width, sem_of in (
            (slice(1536, 1920), w_out, 384, sem_out), (slice(0, 1536), up, 1536, sem)):
            columns = pl.ds(pl.multiple_of(core * width, 128), width)
            pltpu.make_async_copy(block.at[:, source], target.at[rows, columns], sem_of).start()

    load_pack(where, pieces, start)


def back_norm(grad, xhat, spread, gain):
    scaled = grad * gain
    flat = jnp.mean(scaled, axis=1, keepdims=True)
    tilt = jnp.mean(scaled * xhat, axis=1, keepdims=True)
    return (scaled - flat - xhat * tilt) * spread


def add_rows(target, row, values, step):
    value = jnp.sum(values, axis=0, keepdims=True)
    target[row : row + 1, :] = jnp.where(step == 0, value, target[row : row + 1, :] + value)


def feed_tile(step, att_t, tok, cot, bias, vec, weights, kept, outs, before):
    up, down, w_out = weights
    normed, act, hid = kept
    output, middle_grad, branch_grad, att_grad, sums, bias_grad = outs
    here = pl.ds(pl.multiple_of(step * TILE, TILE), TILE)
    before(0)
    mid = tok[...].astype(FULL) + t_mul(att_t[...], w_out[...]) + vec[4:5, :]
    xhat, spread = normalise(mid)
    rows = (xhat * vec[5:6, :] + vec[6:7, :]).astype(LOW)
    normed[here, :] = rows
    outer = cot[here, :]
    before(1)
    chunks = [slice(k * CHUNK, k * CHUNK + CHUNK) for k in range(3072 // CHUNK)]
    hidden = mul(rows, up[:, chunks[0]])
    for k, at in enumerate(chunks):
        following = mul(rows, up[:, chunks[k + 1]]) if k + 1 < len(chunks) else None
        if k == 0:
            before(2)
        active_grad = mul_t(outer, down[at, :])
        value, tilt = gate_pair(hidden + bias[:, at])
        act[here, at] = value.astype(LOW)
        grad = (tilt * active_grad).astype(LOW)
        hid[here, at] = grad
        line = jnp.sum(grad.astype(FULL), axis=0, keepdims=True)
        bias_grad[:, at] = jnp.where(step == 0, line, bias_grad[:, at] + line)
        hidden = following

    output[...] = (mid + vec[7:8, :] + mul(act[here, :], down[...])).astype(LOW)
    grad = mul_t(hid[here, :], up[...])
    outer = outer.astype(FULL)
    mid_grad = outer + back_norm(grad, xhat, spread, vec[5:6, :])
    middle_grad[...] = mid_grad
    low = mid_grad.astype(LOW)
    branch_grad[...] = low
    add_rows(sums, 0, grad * xhat, step)
    add_rows(sums, 1, grad, step)
    add_rows(sums, 2, low.astype(FULL), step)
    add_rows(sums, 3, outer, step)
    att_grad[...] = mul_t(low, w_out[...]).astype(LOW)


def feed_kernel(where, att_t, tok, cot, bias, vec, *refs):
    pieces, pieces_down = refs[:10], refs[10:20]
    outs = refs[20:26]
    down_packs, up_packs = refs[26:28], refs[28:30]
    up, down, w_out, normed, act, hid, sems = refs[30:]
    step = pl.program_id(0)
    core = where[3]

    def before(stage):
        @pl.when(step == 0)
        def _():
            if stage == 0:
                load_up(where, pieces, up, w_out, sems.at[1], sems.at[0])

                def start(block, chip, owner):
                    rows = pl.ds(pl.multiple_of(chip * 192, 16), 192)
                    columns = pl.ds(pl.multiple_of(owner * 384, 128), 384)
                    pltpu.make_async_copy(block, down.at[rows, columns], sems.at[2]).start()

                load_pack(where, pieces_down, start)
            target = (w_out, up, down)[stage]
            wait_pack(target, sems.at[stage])

    @pl.when(step < TILES)
    def _():
        feed_tile(step, att_t, tok, cot, bias, vec, (up, down, w_out), (normed, act, hid), outs, before)

    @pl.when(step >= TILES)
    def _():
        pair = step - TILES
        at = pl.multiple_of(pair * 1536, 1536)
        grad_down = t_mul(act[:, pl.ds(at, 1536)], cot[...]).astype(LOW)
        at = pl.multiple_of(pair * 384, 384)
        grad_up = t_mul(normed[:, pl.ds(at, 384)], hid[...])

        def put(side):
            for o in range(2):
                for k in range(8):
                    spot = ((k // 2 % 2) ^ where[1], (k % 2) ^ where[2], (k // 4) ^ (where[0] % 2))
                    at = k * 192 + o * 96
                    for h in range(2):
                        down_packs[o ^ side][spot + (slice(h * 96, h * 96 + 96),)] = grad_down[
                            at : at + 96, h * 384 : h * 384 + 384
                        ]
                    rows = grad_up[k * 48 + o * 24 : k * 48 + o * 24 + 24]
                    for j in range(4):
                        both = [rows[:, i * 384 : i * 384 + 384] for i in (2 * j, 2 * j + 1)]
                        up_packs[o ^ side][spot + (slice(j * 48, j * 48 + 48),)] = jnp.concatenate(
                            both, axis=0
                        ).astype(LOW)

        for side in range(2):
            pl.when(core == side)(functools.partial(put, side))


def feed_call(where, att_t, tokens, cot, bias_up, vec, pieces, pieces_down):
    tile = lambda step: jnp.minimum(step, TILES - 1)
    rows = pl.BlockSpec((TILE, 768), lambda s, where: (tile(s), 0))
    fixed = lambda shape: pl.BlockSpec(shape, lambda s, where: (0,) * len(shape), pipeline_mode=pl.Buffered(1))
    pack = (2, 2, 4, 192, 384)
    pack_block = pl.BlockSpec(
        (2, 2, 2, 192, 384), lambda s, where: (0, 0, jnp.clip(s - TILES, 0, 1) ^ (where[0] // 2), 0, 0))
    return pl.pallas_call(
        feed_kernel,
        grid_spec=pltpu.PrefetchScalarGridSpec(
            num_scalar_prefetch=1,
            grid=(TILES + 2,),
            in_specs=[
                pl.BlockSpec((768, TILE), lambda s, where: (0, tile(s))), rows, fixed((1024, 768)),
                fixed((1, 3072)), fixed((16, 768)),
            ] + [ANY] * 20,
            out_specs=[
                rows, rows, rows, rows, fixed((8, 768)), fixed((1, 3072)), *([pack_block] * 4),
            ],
            scratch_shapes=[
                pltpu.VMEM((768, 3072), LOW),
                pltpu.VMEM((3072, 768), LOW),
                pltpu.VMEM((768, 768), LOW),
                pltpu.VMEM((1024, 768), LOW),
                pltpu.VMEM((1024, 3072), LOW),
                pltpu.VMEM((1024, 3072), LOW),
                pltpu.SemaphoreType.DMA((3,)),
            ],
        ),
        out_shape=[
            jax.ShapeDtypeStruct((1024, 768), LOW),
            jax.ShapeDtypeStruct((1024, 768), FULL),
            jax.ShapeDtypeStruct((1024, 768), LOW),
            jax.ShapeDtypeStruct((1024, 768), LOW),
            jax.ShapeDtypeStruct((8, 768), FULL),
            jax.ShapeDtypeStruct((1, 3072), FULL),
        ] + [jax.ShapeDtypeStruct(pack, LOW)] * 4,
        compiler_params=params(),
        cost_estimate=cost(26 * 1024 * 768 * 768 * 2, 35e6, 3e6, scale=FEED_SCALE),
        name="feed",
    )(where, att_t, tokens, cot, bias_up, vec, *pieces, *pieces_down)


ROWS_STEP = 2


def unattend_kernel(groups, with_out, where, *refs):
    count = len(groups)
    parts = [refs[5 * g : 5 * g + 5] for g in range(count)]
    refs = refs[5 * count + (0 if with_out else 2) :]
    probs, normed = refs[:count], refs[count]
    refs = refs[count + 1 :]
    if with_out:
        att_t, branch_grad, refs = refs[0], refs[1], refs[2:]
        mixed, mine, theirs, sums, acc, wide, slim, stacks, out_acc = refs
    else:
        mixed, mine, theirs, sums, acc, wide, slim, stacks = refs
    step = pl.program_id(0)
    width = 128 * count
    blocks = [(r, g, h) for r in range(ROWS_STEP) for g in range(count) for h in range(2)]

    def keys_of(r, b):
        return slice(256 * r + 64 * b, 256 * r + 64 * b + 192)

    def queries_of(r, b):
        return slice(256 * r + 128 * b, 256 * r + 128 * b + 128)

    for i, (r, g, half) in enumerate(blocks):
        query, key, value = parts[g][:3]
        grads = parts[g][3 + half]
        for b in range(2):
            stacks[0, 2 * i + b] = masked_pair(query[half, queries_of(r, b), :])
            stack = masked_pair(grads[queries_of(r, b), :])
            stacks[1, 2 * i + b] = stack
            wide[2 * i + b] = mul_t(value[half, keys_of(r, b), :], stack)
    for i, (r, g, half) in enumerate(blocks):
        for b in range(2):
            weights = probs[g][r, 0, half, b].astype(FULL)
            prob_grad = wide[2 * i + b]
            inner = jnp.sum(prob_grad * weights, axis=0, keepdims=True)
            slim[2 * i + b] = (weights * (prob_grad - inner)).astype(LOW)

    def merge(first, second):
        return jnp.concatenate([first[0:64], first[64:192] + second[0:128], second[128:192]], axis=0)

    for i, (r, g, half) in enumerate(blocks):
        key = parts[g][1]
        rows = slice(256 * r, 256 * r + 256)
        value_grad = [mul(probs[g][r, 0, half, b], stacks[1, 2 * i + b]) for b in range(2)]
        key_grad = [mul(slim[2 * i + b], stacks[0, 2 * i + b]) for b in range(2)]
        turned = [unmask(t_mul(key[half, keys_of(r, b), :], slim[2 * i + b])) for b in range(2)]
        query_grad = jnp.transpose(jnp.concatenate(turned, axis=1)) * 0.125
        at = g * 128
        mixed[half, rows, at : at + 128] = query_grad.astype(LOW)
        mixed[half, rows, width + at : width + at + 128] = merge(*key_grad).astype(LOW)
        mixed[half, rows, 2 * width + at : 2 * width + at + 128] = merge(*value_grad).astype(LOW)

    def add(target, more):
        @pl.when(step == 0)
        def _():
            target[...] = more

        @pl.when(step > 0)
        def _():
            target[...] += more

    for half in range(2):
        add_rows(sums.at[half], 0, mixed[half].astype(FULL), step)
        add(acc.at[half], t_mul(normed[...], mixed[half]))
    if with_out:
        add(out_acc, mul(att_t[...], branch_grad[...]))

    def write(side):
        for owner in range(2):
            dest = mine if owner == side else theirs
            for chip in range(16):
                rows = slice(chip * 48 + owner * 24, chip * 48 + owner * 24 + 24)
                spot = ((chip // 2 % 2) ^ where[1], (chip % 2) ^ where[2], (chip // 4) ^ where[0], slice(None))
                if with_out:
                    lines = [out_acc[rows, :], jnp.concatenate([acc[0, rows, :], acc[1, rows, :]], axis=1)]
                else:
                    lines = [acc[0, rows, :], acc[1, rows, :]]
                dest[spot + (slice(0, 768),)] = jnp.concatenate(lines, axis=0).astype(LOW)

    for side in range(2):
        pl.when((step == 4 // ROWS_STEP - 1) & (where[3] == side))(functools.partial(write, side))


def unattend_call(groups, where, qkv, att_grad, probs, normed, packs=None, att_t=None, branch_grad=None):
    with_out = att_t is not None
    count = len(groups)
    width = 384 * count
    tall = 256 * ROWS_STEP
    operands, specs = [], []
    for p in groups:
        for part in range(3):
            operands.append(qkv)
            specs.append(pl.BlockSpec((2, tall, 128), lambda r, c=part * 3 + p: (0, r, c)))
        for half in range(2):
            operands.append(att_grad)
            specs.append(pl.BlockSpec((tall, 128), lambda r, c=half * 3 + p: (r, c)))
    if not with_out:
        operands += list(packs)
        specs += [ANY, ANY]
    for p in groups:
        operands.append(probs)
        specs.append(pl.BlockSpec((ROWS_STEP, 1, 2, 2, 192, 256), lambda r, p=p: (r, p, 0, 0, 0, 0)))
    operands.append(normed)
    specs.append(pl.BlockSpec((tall, 768), lambda r: (r, 0)))
    if with_out:
        operands += [att_t, branch_grad]
        specs += [pl.BlockSpec((768, tall), lambda r: (0, r)), pl.BlockSpec((tall, 768), lambda r: (r, 0))]
    shape = (2, 2, 4, 48, 1536)
    lanes = 0 if with_out else 1
    part_of = pl.BlockSpec((2, 2, 4, 48, 768), lambda r: (0, 0, 0, 0, lanes), pipeline_mode=pl.Buffered(1))
    many = 4 * count * ROWS_STEP
    return pl.pallas_call(
        functools.partial(unattend_kernel, groups, with_out),
        grid=(4 // ROWS_STEP,),
        out_shape=[
            jax.ShapeDtypeStruct((2, 1024, width), LOW),
            jax.ShapeDtypeStruct(shape, LOW),
            jax.ShapeDtypeStruct(shape, LOW),
            jax.ShapeDtypeStruct((2, 8, width), FULL),
        ],
        in_specs=[SMEM] + specs,
        out_specs=[
            pl.BlockSpec((2, tall, width), lambda r: (0, r, 0)),
            part_of,
            part_of,
            whole((2, 8, width)),
        ],
        input_output_aliases={} if with_out else {1 + 5 * count + k: 1 + k for k in range(2)},
        scratch_shapes=[
            pltpu.VMEM((2, 768, width), FULL),
            pltpu.VMEM((many, 192, 256), FULL),
            pltpu.VMEM((many, 192, 256), LOW),
            pltpu.VMEM((2, many, 256, 128), LOW),
        ] + ([pltpu.VMEM((768, 768), FULL)] if with_out else []),
        compiler_params=params(),
        cost_estimate=cost(count * 2.5e9, count * 8e6),
        name="unattend%d" % groups[0],
    )(where, *operands)


def tokens_kernel(m0, m1, w1, tok, vec, middle_grad, sums, sums0, sums1, bias, grad, lines):
    step = pl.program_id(0)
    total = None
    for half in range(2):
        joined = []
        for part in range(3):
            joined.append(m0[half, :, part * 128 : part * 128 + 128])
            joined.append(m1[half, :, part * 256 : part * 256 + 256])
        more = mul_t(jnp.concatenate(joined, axis=1), w1[half])
        total = more if total is None else total + more
    xhat, spread = normalise(tok[...].astype(FULL))
    grad[...] = middle_grad[...] + back_norm(total, xhat, spread, vec[0:1, :])
    add_rows(lines, 0, total * xhat, step)
    add_rows(lines, 1, total, step)

    @pl.when(step == 3)
    def _():
        for half in range(2):
            at = half * 384
            for row, part in ((2, 0), (3, 2)):
                lines[row : row + 1, at : at + 128] = sums0[half, 0:1, part * 128 : part * 128 + 128]
                lines[row : row + 1, at + 128 : at + 384] = sums1[half, 0:1, part * 256 : part * 256 + 256]
        lines[4:5, :] = sums[2:3, :]
        lines[5:6, :] = sums[0:1, :]
        lines[6:7, :] = sums[1:2, :]
        lines[7:8, :] = sums[3:4, :]
        for k in range(4):
            lines[8 + k : 9 + k, :] = bias[0:1, k * 768 : k * 768 + 768]
        lines[12:16, :] = jnp.zeros((4, 768), FULL)


def tokens_call(mixed0, mixed1, w1, tokens, vec, middle_grad, sums, sums0, sums1, bias):
    rows = pl.BlockSpec((256, 768), lambda r: (r, 0))
    return pl.pallas_call(
        tokens_kernel,
        grid=(4,),
        out_shape=[jax.ShapeDtypeStruct((1024, 768), FULL), jax.ShapeDtypeStruct((16, 768), FULL)],
        in_specs=[pl.BlockSpec((2, 256, w), lambda r: (0, r, 0)) for w in (384, 768)] + [
            whole((2, 768, 1152)), rows, whole((16, 768)), rows, whole((8, 768)), whole((2, 8, 384)),
            whole((2, 8, 768)), whole((1, 3072)),
        ],
        out_specs=[rows, whole((16, 768))],
        compiler_params=params(),
        cost_estimate=cost(2 * 1024 * 768 * 2304, 16e6),
        name="tokens",
    )(mixed0, mixed1, w1, tokens, vec, middle_grad, sums, sums0, sums1, bias)


def after(value, *before):
    return lax.optimization_barrier((value, before))[0]


class Total:
    def __init__(self, mine, theirs):
        self.mine = mine
        self.block = mine.shape[3:]
        self.got = send(theirs, SWAP_C)

    def spec(self, size, place_of):
        return pl.BlockSpec(size + self.block, lambda i: place_of(i) + (0, 0))

    def low(self, *lead):
        return jax.ShapeDtypeStruct(lead + self.block, LOW)

    def first(self):
        def body(mine_x, got_x, mine_y, got_y, out_x, out_y):
            out_x[...] = (mine_x[...].astype(FULL) + got_x[...].astype(FULL)).reshape(out_x.shape).astype(LOW)
            out_y[...] = (mine_y[...].astype(FULL) + got_y[...].astype(FULL)).reshape(out_y.shape).astype(LOW)

        to_x = self.spec((1, 1, 2), lambda i: (i, 1, 0))
        to_y = self.spec((1, 1, 2), lambda i: (1, i, 1))
        out = self.spec((1, 2), lambda i: (i, 0))

        def keep(one_x, one_y):
            self.one_x, self.one_y = send(one_x, SWAP_X), send(one_y, SWAP_Y)

        return (body, [self.mine, self.got] * 2, [to_x, to_x, to_y, to_y], [self.low(2, 2)] * 2, [out] * 2, keep)

    def second(self):
        def body(mine_y, got_y, one_x, mine_x, got_x, one_y, out_y, out_x):
            add = lambda *refs: sum(r[...].astype(FULL).reshape(out_y.shape) for r in refs)
            out_y[...] = add(mine_y, got_y, one_x).astype(LOW)
            out_x[...] = add(mine_x, got_x, one_y).astype(LOW)

        to_y = self.spec((1, 1, 1), lambda i: (1, 0, i))
        to_x = self.spec((1, 1, 1), lambda i: (0, 1, 2 + i))
        came = self.spec((1, 1), lambda i: (1, i))
        out = self.spec((1,), lambda i: (i,))

        def keep(two_y, two_x):
            self.two_y, self.two_x = send(two_y, SWAP_Y), send(two_x, SWAP_X)

        operands = [self.mine, self.got, self.one_x, self.mine, self.got, self.one_y]
        return (body, operands, [to_y, to_y, came, to_x, to_x, came], [self.low(2)] * 2, [out] * 2, keep)

    def third(self):
        def body(mine, got, one_x, two_y, one_y, two_x, *outs):
            @pl.when(pl.program_id(0) == 0)
            def _():
                for k, target in enumerate(outs):
                    extra = (one_x[0, k], two_y[k]) if k < 2 else (one_y[0, k - 2], two_x[k - 2])
                    total = mine[0, 0, k].astype(FULL) + got[0, 0, k].astype(FULL)
                    total = total + extra[0].astype(FULL) + extra[1].astype(FULL)
                    target[...] = total.astype(target.dtype)

        near = self.spec((1, 1, 4), lambda i: (0, 0, 0))
        came = self.spec((1, 2), lambda i: (0, 0))
        two = self.spec((2,), lambda i: (0,))
        one = pl.BlockSpec(self.block, lambda i: (0, 0))
        out = [jax.ShapeDtypeStruct(self.block, FULL)] + [self.low()] * 3

        def keep(own, *three):
            self.own = own
            self.parts = [send(v, SWAP_Z[k + 1]) for k, v in enumerate(three)]

        operands = [self.mine, self.got, self.one_x, self.two_y, self.one_y, self.two_x]
        return (body, operands, [near, near, came, two, came, two], out, [one] * 4, keep)

    def last(self, write, shapes, more=()):
        def body(own, part1, part2, part3, *refs):
            @pl.when(pl.program_id(0) == 0)
            def _():
                total = own[...] + part1[...].astype(FULL) + part2[...].astype(FULL) + part3[...].astype(FULL)
                write(total, *refs)

        block = pl.BlockSpec(self.block, lambda i: (0, 0))
        same = lambda shape: pl.BlockSpec(shape, lambda i: (0,) * len(shape))

        def keep(*given):
            self.final = given

        return (
            body, [self.own, *self.parts, *more], [block] * 4 + [same(v.shape) for v in more],
            [jax.ShapeDtypeStruct(v, FULL) for v in shapes], [same(v) for v in shapes], keep,
        )


def write_down(total, share):
    share[...] = jnp.concatenate([total[0:96], total[96:192]], axis=1)


def write_up(total, share):
    share[...] = jnp.concatenate([total[j * 24 : j * 24 + 24] for j in range(8)], axis=1)


def write_head(total, share_out, share):
    share_out[...] = total[0:24, 0:768]
    for half in range(2):
        for part in range(3):
            at = part * 768 + half * 384
            first = half * 384 + part * 128
            share[:, at : at + 128] = total[24:48, first : first + 128]
            rest = 768 + part * 256
            share[:, at + 128 : at + 384] = total[half * 24 : half * 24 + 24, rest : rest + 256]


def run_stages(stages, *before):
    ins = [len(s[1]) for s in stages]
    outs = [len(s[3]) for s in stages]

    def kernel(*refs):
        at_in, at_out = 0, sum(ins)
        for stage, n_in, n_out in zip(stages, ins, outs):
            stage[0](*refs[at_in : at_in + n_in], *refs[at_out : at_out + n_out])
            at_in, at_out = at_in + n_in, at_out + n_out

    operands = after([v for s in stages for v in s[1]], *before)
    results = pl.pallas_call(
        kernel,
        grid=(2,),
        out_shape=[v for s in stages for v in s[3]],
        in_specs=[v for s in stages for v in s[2]],
        out_specs=[v for s in stages for v in s[4]],
        compiler_params=params(),
        cost_estimate=cost(1e6, 4e6),
        name="sums",
    )(*operands)
    at = 0
    for stage, n_out in zip(stages, outs):
        stage[5](*results[at : at + n_out])
        at += n_out
    return results


def halves_of(own, sibling, core):
    return jnp.where(core == 0, own, sibling), jnp.where(core == 0, sibling, own)


def on_device(
    tokens, segment_ids, pad_mask, w_qkv, w_out, w_up, w_down, gain_one, shift_one, bias_query,
    bias_value, bias_out, gain_two, shift_two, bias_up, bias_down, cotangent,
):
    z0, y0, x0, core = place()
    where = jnp.stack([z0, y0, x0, core]).astype(jnp.int32)
    row_count, length, width = tokens.shape
    total_rows = row_count * length
    flat = tokens.reshape(total_rows, width)
    cot = cotangent.reshape(total_rows, width)
    vectors = (gain_one, shift_one, bias_query, bias_value, bias_out, gain_two, shift_two, bias_down, bias_up)

    def along_z(own):
        return [send(own[None], SWAP_Z[k]) for k in (1, 2, 3)]

    def column(own, rest):
        return jnp.concatenate([own[None], *rest], axis=0)

    def plane(col):
        return send(col, SWAP_X), send(col, SWAP_Y)

    def corner(along_x, along_y):
        return send(along_x[0:2], SWAP_Y), send(along_y[2:4], SWAP_X)

    def across(blocks):
        return [send(v, SWAP_C) for v in blocks]

    p1 = first_call(w_qkv, vectors)
    rest1 = along_z(p1)
    mine = (w_out, w_up, w_down)
    p2, p3 = prep(where, after(mine, p1), across(mine))
    col1 = column(after(p1, p2), rest1)
    x1, y1 = plane(col1)
    rest2 = along_z(after(p2, col1))
    col2 = column(p2, rest2)
    far1 = corner(x1, y1)
    own1 = [col1, x1, y1]
    pack1 = own1 + list(far1) + across(own1) + across(far1)
    col2 = after(col2, far1)
    x2, y2 = plane(col2)
    rest3 = along_z(after(p3, col2))
    qkv, normed_one, w1, vec, up_line = qkv_call(where, after(flat, col2), pack1)
    col3 = column(after(p3, qkv), rest3)
    x3, y3 = plane(col3)
    held = attend_call(0, 2, after(qkv, col3), segment_ids, pad_mask, None)
    far2 = corner(x2, y2)
    other2 = across(after([col2, x2, y2], held))
    probs, att_t = attend_call(2, 2, after(qkv, x2, y2), segment_ids, pad_mask, held)
    pack2 = [col2, x2, y2, *far2] + other2 + across(after(far2, att_t))
    far3 = corner(after(x3, att_t), after(y3, att_t))
    own3 = [col3, x3, y3]
    pack3 = own3 + list(far3) + across(after(own3, att_t, other2)) + across(far3)
    output, middle_grad, branch_grad, att_grad, sums, bias_grad, *grads = feed_call(
        where, att_t, flat, cot, up_line, vec, pack2, pack3)

    sum_a, sum_b = Total(*grads[:2]), Total(*grads[2:])
    ready = run_stages([sum_a.first()])
    mixed0, mine, theirs, sums0 = unattend_call(
        (0,), where, qkv, after(att_grad, ready), probs, normed_one, None, att_t, branch_grad)
    ready = run_stages([sum_a.second(), sum_b.first()], mixed0)
    mixed1, mine, theirs, sums1 = unattend_call(
        (1, 2), where, qkv, after(att_grad, ready), probs, normed_one, (mine, theirs))
    head = Total(mine, theirs)
    ready = run_stages([sum_a.third(), sum_b.second()], mixed1)
    grad_tokens, lines = tokens_call(
        mixed0, after(mixed1, ready), w1, flat, vec, middle_grad, sums, sums0, sums1, bias_grad)
    ready = run_stages([sum_b.third(), head.first(), sum_a.last(write_down, [(96, 768)])], grad_tokens)
    lines = after(lines, ready)
    got = [send(lines, move) for move in SWAP_Z[1:]]
    ready = run_stages([head.second(), sum_b.last(write_up, [(24, 3072)])], ready)
    lines = after(lines, ready) + got[0] + (got[1] + got[2])
    got = [send(lines, move) for move in (SWAP_X, SWAP_Y, SWAP_D)]
    ready = run_stages([head.third()], ready)
    lines = after(lines, ready) + got[0] + (got[1] + got[2])
    got = send(lines, SWAP_C)
    run_stages([head.last(write_head, [(24, 768), (24, 2304)])], ready)
    lines = lines + got
    share_out, share_qkv = head.final
    share_up, share_down = sum_b.final[0], sum_a.final[0]

    device = ((z0 * 2 + y0) * 2 + x0) * 2 + core
    own = lax.dynamic_slice(lines, (0, device * 24), (8, 24))
    own_up = lax.dynamic_slice(lines, (8 + device // 8, device % 8 * 96), (1, 96))[0]
    return (
        output.reshape(row_count, length, width),
        grad_tokens.reshape(row_count, length, width),
        share_qkv, share_out, share_up, share_down,
        own[0], own[1], own[2], own[3], own[4], own[5], own[6], own_up, own[7],
    )


def solution(mesh):
    fits = dict(mesh.shape) == {"gx": 8, "gy": 4}
    device = on_device if fits else generic_device
    names = AXES if fits else ("gx", "gy")
    if fits:
        mesh = Mesh(mesh.devices.reshape(4, 2, 2, 2), AXES)
    return jax.shard_map(
        device,
        mesh=mesh,
        in_specs=(
            P(names, None, None),
            P(names, None),
            P(names, None),
            P(names, None),
            P(names, None),
            P(names, None),
            P(names, None),
            P(names),
            P(names),
            P(names),
            P(names),
            P(names),
            P(names),
            P(names),
            P(names),
            P(names),
            P(names, None, None),
        ),
        out_specs=(
            P(names, None, None),
            P(names, None, None),
            P(names, None),
            P(names, None),
            P(names, None),
            P(names, None),
            P(names),
            P(names),
            P(names),
            P(names),
            P(names),
            P(names),
            P(names),
            P(names),
            P(names),
        ),
        check_vma=False,
    )
```
